512 devices in a mesh: dp: 32 (over z, x), mp: 16 (over y, core).
Axes of the slice: x: 4, y: 8, z: 8, core: 2. Of those that a mesh axis runs over, the one named last changes fastest.
Arguments:
- gradients: bfloat16 [32, 240, 28672], P('dp', None, 'mp'), may hold values from -6 to 6
- errors: float32 [32, 240, 28672], P('dp', None, 'mp'), may hold values from -4 to 4
- q_start: float32 [1, 240, 64], replicated, may hold values from -0.3 to 2.3
Outputs:
- update_grad: bfloat16 [240, 28672], P(None, 'mp')
- new_errors: float32 [32, 240, 28672], P('dp', None, 'mp')
- q_next: float32 [1, 240, 64], replicated
The draws below stay inside these ranges and needn't reach their ends.
All inputs are finite; a program needn't handle non-finite values.
Results may differ from the reference program's by a relative error of at most 0.001.
Values sent between devices are 32-bit elements; how exact they have to be, the bound alone decides.
A program may use at most 64 MiB of HBM per device.

```python
import jax
import jax.numpy as jnp
from jax import lax

FF = 28672
DW = 240
MATS = 1
RANK = 64
N_DP = 32


def draw_q_start(key, part):
    key = jax.random.fold_in(key, 7)
    base = 2.0 * jnp.eye(DW, RANK, dtype=jnp.float32)
    noise = jnp.clip(0.08 * jax.random.normal(key, (MATS, DW, RANK), jnp.float32), -0.3, 0.3)
    return base[None] + noise


def block_levels(key, extent, cuts, least, high):
    def one(position, blocks):
        heights = jax.random.uniform(jax.random.fold_in(jax.random.fold_in(key, 6), position), (blocks,), jnp.float32, least / len(cuts), high / len(cuts))
        return jnp.repeat(jnp.exp(heights), extent[position] // blocks).reshape((-1,) + (1,) * (len(extent) - position - 1))

    factor_of = one(*cuts[0])
    for cut in cuts[1:]:
        factor_of = factor_of * one(*cut)
    return factor_of


def scatter_about(rng, dims, deviation, limit, shards=(), held_as=jnp.bfloat16):
    drawn = deviation * jax.random.normal(rng, dims, jnp.float32)
    if shards:
        drawn = drawn * block_levels(rng, dims, shards, -0.22, 0.18)
    return jnp.clip(drawn, -limit, limit).astype(held_as)


def setup_inputs(seed: int = 0) -> dict:
    splits = jax.random.split(jax.random.key(seed), 4)
    gradients = scatter_about(splits[0], (N_DP, MATS * DW, FF), 1.0, 6.0, ((0, 32), (2, 16)))
    errors = scatter_about(splits[1], (N_DP, MATS * DW, FF), 0.5, 4.0, ((0, 32), (2, 16)), jnp.float32)
    q_start = draw_q_start(jax.random.fold_in(splits[3], 71), 0)
    return dict(gradients=gradients, errors=errors, q_start=q_start)


def orthonormal_rows(left_rows, gram_sum):
    lower = jnp.linalg.cholesky(gram_sum)
    return lax.linalg.triangular_solve(lower, left_rows, left_side=True, lower=True)

def reference(gradients, errors, q_start):
    highest = lax.Precision.HIGHEST
    merged = gradients.astype(jnp.float32) + errors
    blocks = merged.reshape(N_DP, MATS, DW, FF)
    local_p = jnp.einsum('nkdf,kdr->nkrf', blocks, q_start, precision=highest)
    p_mean = jnp.sum(local_p, axis=0) / N_DP
    gram_sum = jnp.einsum('krf,ksf->krs', p_mean, p_mean, precision=highest)
    ortho = orthonormal_rows(p_mean, gram_sum)
    q_next = jnp.einsum('nkdf,krf->kdr', blocks, ortho, precision=highest) / N_DP
    update = jnp.einsum('krf,kdr->kdf', ortho, q_next, precision=highest)
    new_errors = blocks - update[None]
    update_grad = update.reshape(MATS * DW, FF).astype(jnp.bfloat16)
    return (update_grad, new_errors.reshape(N_DP, MATS * DW, FF), q_next)
```

```python
import jax
import jax.numpy as jnp
from jax import lax
from jax.experimental import pallas as pl
from jax.experimental.pallas import tpu as pltpu
from jax.sharding import PartitionSpec as P

MESH = pl.DeviceIdType.MESH
NX, NZ, NMP = 4, 8, 16
NDP = NX * NZ
COLS, RANK, FL = 240, 64, 1792
CHUNK = 256
NCHUNK = FL // CHUNK
HALF = FL // 2
ROWS_T = 384
F32, BF16 = jnp.float32, jnp.bfloat16
FAR_FIRST = (4, 3, 5, 2, 6, 1, 7, 0)
NEAR_FIRST = (1, 7, 2, 6, 3, 5, 4)


def split(value):
    high = value.astype(BF16)
    return high, (value - high.astype(F32)).astype(BF16)


def dot(a, b, dims):
    return lax.dot_general(a, b, (dims, ((), ())), preferred_element_type=F32)


def remote(src, dst, send, recv, target):
    return pltpu.make_async_remote_copy(
        src_ref=src, dst_ref=dst, send_sem=send, recv_sem=recv,
        device_id=target, device_id_type=MESH,
    )


def inverse_factor(gram):
    row_at = lax.broadcasted_iota(jnp.int32, (RANK, 2 * RANK), 0)
    col_at = lax.broadcasted_iota(jnp.int32, (RANK, 2 * RANK), 1)
    work = jnp.where(col_at == row_at + RANK, 1.0, gram)
    done = []
    for j in range(RANK):
        base = 8 * (j // 8)
        local = j - base
        pivot = work[local:local + 1, j:j + 1]
        row = work[local:local + 1, :]
        below = lax.broadcasted_iota(jnp.int32, work.shape, 0) > local
        factor = work[:, j:j + 1] / pivot
        work = work - jnp.where(below, factor * row, 0.0)
        if local == 7:
            done.append(work[:8])
            work = work[8:]
    full = jnp.concatenate(done, axis=0)
    diagonal = jnp.sum(jnp.where(col_at == row_at, full, 0.0), axis=1, keepdims=True)
    return (full / jnp.sqrt(diagonal))[:, RANK:]


def round_kernel(g_hbm, e_hbm, q_ref, p_out, v_out, q_out,
                 g_buf, e_buf, mh, ml, local_p, x_recv, z_send, z_recv, gathered, p_full,
                 t_send, t_recv, t_part, t_all, t_gather, g_gather, t_full, g_full,
                 load_sem, x_ssem, x_rsem, z_ssem, z_rsem, az_ssem, az_rsem, ax_ssem, ax_rsem,
                 ts_sem, tr_sem, ta_ssem, ta_rsem, tg_ssem, tg_rsem, gg_ssem, gg_rsem):
    dp = lax.axis_index("dp")
    mp = lax.axis_index("mp")
    z, x = dp // NX, dp % NX

    def load(c):
        cols = pl.ds(c * CHUNK, CHUNK)
        return (
            pltpu.make_async_copy(g_hbm.at[0, :, cols], g_buf.at[:, cols], load_sem.at[c, 0]),
            pltpu.make_async_copy(e_hbm.at[0, :, cols], e_buf.at[:, cols], load_sem.at[c, 1]),
        )

    for c in range(NCHUNK):
        for copy in load(c):
            copy.start()

    barrier = pltpu.get_barrier_semaphore()

    def greet_dp(k, carry):
        pl.semaphore_signal(barrier, inc=1, device_id=((dp + k) % NDP, mp), device_id_type=MESH)
        return carry

    def greet_mp(k, carry):
        pl.semaphore_signal(barrier, inc=1, device_id=(dp, (mp + k) % NMP), device_id_type=MESH)
        return carry

    lax.fori_loop(1, NDP, greet_dp, 0)
    lax.fori_loop(1, NMP, greet_mp, 0)

    q_high, q_low = split(q_ref[0].T)
    q_both = jnp.concatenate([q_high, q_low], axis=0)
    mh[COLS:256, :] = jnp.zeros((256 - COLS, FL), BF16)
    ml[COLS:256, :] = jnp.zeros((256 - COLS, FL), BF16)
    mh[256 + RANK:, :] = jnp.zeros((ROWS_T - 256 - RANK, FL), BF16)
    ml[256 + RANK:, :] = jnp.zeros((ROWS_T - 256 - RANK, FL), BF16)

    for c in range(NCHUNK):
        for copy in load(c):
            copy.wait()
        cols = slice(c * CHUNK, (c + 1) * CHUNK)
        merged = g_buf[:, cols].astype(F32) + e_buf[:, cols]
        high, low = split(merged)
        mh[:COLS, cols] = high
        ml[:COLS, cols] = low
        both = dot(q_both, high, ((1,), (0,)))
        part = both[:RANK] + both[RANK:] + dot(q_high, low, ((1,), (0,)))
        for xl in range(2):
            tile = part[:, xl * 128:(xl + 1) * 128]
            for xh in range(2):
                for t in range(NZ):
                    first = xh * 32 + t * 4
                    local_p[t, 2 * xh + xl, :, c * 128:(c + 1) * 128] = tile[first:first + 4]

    pl.semaphore_wait(barrier, NDP - 1 + NMP - 1)

    for k in FAR_FIRST:
        t = (z + k) % NZ
        for i in range(1, NX):
            to = (x + i) % NX
            remote(local_p.at[t, to], x_recv.at[t, i - 1], x_ssem, x_rsem.at[t], (z * NX + to, mp)).start()
    for k in FAR_FIRST:
        t = (z + k) % NZ
        remote(x_recv.at[t], x_recv.at[t], x_ssem, x_rsem.at[t], (dp, mp)).wait_recv()
        total = local_p[t, x] + x_recv[t, 0] + x_recv[t, 1] + x_recv[t, 2]
        z_send[k] = total
        if k:
            remote(z_send.at[k], z_recv.at[k - 1], z_ssem, z_rsem, (t * NX + x, mp)).start()
    remote(z_recv, z_recv, z_ssem, z_rsem, (dp, mp)).wait_recv()
    mean = z_send[0]
    for k in range(NZ - 1):
        mean = mean + z_recv[k]
    gathered[z, x] = mean * (1.0 / NDP)

    for k in NEAR_FIRST:
        remote(gathered.at[z, x], gathered.at[z, x], az_ssem, az_rsem.at[k], ((z + k) % NZ * NX + x, mp)).start()

    def on_to_x(t):
        for i in range(1, NX):
            remote(gathered.at[t, x], gathered.at[t, x], ax_ssem, ax_rsem, (z * NX + (x + i) % NX, mp)).start()

    on_to_x(z)
    remote(x_recv, x_recv, x_ssem, x_rsem.at[0], (dp, mp)).wait_send()
    remote(z_recv, z_recv, z_ssem, z_rsem, (dp, mp)).wait_send()
    for k in NEAR_FIRST:
        t = (z + NZ - k) % NZ
        remote(gathered.at[t, x], gathered.at[t, x], az_ssem, az_rsem.at[k], (dp, mp)).wait_recv()
        on_to_x(t)
    remote(x_recv, x_recv, ax_ssem, ax_rsem, (dp, mp)).wait_recv()

    for c in range(NCHUNK):
        for xl in range(2):
            cols = slice((2 * c + xl) * 128, (2 * c + xl + 1) * 128)
            for xh in range(2):
                for t in range(NZ):
                    first = xh * 32 + t * 4
                    p_full[first:first + 4, cols] = gathered[t, 2 * xh + xl, :, c * 128:(c + 1) * 128]
    p_high, p_low = split(p_full[...])
    p_out[:RANK, :] = p_high
    p_out[RANK:, :] = p_low
    mh[256:256 + RANK, :] = p_high
    ml[256:256 + RANK, :] = p_low

    both = dot(p_out[...], mh[...], ((1,), (1,)))
    t_local = both[:RANK] + both[RANK:] + dot(p_out[:RANK, :], ml[...], ((1,), (1,)))
    for j in range(NMP):
        t_send[j] = t_local[4 * j:4 * j + 4]

    def scatter_t(k, carry):
        to = (mp + k) % NMP
        remote(t_send.at[to], t_recv.at[k - 1], ts_sem, tr_sem, (dp, to)).start()
        return carry

    lax.fori_loop(1, NMP, scatter_t, 0)
    remote(x_recv, x_recv, ax_ssem, ax_rsem, (dp, mp)).wait_send()
    remote(z_recv, z_recv, az_ssem, az_rsem.at[1], (dp, mp)).wait_send()
    remote(t_recv, t_recv, ts_sem, tr_sem, (dp, mp)).wait_recv()
    slice_sum = t_send[mp]
    for k in range(NMP - 1):
        slice_sum = slice_sum + t_recv[k]
    t_all[dp] = slice_sum[:, :256]
    t_part[...] = slice_sum[:, :256]
    g_gather[mp] = slice_sum[:, 256:]

    def spread_t(k, carry):
        to = (dp + k) % NDP
        remote(t_part, t_all.at[dp], ta_ssem, ta_rsem, (to, mp)).start()
        return carry

    def gather_g(k, carry):
        remote(g_gather.at[mp], g_gather.at[mp], gg_ssem, gg_rsem, (dp, (mp + k) % NMP)).start()
        return carry

    lax.fori_loop(1, NMP, gather_g, 0)
    lax.fori_loop(1, NDP, spread_t, 0)
    rest_g = g_gather.at[pl.ds(0, NMP - 1)]
    remote(rest_g, rest_g, gg_ssem, gg_rsem, (dp, mp)).wait_recv()
    for j in range(NMP):
        g_full[4 * j:4 * j + 4, :] = g_gather[j]
    remote(t_recv, t_recv, ts_sem, tr_sem, (dp, mp)).wait_send()
    remote(rest_g, rest_g, gg_ssem, gg_rsem, (dp, mp)).wait_send()

    rest_t = t_all.at[pl.ds(0, NDP - 1)]
    remote(rest_t, rest_t, ta_ssem, ta_rsem, (dp, mp)).wait_recv()
    total = t_all[0]
    for k in range(1, NDP):
        total = total + t_all[k]
    t_gather[mp] = total

    def gather_t(k, carry):
        remote(t_gather.at[mp], t_gather.at[mp], tg_ssem, tg_rsem, (dp, (mp + k) % NMP)).start()
        return carry

    lax.fori_loop(1, NMP, gather_t, 0)
    remote(rest_t, rest_t, ta_ssem, ta_rsem, (dp, mp)).wait_send()
    inverse = inverse_factor(g_full[...])
    rest_s = t_gather.at[pl.ds(0, NMP - 1)]
    remote(rest_s, rest_s, tg_ssem, tg_rsem, (dp, mp)).wait_recv()
    for j in range(NMP):
        t_full[4 * j:4 * j + 4, :] = t_gather[j]
    exact = lax.Precision.HIGHEST
    q_next = lax.dot_general(
        t_full[...].T * (1.0 / NDP), inverse, (((1,), (1,)), ((), ())),
        precision=exact, preferred_element_type=F32,
    )[:COLS]
    q_out[...] = q_next
    v_out[...] = lax.dot_general(
        q_next, inverse, (((1,), (0,)), ((), ())), precision=exact, preferred_element_type=F32
    )
    remote(rest_s, rest_s, tg_ssem, tg_rsem, (dp, mp)).wait_send()


def output_kernel(g_ref, e_ref, p_ref, v_ref, q_ref, u_out, e_out, q_out):
    @pl.when(pl.program_id(0) == 0)
    def _():
        q_out[0] = q_ref[...]

    v_high, v_low = split(v_ref[...])
    left = jnp.concatenate([v_high, v_low, v_high], axis=1)
    p_high = p_ref[:RANK, :]
    right = jnp.concatenate([p_high, p_high, p_ref[RANK:, :]], axis=0)
    update = dot(left, right, ((1,), (0,)))
    u_out[...] = update.astype(BF16)
    e_out[0] = g_ref[0].astype(F32) + e_ref[0] - update


def on_device(gradients, errors, q_start):
    vmem = pl.BlockSpec(memory_space=pltpu.VMEM)
    hbm = pl.BlockSpec(memory_space=pl.ANY)
    dma, reg = pltpu.SemaphoreType.DMA, pltpu.SemaphoreType.REGULAR
    p_both, v, q_next = pl.pallas_call(
        round_kernel,
        name="power_round",
        out_shape=(
            jax.ShapeDtypeStruct((2 * RANK, FL), BF16),
            jax.ShapeDtypeStruct((COLS, RANK), F32),
            jax.ShapeDtypeStruct((COLS, RANK), F32),
        ),
        in_specs=[hbm, hbm, vmem],
        out_specs=(vmem, vmem, vmem),
        scratch_shapes=[
            pltpu.VMEM((COLS, FL), BF16),
            pltpu.VMEM((COLS, FL), F32),
            pltpu.VMEM((ROWS_T, FL), BF16),
            pltpu.VMEM((ROWS_T, FL), BF16),
            pltpu.VMEM((NZ, NX, 4, HALF), F32),
            pltpu.VMEM((NZ, NX - 1, 4, HALF), F32),
            pltpu.VMEM((NZ, 4, HALF), F32),
            pltpu.VMEM((NZ - 1, 4, HALF), F32),
            pltpu.VMEM((NZ, NX, 4, HALF), F32),
            pltpu.VMEM((RANK, FL), F32),
            pltpu.VMEM((NMP, 4, ROWS_T), F32),
            pltpu.VMEM((NMP - 1, 4, ROWS_T), F32),
            pltpu.VMEM((4, 256), F32),
            pltpu.VMEM((NDP, 4, 256), F32),
            pltpu.VMEM((NMP, 4, 256), F32),
            pltpu.VMEM((NMP, 4, 128), F32),
            pltpu.VMEM((RANK, 256), F32),
            pltpu.VMEM((RANK, 128), F32),
            dma((NCHUNK, 2)),
            dma, dma((NZ,)), dma, dma, dma, dma((NZ,)), dma, dma,
            dma, dma, dma, dma, dma, dma, dma, dma,
        ],
        compiler_params=pltpu.CompilerParams(
            collective_id=0, has_side_effects=True, vmem_limit_bytes=40 << 20
        ),
    )(gradients, errors, q_start)

    def columns(*lead):
        return pl.BlockSpec(lead + (CHUNK,), lambda i: (0,) * len(lead) + (i,))

    def whole(*shape):
        return pl.BlockSpec(shape, lambda i: (0,) * len(shape))

    return pl.pallas_call(
        output_kernel,
        name="outputs",
        grid=(NCHUNK,),
        out_shape=(
            jax.ShapeDtypeStruct((COLS, FL), BF16),
            jax.ShapeDtypeStruct((1, COLS, FL), F32),
            jax.ShapeDtypeStruct((1, COLS, RANK), F32),
        ),
        in_specs=[
            columns(1, COLS), columns(1, COLS), columns(2 * RANK),
            whole(COLS, RANK), whole(COLS, RANK),
        ],
        out_specs=(columns(COLS), columns(1, COLS), whole(1, COLS, RANK)),
        compiler_params=pltpu.CompilerParams(vmem_limit_bytes=32 << 20),
    )(gradients, errors, p_both, v, q_next)


def solution(mesh):
    return jax.shard_map(
        on_device,
        mesh=mesh,
        in_specs=(P("dp", None, "mp"), P("dp", None, "mp"), P()),
        out_specs=(P(None, "mp"), P("dp", None, "mp"), P()),
        check_vma=False,
    )
```

```python
import jax
import jax.numpy as jnp
from jax import lax
from jax.experimental import pallas as pl
from jax.experimental.pallas import tpu as pltpu
from jax.sharding import PartitionSpec as P

MESH = pl.DeviceIdType.MESH
NX, NZ, NMP = 4, 8, 16
NDP = NX * NZ
COLS, RANK, FL = 240, 64, 1792
CHUNK = 256
NCHUNK = FL // CHUNK
LIMIT = 58 << 20
ROWS_T = 384
F32, BF16 = jnp.float32, jnp.bfloat16
UNITS = FL // 128 * 16
PIECE = UNITS // NDP
NEAR_FIRST = (1, 7, 2, 6, 3, 5, 4)
MP_FAR_FIRST = (9, 8, 7, 10, 11, 6, 5, 12, 13, 4, 3, 14, 15, 2, 1)


def ring(offset, size):
    return min(offset % size, -offset % size)


DP_FAR_FIRST = sorted(
    ((i, j) for i in range(NZ) for j in range(NX) if i or j),
    key=lambda o: (-ring(o[0], NZ) - ring(o[1], NX), -o[0], -o[1]),
)


def split(value):
    high = value.astype(BF16)
    return high, (value - high.astype(F32)).astype(BF16)


def dot(a, b, dims):
    return lax.dot_general(a, b, (dims, ((), ())), preferred_element_type=F32)


def remote(src, dst, send, recv, target):
    return pltpu.make_async_remote_copy(
        src_ref=src, dst_ref=dst, send_sem=send, recv_sem=recv,
        device_id=target, device_id_type=MESH,
    )


def inverse_factor(gram):
    row_at = lax.broadcasted_iota(jnp.int32, (RANK, 2 * RANK), 0)
    col_at = lax.broadcasted_iota(jnp.int32, (RANK, 2 * RANK), 1)
    work = jnp.where(col_at == row_at + RANK, 1.0, gram)
    done = []
    for j in range(RANK):
        base = 8 * (j // 8)
        local = j - base
        pivot = work[local:local + 1, j:j + 1]
        row = work[local:local + 1, :]
        below = lax.broadcasted_iota(jnp.int32, work.shape, 0) > local
        factor = work[:, j:j + 1] / pivot
        work = work - jnp.where(below, factor * row, 0.0)
        if local == 7:
            done.append(work[:8])
            work = work[8:]
    full = jnp.concatenate(done, axis=0)
    diagonal = jnp.sum(jnp.where(col_at == row_at, full, 0.0), axis=1, keepdims=True)
    return (full / jnp.sqrt(diagonal))[:, RANK:]


def round_kernel(g_hbm, e_hbm, q_hbm, m_hbm, p_out, v_out, q_out,
                 g_buf, e_buf, q_buf, m_buf, mh, ml, local_p, x_recv, z_send, z_recv, gathered, p_full,
                 t_send, t_recv, t_part, t_all, t_gather, g_gather, t_full, g_full,
                 load_sem, q_sem, m_sem, x_ssem, x_rsem, z_ssem, z_rsem, az_ssem, az_rsem, ax_ssem, ax_rsem,
                 ts_sem, tr_sem, ta_ssem, ta_rsem, tg_ssem, tg_rsem, gg_ssem, gg_rsem):
    dp = lax.axis_index("dp")
    mp = lax.axis_index("mp")
    z, x = dp // NX, dp % NX

    def place(i):
        c = (z + i) % NCHUNK
        return c, pl.ds(pl.multiple_of(c * CHUNK, CHUNK), CHUNK)

    def load(i):
        cols = place(i)[1]
        return (
            pltpu.make_async_copy(g_hbm.at[0, :, cols], g_buf.at[i], load_sem.at[i, 0]),
            pltpu.make_async_copy(e_hbm.at[0, :, cols], e_buf.at[i], load_sem.at[i, 1]),
        )

    q_copy = pltpu.make_async_copy(q_hbm, q_buf, q_sem)
    q_copy.start()
    for i in range(NCHUNK):
        for copy in load(i):
            copy.start()

    barrier = pltpu.get_barrier_semaphore()

    def greet_dp(k, carry):
        pl.semaphore_signal(barrier, inc=1, device_id=((dp + k) % NDP, mp), device_id_type=MESH)
        return carry

    def greet_mp(k, carry):
        pl.semaphore_signal(barrier, inc=1, device_id=(dp, (mp + k) % NMP), device_id_type=MESH)
        return carry

    lax.fori_loop(1, NDP, greet_dp, 0)
    lax.fori_loop(1, NMP, greet_mp, 0)

    mh[COLS:256, :] = jnp.zeros((256 - COLS, FL), BF16)
    ml[COLS:256, :] = jnp.zeros((256 - COLS, FL), BF16)
    mh[256 + RANK:, :] = jnp.zeros((ROWS_T - 256 - RANK, FL), BF16)
    ml[256 + RANK:, :] = jnp.zeros((ROWS_T - 256 - RANK, FL), BF16)
    q_copy.wait()
    q_high, q_low = split(q_buf[0])
    q_both = jnp.concatenate([q_high, q_low], axis=0)

    def piece(t, to):
        return pl.ds((t * NX + to) * PIECE, PIECE)

    def send_x(k):
        t = (z + 1 + k) % NZ
        for i in (2, 1, 3):
            to = (x + i) % NX
            remote(local_p.at[piece(t, to)], x_recv.at[t, i - 1], x_ssem, x_rsem.at[t], (z * NX + to, mp)).start()

    for i in range(NCHUNK):
        c, cols = place(i)
        for copy in load(i):
            copy.wait()
        merged = g_buf[i].astype(F32) + e_buf[i]
        m_buf[i] = merged
        high, low = split(merged)
        mh[:COLS, cols] = high
        ml[:COLS, cols] = low
        both = dot(q_both, high, ((1,), (0,)))
        part = both[:RANK] + both[RANK:] + dot(q_high, low, ((1,), (0,)))
        for j in range(CHUNK // 128):
            for group in range(RANK // 4):
                unit = part[4 * group:4 * group + 4, 128 * j:128 * (j + 1)]
                local_p[c * 32 + (j * 16 + group)] = unit
        if i == 0:
            pl.semaphore_wait(barrier, NDP - 1 + NMP - 1)
        else:
            send_x(i - 1)
    send_x(NCHUNK - 1)
    send_x(NCHUNK)
    for i in range(NCHUNK):
        pltpu.make_async_copy(m_buf.at[i], m_hbm.at[:, place(i)[1]], m_sem).start()

    for k in range(NZ):
        t = (z + 1 + k) % NZ
        remote(x_recv.at[t], x_recv.at[t], x_ssem, x_rsem.at[t], (dp, mp)).wait_recv()
        z_send[k] = local_p[piece(t, x)] + x_recv[t, 0] + x_recv[t, 1] + x_recv[t, 2]
        if k < NZ - 1:
            remote(z_send.at[k], z_recv.at[k], z_ssem, z_rsem, (t * NX + x, mp)).start()
    remote(z_recv, z_recv, z_ssem, z_rsem, (dp, mp)).wait_recv()
    mean = z_send[NZ - 1]
    for k in range(NZ - 1):
        mean = mean + z_recv[k]
    gathered[piece(z, x)] = mean * (1.0 / NDP)

    for k in NEAR_FIRST:
        remote(gathered.at[piece(z, x)], gathered.at[piece(z, x)], az_ssem, az_rsem.at[k], ((z + k) % NZ * NX + x, mp)).start()

    def on_to_x(t):
        for i in range(1, NX):
            remote(gathered.at[piece(t, x)], gathered.at[piece(t, x)], ax_ssem, ax_rsem, (z * NX + (x + i) % NX, mp)).start()

    on_to_x(z)
    remote(x_recv, x_recv, x_ssem, x_rsem.at[0], (dp, mp)).wait_send()
    remote(z_recv, z_recv, z_ssem, z_rsem, (dp, mp)).wait_send()
    for k in NEAR_FIRST:
        t = (z + NZ - k) % NZ
        remote(gathered.at[piece(t, x)], gathered.at[piece(t, x)], az_ssem, az_rsem.at[k], (dp, mp)).wait_recv()
        on_to_x(t)
    remote(x_recv, x_recv, ax_ssem, ax_rsem, (dp, mp)).wait_recv()

    for j in range(FL // 128):
        for group in range(RANK // 4):
            p_full[4 * group:4 * group + 4, 128 * j:128 * (j + 1)] = gathered[16 * j + group]
    p_high, p_low = split(p_full[...])
    p_out[:RANK, :] = p_high
    p_out[RANK:, :] = p_low
    mh[256:256 + RANK, :] = p_high
    ml[256:256 + RANK, :] = p_low

    both = dot(p_out[...], mh[...], ((1,), (1,)))
    t_local = both[:RANK] + both[RANK:] + dot(p_out[:RANK, :], ml[...], ((1,), (1,)))
    for j in range(NMP):
        t_send[j] = t_local[4 * j:4 * j + 4]

    for k in MP_FAR_FIRST:
        to = (mp + k) % NMP
        remote(t_send.at[to], t_recv.at[k - 1], ts_sem, tr_sem, (dp, to)).start()
    remote(x_recv, x_recv, ax_ssem, ax_rsem, (dp, mp)).wait_send()
    remote(z_recv, z_recv, az_ssem, az_rsem.at[1], (dp, mp)).wait_send()
    remote(t_recv, t_recv, ts_sem, tr_sem, (dp, mp)).wait_recv()
    slice_sum = t_send[mp]
    for k in range(NMP - 1):
        slice_sum = slice_sum + t_recv[k]
    t_all[dp] = slice_sum[:, :256]
    t_part[...] = slice_sum[:, :256]
    g_gather[mp] = slice_sum[:, 256:]

    for i, j in DP_FAR_FIRST:
        to = (z + i) % NZ * NX + (x + j) % NX
        remote(t_part, t_all.at[dp], ta_ssem, ta_rsem, (to, mp)).start()
    for k in MP_FAR_FIRST:
        remote(g_gather.at[mp], g_gather.at[mp], gg_ssem, gg_rsem, (dp, (mp + k) % NMP)).start()
    rest_g = g_gather.at[pl.ds(0, NMP - 1)]
    remote(rest_g, rest_g, gg_ssem, gg_rsem, (dp, mp)).wait_recv()
    for j in range(NMP):
        g_full[4 * j:4 * j + 4, :] = g_gather[j]
    remote(t_recv, t_recv, ts_sem, tr_sem, (dp, mp)).wait_send()
    remote(rest_g, rest_g, gg_ssem, gg_rsem, (dp, mp)).wait_send()

    rest_t = t_all.at[pl.ds(0, NDP - 1)]
    remote(rest_t, rest_t, ta_ssem, ta_rsem, (dp, mp)).wait_recv()
    total = t_all[0]
    for k in range(1, NDP):
        total = total + t_all[k]
    t_gather[mp] = total

    for k in MP_FAR_FIRST:
        remote(t_gather.at[mp], t_gather.at[mp], tg_ssem, tg_rsem, (dp, (mp + k) % NMP)).start()
    remote(rest_t, rest_t, ta_ssem, ta_rsem, (dp, mp)).wait_send()
    inverse = inverse_factor(g_full[...])
    rest_s = t_gather.at[pl.ds(0, NMP - 1)]
    remote(rest_s, rest_s, tg_ssem, tg_rsem, (dp, mp)).wait_recv()
    for j in range(NMP):
        t_full[4 * j:4 * j + 4, :] = t_gather[j]
    exact = lax.Precision.HIGHEST
    q_rows = lax.dot_general(
        inverse, t_full[...] * (1.0 / NDP), (((1,), (0,)), ((), ())),
        precision=exact, preferred_element_type=F32,
    )[:, :COLS]
    q_out[0] = q_rows
    v_out[...] = lax.dot_general(
        q_rows, inverse, (((0,), (0,)), ((), ())), precision=exact, preferred_element_type=F32
    )
    remote(rest_s, rest_s, tg_ssem, tg_rsem, (dp, mp)).wait_send()
    pltpu.make_async_copy(m_hbm, m_hbm, m_sem).wait()


def output_kernel(m_hbm, p_hbm, v_hbm, q_hbm, u_hbm, e_hbm, q_out,
                  m_buf, p_buf, v_buf, u_buf, e_buf, load_sem, small_sem, store_sem):
    small = (
        pltpu.make_async_copy(v_hbm, v_buf, small_sem.at[0]),
        pltpu.make_async_copy(p_hbm, p_buf, small_sem.at[1]),
    )
    for copy in small:
        copy.start()

    def load(c):
        cols = pl.ds(c * CHUNK, CHUNK)
        return pltpu.make_async_copy(m_hbm.at[:, cols], m_buf.at[:, cols], load_sem.at[c])

    for c in range(NCHUNK):
        load(c).start()
    q_copy = pltpu.make_async_copy(q_hbm, q_out, small_sem.at[2])
    q_copy.start()
    for copy in small:
        copy.wait()
    v_high, v_low = split(v_buf[...])
    left = jnp.concatenate([v_high, v_low, v_high], axis=1)

    def store(c):
        cols = pl.ds(c * CHUNK, CHUNK)
        return (
            pltpu.make_async_copy(u_buf.at[:, cols], u_hbm.at[:, cols], store_sem.at[c, 0]),
            pltpu.make_async_copy(e_buf.at[:, cols], e_hbm.at[0, :, cols], store_sem.at[c, 1]),
        )

    for c in range(NCHUNK):
        cols = slice(c * CHUNK, (c + 1) * CHUNK)
        p_high = p_buf[:RANK, cols]
        right = jnp.concatenate([p_high, p_high, p_buf[RANK:, cols]], axis=0)
        update = dot(left, right, ((1,), (0,)))
        load(c).wait()
        u_buf[:, cols] = update.astype(BF16)
        e_buf[:, cols] = m_buf[:, cols] - update
        for copy in store(c):
            copy.start()
    q_copy.wait()
    for c in range(NCHUNK):
        for copy in store(c):
            copy.wait()


def on_device(gradients, errors, q_start):
    vmem = pl.BlockSpec(memory_space=pltpu.VMEM)
    hbm = pl.BlockSpec(memory_space=pl.ANY)
    dma, reg = pltpu.SemaphoreType.DMA, pltpu.SemaphoreType.REGULAR
    merged, p_both, v, q_rows = pl.pallas_call(
        round_kernel,
        name="power_round",
        out_shape=(
            jax.ShapeDtypeStruct((COLS, FL), F32),
            jax.ShapeDtypeStruct((2 * RANK, FL), BF16),
            jax.ShapeDtypeStruct((COLS, RANK), F32),
            jax.ShapeDtypeStruct((1, RANK, COLS), F32),
        ),
        in_specs=[hbm, hbm, hbm],
        out_specs=(hbm, vmem, vmem, vmem),
        scratch_shapes=[
            pltpu.VMEM((NCHUNK, COLS, CHUNK), BF16),
            pltpu.VMEM((NCHUNK, COLS, CHUNK), F32),
            pltpu.VMEM((1, RANK, COLS), F32),
            pltpu.VMEM((NCHUNK, COLS, CHUNK), F32),
            pltpu.VMEM((ROWS_T, FL), BF16),
            pltpu.VMEM((ROWS_T, FL), BF16),
            pltpu.VMEM((UNITS, 4, 128), F32),
            pltpu.VMEM((NZ, NX - 1, PIECE, 4, 128), F32),
            pltpu.VMEM((NZ, PIECE, 4, 128), F32),
            pltpu.VMEM((NZ - 1, PIECE, 4, 128), F32),
            pltpu.VMEM((UNITS, 4, 128), F32),
            pltpu.VMEM((RANK, FL), F32),
            pltpu.VMEM((NMP, 4, ROWS_T), F32),
            pltpu.VMEM((NMP - 1, 4, ROWS_T), F32),
            pltpu.VMEM((4, 256), F32),
            pltpu.VMEM((NDP, 4, 256), F32),
            pltpu.VMEM((NMP, 4, 256), F32),
            pltpu.VMEM((NMP, 4, 128), F32),
            pltpu.VMEM((RANK, 256), F32),
            pltpu.VMEM((RANK, 128), F32),
            dma((NCHUNK, 2)), dma, dma,
            dma, dma((NZ,)), dma, dma, dma, dma((NZ,)), dma, dma,
            dma, dma, dma, dma, dma, dma, dma, dma,
        ],
        compiler_params=pltpu.CompilerParams(
            collective_id=0, has_side_effects=True, vmem_limit_bytes=LIMIT
        ),
    )(gradients, errors, jnp.swapaxes(q_start, 1, 2))

    update_grad, new_errors, q_rows = pl.pallas_call(
        output_kernel,
        name="outputs",
        out_shape=(
            jax.ShapeDtypeStruct((COLS, FL), BF16),
            jax.ShapeDtypeStruct((1, COLS, FL), F32),
            jax.ShapeDtypeStruct((1, RANK, COLS), F32),
        ),
        in_specs=[hbm, hbm, hbm, hbm],
        out_specs=(hbm, hbm, hbm),
        scratch_shapes=[
            pltpu.VMEM((COLS, FL), F32),
            pltpu.VMEM((2 * RANK, FL), BF16),
            pltpu.VMEM((COLS, RANK), F32),
            pltpu.VMEM((COLS, FL), BF16),
            pltpu.VMEM((COLS, FL), F32),
            dma((NCHUNK,)), dma((3,)), dma((NCHUNK, 2)),
        ],
        compiler_params=pltpu.CompilerParams(vmem_limit_bytes=LIMIT),
    )(merged, p_both, v, q_rows)
    return update_grad, new_errors, jnp.swapaxes(q_rows, 1, 2)


def solution(mesh):
    return jax.shard_map(
        on_device,
        mesh=mesh,
        in_specs=(P("dp", None, "mp"), P("dp", None, "mp"), P()),
        out_specs=(P(None, "mp"), P("dp", None, "mp"), P()),
        check_vma=False,
    )
```

```python
import jax
import jax.numpy as jnp
from jax import lax
from jax.experimental import pallas as pl
from jax.experimental.pallas import tpu as pltpu
from jax.sharding import PartitionSpec as P

MESH = pl.DeviceIdType.MESH
NX, NZ, NMP = 4, 8, 16
NDP = NX * NZ
COLS, RANK, FL = 240, 64, 1792
CHUNK = 256
NCHUNK = FL // CHUNK
LIMIT = 30 << 20
ROWS_T = 384
F32, BF16 = jnp.float32, jnp.bfloat16
UNITS = FL // 128 * 16
PIECE = UNITS // NDP
NEAR_FIRST = (1, 7, 2, 6, 3, 5, 4)
MP_FAR_FIRST = (9, 8, 7, 10, 11, 6, 5, 12, 13, 4, 3, 14, 15, 2, 1)


def ring(offset, size):
    return min(offset % size, -offset % size)


DP_FAR_FIRST = sorted(
    ((i, j) for i in range(NZ) for j in range(NX) if i or j),
    key=lambda o: (-ring(o[0], NZ) - ring(o[1], NX), -o[0], -o[1]),
)


def split(value):
    high = value.astype(BF16)
    return high, (value - high.astype(F32)).astype(BF16)


def dot(a, b, dims):
    return lax.dot_general(a, b, (dims, ((), ())), preferred_element_type=F32)


def remote(src, dst, send, recv, target):
    return pltpu.make_async_remote_copy(
        src_ref=src, dst_ref=dst, send_sem=send, recv_sem=recv,
        device_id=target, device_id_type=MESH,
    )


def inverse_factor(gram):
    row_at = lax.broadcasted_iota(jnp.int32, (RANK, 2 * RANK), 0)
    col_at = lax.broadcasted_iota(jnp.int32, (RANK, 2 * RANK), 1)
    work = jnp.where(col_at == row_at + RANK, 1.0, gram)
    done = []
    for j in range(RANK):
        base = 8 * (j // 8)
        local = j - base
        pivot = work[local:local + 1, j:j + 1]
        row = work[local:local + 1, :]
        below = lax.broadcasted_iota(jnp.int32, work.shape, 0) > local
        factor = work[:, j:j + 1] / pivot
        work = work - jnp.where(below, factor * row, 0.0)
        if local == 7:
            done.append(work[:8])
            work = work[8:]
    full = jnp.concatenate(done, axis=0)
    diagonal = jnp.sum(jnp.where(col_at == row_at, full, 0.0), axis=1, keepdims=True)
    return (full / jnp.sqrt(diagonal))[:, RANK:]


def round_kernel(g_hbm, e_hbm, q_hbm, m_out, p_out, v_out, q_out,
                 g_buf, e_buf, q_buf, mh, ml, local_p, x_recv, z_send, z_recv, gathered, p_full,
                 t_send, t_recv, t_part, t_all, t_gather, g_gather, t_full, g_full,
                 load_sem, q_sem, x_ssem, x_rsem, z_ssem, z_rsem, az_ssem, az_rsem, ax_ssem, ax_rsem,
                 ts_sem, tr_sem, ta_ssem, ta_rsem, tg_ssem, tg_rsem, gg_ssem, gg_rsem):
    dp = lax.axis_index("dp")
    mp = lax.axis_index("mp")
    z, x = dp // NX, dp % NX

    def place(i):
        c = (z + i) % NCHUNK
        return c, pl.ds(pl.multiple_of(c * CHUNK, CHUNK), CHUNK)

    def load(i):
        cols = place(i)[1]
        return (
            pltpu.make_async_copy(g_hbm.at[0, :, cols], g_buf.at[i], load_sem.at[i, 0]),
            pltpu.make_async_copy(e_hbm.at[0, :, cols], e_buf.at[i], load_sem.at[i, 1]),
        )

    q_copy = pltpu.make_async_copy(q_hbm, q_buf, q_sem)
    q_copy.start()
    for i in range(NCHUNK):
        for copy in load(i):
            copy.start()

    barrier = pltpu.get_barrier_semaphore()

    def greet_dp(k, carry):
        pl.semaphore_signal(barrier, inc=1, device_id=((dp + k) % NDP, mp), device_id_type=MESH)
        return carry

    def greet_mp(k, carry):
        pl.semaphore_signal(barrier, inc=1, device_id=(dp, (mp + k) % NMP), device_id_type=MESH)
        return carry

    lax.fori_loop(1, NDP, greet_dp, 0)
    lax.fori_loop(1, NMP, greet_mp, 0)

    t_send[:, :, 256 + RANK:] = jnp.zeros((NMP, 4, ROWS_T - 256 - RANK), F32)
    mh[COLS:256, :] = jnp.zeros((256 - COLS, FL), BF16)
    ml[COLS:256, :] = jnp.zeros((256 - COLS, FL), BF16)
    q_copy.wait()
    q_high, q_low = split(q_buf[0])
    q_both = jnp.concatenate([q_high, q_low], axis=0)

    def piece(t, to):
        return pl.ds((t * NX + to) * PIECE, PIECE)

    def send_x(k):
        t = (z + 1 + k) % NZ
        for i in (2, 1, 3):
            to = (x + i) % NX
            remote(local_p.at[piece(t, to)], x_recv.at[t, i - 1], x_ssem, x_rsem.at[t], (z * NX + to, mp)).start()

    for i in range(NCHUNK):
        c, cols = place(i)
        for copy in load(i):
            copy.wait()
        merged = g_buf[i].astype(F32) + e_buf[i]
        m_out[:, cols] = merged
        high, low = split(merged)
        mh[:COLS, cols] = high
        ml[:COLS, cols] = low
        both = dot(q_both, high, ((1,), (0,)))
        part = both[:RANK] + both[RANK:] + dot(q_high, low, ((1,), (0,)))
        for j in range(CHUNK // 128):
            for group in range(RANK // 4):
                unit = part[4 * group:4 * group + 4, 128 * j:128 * (j + 1)]
                local_p[c * 32 + (j * 16 + group)] = unit
        if i == 0:
            pl.semaphore_wait(barrier, NDP - 1 + NMP - 1)
        else:
            send_x(i - 1)
    send_x(NCHUNK - 1)
    send_x(NCHUNK)

    for k in range(NZ):
        t = (z + 1 + k) % NZ
        remote(x_recv.at[t], x_recv.at[t], x_ssem, x_rsem.at[t], (dp, mp)).wait_recv()
        z_send[k] = local_p[piece(t, x)] + x_recv[t, 0] + x_recv[t, 1] + x_recv[t, 2]
        if k < NZ - 1:
            remote(z_send.at[k], z_recv.at[k], z_ssem, z_rsem, (t * NX + x, mp)).start()
    remote(z_recv, z_recv, z_ssem, z_rsem, (dp, mp)).wait_recv()
    mean = z_send[NZ - 1]
    for k in range(NZ - 1):
        mean = mean + z_recv[k]
    gathered[piece(z, x)] = mean * (1.0 / NDP)

    for k in NEAR_FIRST:
        remote(gathered.at[piece(z, x)], gathered.at[piece(z, x)], az_ssem, az_rsem.at[k], ((z + k) % NZ * NX + x, mp)).start()

    def on_to_x(t):
        for i in range(1, NX):
            remote(gathered.at[piece(t, x)], gathered.at[piece(t, x)], ax_ssem, ax_rsem, (z * NX + (x + i) % NX, mp)).start()

    on_to_x(z)
    remote(x_recv, x_recv, x_ssem, x_rsem.at[0], (dp, mp)).wait_send()
    remote(z_recv, z_recv, z_ssem, z_rsem, (dp, mp)).wait_send()
    for k in NEAR_FIRST:
        t = (z + NZ - k) % NZ
        remote(gathered.at[piece(t, x)], gathered.at[piece(t, x)], az_ssem, az_rsem.at[k], (dp, mp)).wait_recv()
        on_to_x(t)
    remote(x_recv, x_recv, ax_ssem, ax_rsem, (dp, mp)).wait_recv()

    for j in range(FL // 128):
        for group in range(RANK // 4):
            p_full[4 * group:4 * group + 4, 128 * j:128 * (j + 1)] = gathered[16 * j + group]
    p_high, p_low = split(p_full[...])
    p_out[:RANK, :] = p_high
    p_out[RANK:, :] = p_low
    both = dot(p_out[...], mh[...], ((1,), (1,)))
    t_local = both[:RANK] + both[RANK:] + dot(p_out[:RANK, :], ml[...], ((1,), (1,)))
    both = dot(p_out[...], p_out[...], ((1,), (1,)))
    g_local = both[:RANK, :RANK] + both[:RANK, RANK:] + both[RANK:, :RANK]
    for j in range(NMP):
        t_send[j, :, :256] = t_local[4 * j:4 * j + 4]
        t_send[j, :, 256:256 + RANK] = g_local[4 * j:4 * j + 4]

    for k in MP_FAR_FIRST:
        to = (mp + k) % NMP
        remote(t_send.at[to], t_recv.at[k - 1], ts_sem, tr_sem, (dp, to)).start()
    remote(x_recv, x_recv, ax_ssem, ax_rsem, (dp, mp)).wait_send()
    remote(z_recv, z_recv, az_ssem, az_rsem.at[1], (dp, mp)).wait_send()
    remote(t_recv, t_recv, ts_sem, tr_sem, (dp, mp)).wait_recv()
    slice_sum = t_send[mp]
    for k in range(NMP - 1):
        slice_sum = slice_sum + t_recv[k]
    t_all[dp] = slice_sum[:, :256]
    t_part[...] = slice_sum[:, :256]
    g_gather[mp] = slice_sum[:, 256:]

    for i, j in DP_FAR_FIRST:
        to = (z + i) % NZ * NX + (x + j) % NX
        remote(t_part, t_all.at[dp], ta_ssem, ta_rsem, (to, mp)).start()
    for k in MP_FAR_FIRST:
        remote(g_gather.at[mp], g_gather.at[mp], gg_ssem, gg_rsem, (dp, (mp + k) % NMP)).start()
    rest_g = g_gather.at[pl.ds(0, NMP - 1)]
    remote(rest_g, rest_g, gg_ssem, gg_rsem, (dp, mp)).wait_recv()
    for j in range(NMP):
        g_full[4 * j:4 * j + 4, :] = g_gather[j]
    remote(t_recv, t_recv, ts_sem, tr_sem, (dp, mp)).wait_send()
    remote(rest_g, rest_g, gg_ssem, gg_rsem, (dp, mp)).wait_send()

    rest_t = t_all.at[pl.ds(0, NDP - 1)]
    remote(rest_t, rest_t, ta_ssem, ta_rsem, (dp, mp)).wait_recv()
    total = t_all[0]
    for k in range(1, NDP):
        total = total + t_all[k]
    t_gather[mp] = total

    for k in MP_FAR_FIRST:
        remote(t_gather.at[mp], t_gather.at[mp], tg_ssem, tg_rsem, (dp, (mp + k) % NMP)).start()
    remote(rest_t, rest_t, ta_ssem, ta_rsem, (dp, mp)).wait_send()
    inverse = inverse_factor(g_full[...])
    rest_s = t_gather.at[pl.ds(0, NMP - 1)]
    remote(rest_s, rest_s, tg_ssem, tg_rsem, (dp, mp)).wait_recv()
    for j in range(NMP):
        t_full[4 * j:4 * j + 4, :] = t_gather[j]
    exact = lax.Precision.HIGHEST
    q_rows = lax.dot_general(
        inverse, t_full[...] * (1.0 / NDP), (((1,), (0,)), ((), ())),
        precision=exact, preferred_element_type=F32,
    )[:, :COLS]
    q_out[0] = q_rows
    v_out[...] = lax.dot_general(
        q_rows, inverse, (((0,), (0,)), ((), ())), precision=exact, preferred_element_type=F32
    )
    remote(rest_s, rest_s, tg_ssem, tg_rsem, (dp, mp)).wait_send()


def output_kernel(m_ref, p_ref, v_ref, q_ref, u_hbm, e_hbm, q_out, u_buf, e_buf, store_sem):
    v_high, v_low = split(v_ref[...])
    left = jnp.concatenate([v_high, v_low, v_high], axis=1)

    def store(c):
        cols = pl.ds(c * CHUNK, CHUNK)
        return (
            pltpu.make_async_copy(u_buf.at[:, cols], u_hbm.at[:, cols], store_sem.at[c, 0]),
            pltpu.make_async_copy(e_buf.at[:, cols], e_hbm.at[0, :, cols], store_sem.at[c, 1]),
        )

    for c in range(NCHUNK):
        cols = slice(c * CHUNK, (c + 1) * CHUNK)
        p_high = p_ref[:RANK, cols]
        right = jnp.concatenate([p_high, p_high, p_ref[RANK:, cols]], axis=0)
        update = dot(left, right, ((1,), (0,)))
        u_buf[:, cols] = update.astype(BF16)
        e_buf[:, cols] = m_ref[:, cols] - update
        for copy in store(c):
            copy.start()
    q_out[...] = q_ref[...]
    for c in range(NCHUNK):
        for copy in store(c):
            copy.wait()


def on_device(gradients, errors, q_start):
    vmem = pl.BlockSpec(memory_space=pltpu.VMEM)
    hbm = pl.BlockSpec(memory_space=pl.ANY)
    dma, reg = pltpu.SemaphoreType.DMA, pltpu.SemaphoreType.REGULAR
    merged, p_both, v, q_rows = pl.pallas_call(
        round_kernel,
        name="power_round",
        out_shape=(
            jax.ShapeDtypeStruct((COLS, FL), F32),
            jax.ShapeDtypeStruct((2 * RANK, FL), BF16),
            jax.ShapeDtypeStruct((COLS, RANK), F32),
            jax.ShapeDtypeStruct((1, RANK, COLS), F32),
        ),
        in_specs=[hbm, hbm, hbm],
        out_specs=(vmem, vmem, vmem, vmem),
        scratch_shapes=[
            pltpu.VMEM((NCHUNK, COLS, CHUNK), BF16),
            pltpu.VMEM((NCHUNK, COLS, CHUNK), F32),
            pltpu.VMEM((1, RANK, COLS), F32),
            pltpu.VMEM((256, FL), BF16),
            pltpu.VMEM((256, FL), BF16),
            pltpu.VMEM((UNITS, 4, 128), F32),
            pltpu.VMEM((NZ, NX - 1, PIECE, 4, 128), F32),
            pltpu.VMEM((NZ, PIECE, 4, 128), F32),
            pltpu.VMEM((NZ - 1, PIECE, 4, 128), F32),
            pltpu.VMEM((UNITS, 4, 128), F32),
            pltpu.VMEM((RANK, FL), F32),
            pltpu.VMEM((NMP, 4, ROWS_T), F32),
            pltpu.VMEM((NMP - 1, 4, ROWS_T), F32),
            pltpu.VMEM((4, 256), F32),
            pltpu.VMEM((NDP, 4, 256), F32),
            pltpu.VMEM((NMP, 4, 256), F32),
            pltpu.VMEM((NMP, 4, 128), F32),
            pltpu.VMEM((RANK, 256), F32),
            pltpu.VMEM((RANK, 128), F32),
            dma((NCHUNK, 2)), dma,
            dma, dma((NZ,)), dma, dma, dma, dma((NZ,)), dma, dma,
            dma, dma, dma, dma, dma, dma, dma, dma,
        ],
        compiler_params=pltpu.CompilerParams(
            collective_id=0, has_side_effects=True, vmem_limit_bytes=LIMIT
        ),
    )(*(pltpu.with_memory_space_constraint(a, pltpu.HBM) for a in (gradients, errors, jnp.swapaxes(q_start, 1, 2))))

    update_grad, new_errors, q_rows = pl.pallas_call(
        output_kernel,
        name="outputs",
        out_shape=(
            jax.ShapeDtypeStruct((COLS, FL), BF16),
            jax.ShapeDtypeStruct((1, COLS, FL), F32),
            jax.ShapeDtypeStruct((1, RANK, COLS), F32),
        ),
        in_specs=[vmem, vmem, vmem, vmem],
        out_specs=(hbm, hbm, vmem),
        scratch_shapes=[
            pltpu.VMEM((COLS, FL), BF16),
            pltpu.VMEM((COLS, FL), F32),
            dma((NCHUNK, 2)),
        ],
        compiler_params=pltpu.CompilerParams(vmem_limit_bytes=LIMIT),
    )(merged, p_both, v, q_rows)
    return update_grad, new_errors, jnp.swapaxes(q_rows, 1, 2)


def solution(mesh):
    return jax.shard_map(
        on_device,
        mesh=mesh,
        in_specs=(P("dp", None, "mp"), P("dp", None, "mp"), P()),
        out_specs=(P(None, "mp"), P("dp", None, "mp"), P()),
        check_vma=False,
    )
```

```python
import functools

import jax
import jax.numpy as jnp
from jax import lax
from jax.experimental import pallas as pl
from jax.experimental.pallas import tpu as pltpu
from jax.sharding import PartitionSpec as P

MESH = pl.DeviceIdType.MESH
NX, NZ, NMP = 4, 8, 16
NDP = NX * NZ
COLS, RANK, FL = 240, 64, 1792
CHUNK = 256
NCHUNK = FL // CHUNK
LIMIT = 30 << 20
ROWS_T = 384
F32, BF16 = jnp.float32, jnp.bfloat16
UNITS = FL // 128 * 16
PIECE = UNITS // NDP
NEAR_FIRST = (1, 7, 2, 6, 3, 5, 4)
MP_FAR_FIRST = (9, 8, 7, 10, 11, 6, 5, 12, 13, 4, 3, 14, 15, 2, 1)


def ring(offset, size):
    return min(offset % size, -offset % size)


DP_FAR_FIRST = sorted(
    ((i, j) for i in range(NZ) for j in range(NX) if i or j),
    key=lambda o: (-ring(o[0], NZ) - ring(o[1], NX), -o[0], -o[1]),
)


def split(value):
    high = value.astype(BF16)
    return high, (value - high.astype(F32)).astype(BF16)


def dot(a, b, dims):
    return lax.dot_general(a, b, (dims, ((), ())), preferred_element_type=F32)


def remote(src, dst, send, recv, target):
    return pltpu.make_async_remote_copy(
        src_ref=src, dst_ref=dst, send_sem=send, recv_sem=recv,
        device_id=target, device_id_type=MESH,
    )


def inverse_factor(gram):
    row_at = lax.broadcasted_iota(jnp.int32, (RANK, 2 * RANK), 0)
    col_at = lax.broadcasted_iota(jnp.int32, (RANK, 2 * RANK), 1)
    work = jnp.where(col_at == row_at + RANK, 1.0, gram)
    done = []
    for j in range(RANK):
        base = 8 * (j // 8)
        local = j - base
        pivot = work[local:local + 1, j:j + 1]
        row = work[local:local + 1, :]
        below = lax.broadcasted_iota(jnp.int32, work.shape, 0) > local
        factor = work[:, j:j + 1] / pivot
        work = work - jnp.where(below, factor * row, 0.0)
        if local == 7:
            done.append(work[:8])
            work = work[8:]
    full = jnp.concatenate(done, axis=0)
    diagonal = jnp.sum(jnp.where(col_at == row_at, full, 0.0), axis=1, keepdims=True)
    return (full / jnp.sqrt(diagonal))[:, RANK:]


def round_kernel(g_hbm, e_hbm, q_hbm, m_out, p_out, v_out, q_out,
                 g_buf, e_buf, q_buf, mh, ml, local_p, x_recv, z_send, z_recv, gathered, p_full,
                 t_send, t_recv, t_part, t_all, t_gather, g_gather, t_full, g_full,
                 load_sem, q_sem, x_ssem, x_rsem, z_ssem, z_rsem, az_ssem, az_rsem, ax_ssem, ax_rsem,
                 ts_sem, tr_sem, ta_ssem, ta_rsem, tg_ssem, tg_rsem, gg_ssem, gg_rsem):
    dp = lax.axis_index("dp")
    mp = lax.axis_index("mp")
    z, x = dp // NX, dp % NX

    barrier = pltpu.get_barrier_semaphore()

    def greet(target):
        pl.semaphore_signal(barrier, inc=1, device_id=target, device_id_type=MESH)

    for k in reversed(NEAR_FIRST):
        greet(((z + k) % NZ * NX + x, mp))
    for k in MP_FAR_FIRST:
        greet((dp, (mp + k) % NMP))
    for i in (2, 1, 3):
        greet((z * NX + (x + i) % NX, mp))

    def place(i):
        c = (z + i) % NCHUNK
        return c, pl.ds(pl.multiple_of(c * CHUNK, CHUNK), CHUNK)

    def load(i):
        cols = place(i)[1]
        return (
            pltpu.make_async_copy(g_hbm.at[0, :, cols], g_buf.at[i], load_sem.at[i, 0]),
            pltpu.make_async_copy(e_hbm.at[0, :, cols], e_buf.at[i], load_sem.at[i, 1]),
        )

    q_copy = pltpu.make_async_copy(q_hbm, q_buf, q_sem)
    q_copy.start()
    for i in range(NCHUNK):
        for copy in load(i):
            copy.start()

    mh[COLS:256, :] = jnp.zeros((256 - COLS, FL), BF16)
    ml[COLS:256, :] = jnp.zeros((256 - COLS, FL), BF16)
    q_copy.wait()
    q_high, q_low = split(q_buf[0])
    q_both = jnp.concatenate([q_high, q_low], axis=0)

    def piece(t, to):
        return pl.ds((t * NX + to) * PIECE, PIECE)

    def send_x(k):
        t = (z + 1 + k) % NZ
        for i in (2, 1, 3):
            to = (x + i) % NX
            remote(local_p.at[piece(t, to)], x_recv.at[t, i - 1], x_ssem, x_rsem.at[t], (z * NX + to, mp)).start()

    for i in range(NCHUNK):
        c, cols = place(i)
        for copy in load(i):
            copy.wait()
        merged = g_buf[i].astype(F32) + e_buf[i]
        m_out[:, cols] = merged
        high, low = split(merged)
        mh[:COLS, cols] = high
        ml[:COLS, cols] = low
        both = dot(q_both, high, ((1,), (0,)))
        part = both[:RANK] + both[RANK:] + dot(q_high, low, ((1,), (0,)))
        for j in range(CHUNK // 128):
            for group in range(RANK // 4):
                unit = part[4 * group:4 * group + 4, 128 * j:128 * (j + 1)]
                local_p[c * 32 + (j * 16 + group)] = unit
        if i == 1:
            pl.semaphore_wait(barrier, NX - 1 + NZ - 1 + NMP - 1)
        if i:
            send_x(i - 1)
    send_x(NCHUNK - 1)
    send_x(NCHUNK)

    for k in range(NZ):
        t = (z + 1 + k) % NZ
        remote(x_recv.at[t], x_recv.at[t], x_ssem, x_rsem.at[t], (dp, mp)).wait_recv()
        z_send[k] = local_p[piece(t, x)] + x_recv[t, 0] + x_recv[t, 1] + x_recv[t, 2]
        if k < NZ - 1:
            remote(z_send.at[k], z_recv.at[k], z_ssem, z_rsem, (t * NX + x, mp)).start()
    remote(z_recv, z_recv, z_ssem, z_rsem, (dp, mp)).wait_recv()
    mean = z_send[NZ - 1]
    for k in range(NZ - 1):
        mean = mean + z_recv[k]
    gathered[piece(z, x)] = mean * (1.0 / NDP)

    for k in NEAR_FIRST:
        remote(gathered.at[piece(z, x)], gathered.at[piece(z, x)], az_ssem, az_rsem.at[k], ((z + k) % NZ * NX + x, mp)).start()

    def on_to_x(t):
        for i in range(1, NX):
            remote(gathered.at[piece(t, x)], gathered.at[piece(t, x)], ax_ssem, ax_rsem.at[t], (z * NX + (x + i) % NX, mp)).start()

    on_to_x(z)
    remote(x_recv, x_recv, x_ssem, x_rsem.at[0], (dp, mp)).wait_send()
    remote(z_recv, z_recv, z_ssem, z_rsem, (dp, mp)).wait_send()
    for k in NEAR_FIRST:
        t = (z + NZ - k) % NZ
        remote(gathered.at[piece(t, x)], gathered.at[piece(t, x)], az_ssem, az_rsem.at[k], (dp, mp)).wait_recv()
        on_to_x(t)

    def accumulate(c):
        cols = pl.ds(pl.multiple_of(c * CHUNK, CHUNK), CHUNK)
        for j in range(CHUNK // 128):
            for group in range(RANK // 4):
                p_full[4 * group:4 * group + 4, 128 * j:128 * (j + 1)] = gathered[c * 32 + (j * 16 + group)]
        p_high, p_low = split(p_full[...])
        p_out[:RANK, cols] = p_high
        p_out[RANK:, cols] = p_low
        p_both = jnp.concatenate([p_high, p_low], axis=0)
        both = dot(p_both, mh[:, cols], ((1,), (1,)))
        t_full[...] += both[:RANK] + both[RANK:] + dot(p_high, ml[:, cols], ((1,), (1,)))
        both = dot(p_both, p_both, ((1,), (1,)))
        g_full[:, :RANK] += both[:RANK, :RANK] + both[:RANK, RANK:] + both[RANK:, :RANK]

    t_full[...] = jnp.zeros_like(t_full)
    g_full[...] = jnp.zeros_like(g_full)
    for k, chunks in ((0, ()), (1, (0,)), (7, (7,)), (2, (1,)), (6, (6,)), (3, (2,)), (5, (5,)), (4, (3, 4))):
        t = (z + k) % NZ
        remote(x_recv.at[t], x_recv.at[t], ax_ssem, ax_rsem.at[t], (dp, mp)).wait_recv()
        for o in chunks:
            c = (z + o) % NZ
            pl.when(c < NCHUNK)(functools.partial(accumulate, c))

    for j in range(NMP):
        t_send[j, :, :256] = t_full[4 * j:4 * j + 4, :]
        t_send[j, :, 256:] = g_full[4 * j:4 * j + 4, :]

    for k in MP_FAR_FIRST:
        to = (mp + k) % NMP
        remote(t_send.at[to], t_recv.at[k - 1], ts_sem, tr_sem, (dp, to)).start()
    remote(x_recv, x_recv, ax_ssem, ax_rsem.at[0], (dp, mp)).wait_send()
    remote(z_recv, z_recv, az_ssem, az_rsem.at[1], (dp, mp)).wait_send()
    remote(t_recv, t_recv, ts_sem, tr_sem, (dp, mp)).wait_recv()
    slice_sum = t_send[mp]
    for k in range(NMP - 1):
        slice_sum = slice_sum + t_recv[k]
    t_all[dp] = slice_sum[:, :256]
    t_part[...] = slice_sum[:, :256]
    g_gather[mp] = slice_sum[:, 256:]

    for i, j in DP_FAR_FIRST:
        to = (z + i) % NZ * NX + (x + j) % NX
        remote(t_part, t_all.at[dp], ta_ssem, ta_rsem, (to, mp)).start()
    for k in MP_FAR_FIRST:
        remote(g_gather.at[mp], g_gather.at[mp], gg_ssem, gg_rsem, (dp, (mp + k) % NMP)).start()
    rest_g = g_gather.at[pl.ds(0, NMP - 1)]
    remote(rest_g, rest_g, gg_ssem, gg_rsem, (dp, mp)).wait_recv()
    for j in range(NMP):
        g_full[4 * j:4 * j + 4, :] = g_gather[j]
    remote(t_recv, t_recv, ts_sem, tr_sem, (dp, mp)).wait_send()
    remote(rest_g, rest_g, gg_ssem, gg_rsem, (dp, mp)).wait_send()

    rest_t = t_all.at[pl.ds(0, NDP - 1)]
    remote(rest_t, rest_t, ta_ssem, ta_rsem, (dp, mp)).wait_recv()
    total = t_all[0]
    for k in range(1, NDP):
        total = total + t_all[k]
    t_gather[mp] = total

    for k in MP_FAR_FIRST:
        remote(t_gather.at[mp], t_gather.at[mp], tg_ssem, tg_rsem, (dp, (mp + k) % NMP)).start()
    remote(rest_t, rest_t, ta_ssem, ta_rsem, (dp, mp)).wait_send()
    inverse = inverse_factor(g_full[...])
    rest_s = t_gather.at[pl.ds(0, NMP - 1)]
    remote(rest_s, rest_s, tg_ssem, tg_rsem, (dp, mp)).wait_recv()
    for j in range(NMP):
        t_full[4 * j:4 * j + 4, :] = t_gather[j]
    exact = lax.Precision.HIGHEST
    q_rows = lax.dot_general(
        inverse, t_full[...] * (1.0 / NDP), (((1,), (0,)), ((), ())),
        precision=exact, preferred_element_type=F32,
    )[:, :COLS]
    q_out[0] = q_rows
    v_out[...] = lax.dot_general(
        q_rows, inverse, (((0,), (0,)), ((), ())), precision=exact, preferred_element_type=F32
    )
    remote(rest_s, rest_s, tg_ssem, tg_rsem, (dp, mp)).wait_send()


def output_kernel(m_ref, p_ref, v_ref, q_ref, u_hbm, e_hbm, q_out, u_buf, e_buf, store_sem):
    v_high, v_low = split(v_ref[...])
    left = jnp.concatenate([v_high, v_low, v_high], axis=1)

    def store(c):
        cols = pl.ds(c * CHUNK, CHUNK)
        return (
            pltpu.make_async_copy(u_buf.at[:, cols], u_hbm.at[:, cols], store_sem.at[c, 0]),
            pltpu.make_async_copy(e_buf.at[:, cols], e_hbm.at[0, :, cols], store_sem.at[c, 1]),
        )

    for c in range(NCHUNK):
        cols = slice(c * CHUNK, (c + 1) * CHUNK)
        p_high = p_ref[:RANK, cols]
        right = jnp.concatenate([p_high, p_high, p_ref[RANK:, cols]], axis=0)
        update = dot(left, right, ((1,), (0,)))
        u_buf[:, cols] = update.astype(BF16)
        e_buf[:, cols] = m_ref[:, cols] - update
        for copy in store(c):
            copy.start()
    q_out[...] = q_ref[...]
    for c in range(NCHUNK):
        for copy in store(c):
            copy.wait()


def on_device(gradients, errors, q_start):
    vmem = pl.BlockSpec(memory_space=pltpu.VMEM)
    hbm = pl.BlockSpec(memory_space=pl.ANY)
    dma, reg = pltpu.SemaphoreType.DMA, pltpu.SemaphoreType.REGULAR
    merged, p_both, v, q_rows = pl.pallas_call(
        round_kernel,
        name="power_round",
        out_shape=(
            jax.ShapeDtypeStruct((COLS, FL), F32),
            jax.ShapeDtypeStruct((2 * RANK, FL), BF16),
            jax.ShapeDtypeStruct((COLS, RANK), F32),
            jax.ShapeDtypeStruct((1, RANK, COLS), F32),
        ),
        in_specs=[hbm, hbm, hbm],
        out_specs=(vmem, vmem, vmem, vmem),
        scratch_shapes=[
            pltpu.VMEM((NCHUNK, COLS, CHUNK), BF16),
            pltpu.VMEM((NCHUNK, COLS, CHUNK), F32),
            pltpu.VMEM((1, RANK, COLS), F32),
            pltpu.VMEM((256, FL), BF16),
            pltpu.VMEM((256, FL), BF16),
            pltpu.VMEM((UNITS, 4, 128), F32),
            pltpu.VMEM((NZ, NX - 1, PIECE, 4, 128), F32),
            pltpu.VMEM((NZ, PIECE, 4, 128), F32),
            pltpu.VMEM((NZ - 1, PIECE, 4, 128), F32),
            pltpu.VMEM((UNITS, 4, 128), F32),
            pltpu.VMEM((RANK, CHUNK), F32),
            pltpu.VMEM((NMP, 4, ROWS_T), F32),
            pltpu.VMEM((NMP - 1, 4, ROWS_T), F32),
            pltpu.VMEM((4, 256), F32),
            pltpu.VMEM((NDP, 4, 256), F32),
            pltpu.VMEM((NMP, 4, 256), F32),
            pltpu.VMEM((NMP, 4, 128), F32),
            pltpu.VMEM((RANK, 256), F32),
            pltpu.VMEM((RANK, 128), F32),
            dma((NCHUNK, 2)), dma,
            dma, dma((NZ,)), dma, dma, dma, dma((NZ,)), dma, dma((NZ,)),
            dma, dma, dma, dma, dma, dma, dma, dma,
        ],
        compiler_params=pltpu.CompilerParams(
            collective_id=0, has_side_effects=True, vmem_limit_bytes=LIMIT
        ),
    )(*(pltpu.with_memory_space_constraint(a, pltpu.HBM) for a in (gradients, errors, jnp.swapaxes(q_start, 1, 2))))

    update_grad, new_errors, q_rows = pl.pallas_call(
        output_kernel,
        name="outputs",
        out_shape=(
            jax.ShapeDtypeStruct((COLS, FL), BF16),
            jax.ShapeDtypeStruct((1, COLS, FL), F32),
            jax.ShapeDtypeStruct((1, RANK, COLS), F32),
        ),
        in_specs=[vmem, vmem, vmem, vmem],
        out_specs=(hbm, hbm, vmem),
        scratch_shapes=[
            pltpu.VMEM((COLS, FL), BF16),
            pltpu.VMEM((COLS, FL), F32),
            dma((NCHUNK, 2)),
        ],
        compiler_params=pltpu.CompilerParams(vmem_limit_bytes=LIMIT),
    )(merged, p_both, v, q_rows)
    return update_grad, new_errors, jnp.swapaxes(q_rows, 1, 2)


def solution(mesh):
    return jax.shard_map(
        on_device,
        mesh=mesh,
        in_specs=(P("dp", None, "mp"), P("dp", None, "mp"), P()),
        out_specs=(P(None, "mp"), P("dp", None, "mp"), P()),
        check_vma=False,
    )
```

```python
import functools

import jax
import jax.numpy as jnp
from jax import lax
from jax.experimental import pallas as pl
from jax.experimental.pallas import tpu as pltpu
from jax.sharding import PartitionSpec as P

MESH = pl.DeviceIdType.MESH
NX, NZ, NMP = 4, 8, 16
NDP = NX * NZ
COLS, RANK, FL = 240, 64, 1792
CHUNK = 256
NCHUNK = FL // CHUNK
LIMIT = 30 << 20
F32, BF16 = jnp.float32, jnp.bfloat16
UNITS = FL // 128 * 16
BLOCK = UNITS // NZ
PIECE = 6
REST = NX * PIECE
NEAR_FIRST = (1, 7, 2, 6, 3, 5, 4)
MP_FAR_FIRST = (9, 8, 7, 10, 11, 6, 5, 12, 13, 4, 3, 14, 15, 2, 1)


def ring(offset, size):
    return min(offset % size, -offset % size)


DP_FAR_FIRST = sorted(
    ((i, j) for i in range(NZ) for j in range(NX) if i or j),
    key=lambda o: (-ring(o[0], NZ) - ring(o[1], NX), -o[0], -o[1]),
)


def split(value):
    high = value.astype(BF16)
    return high, (value - high.astype(F32)).astype(BF16)


def dot(a, b, dims):
    return lax.dot_general(a, b, (dims, ((), ())), preferred_element_type=F32)


def remote(src, dst, send, recv, target):
    return pltpu.make_async_remote_copy(
        src_ref=src, dst_ref=dst, send_sem=send, recv_sem=recv,
        device_id=target, device_id_type=MESH,
    )


def inverse_factor(gram):
    row_at = lax.broadcasted_iota(jnp.int32, (RANK, 2 * RANK), 0)
    col_at = lax.broadcasted_iota(jnp.int32, (RANK, 2 * RANK), 1)
    work = jnp.where(col_at == row_at + RANK, 1.0, gram)
    done = []
    for j in range(RANK):
        base = 8 * (j // 8)
        local = j - base
        pivot = work[local:local + 1, j:j + 1]
        row = work[local:local + 1, :]
        below = lax.broadcasted_iota(jnp.int32, work.shape, 0) > local
        factor = work[:, j:j + 1] / pivot
        work = work - jnp.where(below, factor * row, 0.0)
        if local == 7:
            done.append(work[:8])
            work = work[8:]
    full = jnp.concatenate(done, axis=0)
    diagonal = jnp.sum(jnp.where(col_at == row_at, full, 0.0), axis=1, keepdims=True)
    return (full / jnp.sqrt(diagonal))[:, RANK:]


def round_kernel(g_hbm, e_hbm, q_hbm, m_out, p_out, v_out, q_out,
                 g_buf, e_buf, q_buf, mh, ml, local_p, x_recv, z_send, z_recv, zb_recv, b_send, xb_recv, gathered, p_full,
                 t_send, t_recv, g_send, g_recv, t_part, t_all, t_gather, g_gather, t_full, g_full,
                 load_sem, q_sem, x_ssem, x_rsem, z_ssem, z_rsem, az_ssem, az_rsem, ax_ssem, ax_rsem,
                 zb_ssem, zb_rsem, xb_ssem, xb_rsem, xg_ssem, xg_rsem, bz_ssem, bz_rsem,
                 ts_sem, tr_sem, gs_sem, gr_sem, ta_ssem, ta_rsem, tg_ssem, tg_rsem, gg_ssem, gg_rsem):
    dp = lax.axis_index("dp")
    mp = lax.axis_index("mp")
    z, x = dp // NX, dp % NX

    barrier = pltpu.get_barrier_semaphore()

    def greet(target):
        pl.semaphore_signal(barrier, inc=1, device_id=target, device_id_type=MESH)

    for k in reversed(NEAR_FIRST):
        greet(((z + k) % NZ * NX + x, mp))
    for k in MP_FAR_FIRST:
        greet((dp, (mp + k) % NMP))
    for i in (2, 1, 3):
        greet((z * NX + (x + i) % NX, mp))

    def place(i):
        c = (z + i) % NCHUNK
        return c, pl.ds(pl.multiple_of(c * CHUNK, CHUNK), CHUNK)

    def load(i):
        cols = place(i)[1]
        return (
            pltpu.make_async_copy(g_hbm.at[0, :, cols], g_buf.at[i], load_sem.at[i, 0]),
            pltpu.make_async_copy(e_hbm.at[0, :, cols], e_buf.at[i], load_sem.at[i, 1]),
        )

    q_copy = pltpu.make_async_copy(q_hbm, q_buf, q_sem)
    q_copy.start()
    for i in range(NCHUNK):
        for copy in load(i):
            copy.start()

    mh[COLS:256, :] = jnp.zeros((256 - COLS, FL), BF16)
    ml[COLS:256, :] = jnp.zeros((256 - COLS, FL), BF16)
    q_copy.wait()
    q_high, q_low = split(q_buf[0])
    q_both = jnp.concatenate([q_high, q_low], axis=0)

    def piece(t, to):
        return pl.ds(t * BLOCK + to * PIECE, PIECE)

    def rest(t):
        return pl.ds(t * BLOCK + REST, NX)

    def send_x(k):
        t = (z + 1 + k) % NZ
        for i in (2, 1, 3):
            to = (x + i) % NX
            remote(local_p.at[piece(t, to)], x_recv.at[t, i - 1], x_ssem, x_rsem.at[t], (z * NX + to, mp)).start()
        if k < NZ - 1:
            remote(local_p.at[rest(t)], zb_recv.at[k], zb_ssem, zb_rsem, (t * NX + x, mp)).start()

    for i in range(NCHUNK):
        c, cols = place(i)
        for copy in load(i):
            copy.wait()
        merged = g_buf[i].astype(F32) + e_buf[i]
        m_out[:, cols] = merged
        high, low = split(merged)
        mh[:COLS, cols] = high
        ml[:COLS, cols] = low
        both = dot(q_both, high, ((1,), (0,)))
        part = both[:RANK] + both[RANK:] + dot(q_high, low, ((1,), (0,)))
        for j in range(CHUNK // 128):
            for group in range(RANK // 4):
                unit = part[4 * group:4 * group + 4, 128 * j:128 * (j + 1)]
                local_p[c * 32 + (j * 16 + group)] = unit
        if i == 1:
            pl.semaphore_wait(barrier, NX - 1 + NZ - 1 + NMP - 1)
        if i:
            send_x(i - 1)
    send_x(NCHUNK - 1)
    send_x(NCHUNK)

    for k in range(NZ):
        t = (z + 1 + k) % NZ
        remote(x_recv.at[t], x_recv.at[t], x_ssem, x_rsem.at[t], (dp, mp)).wait_recv()
        z_send[k] = local_p[piece(t, x)] + x_recv[t, 0] + x_recv[t, 1] + x_recv[t, 2]
        if k < NZ - 1:
            remote(z_send.at[k], z_recv.at[k], z_ssem, z_rsem, (t * NX + x, mp)).start()
        if k == 4:
            remote(zb_recv, zb_recv, zb_ssem, zb_rsem, (dp, mp)).wait_recv()
            total = local_p[rest(z)]
            for j in range(NZ - 1):
                total = total + zb_recv[j]
            b_send[...] = total
            for i in (2, 1, 3):
                to = (x + i) % NX
                remote(b_send.at[to], xb_recv.at[i - 1], xb_ssem, xb_rsem, (z * NX + to, mp)).start()
    remote(z_recv, z_recv, z_ssem, z_rsem, (dp, mp)).wait_recv()
    mean = z_send[NZ - 1]
    for k in range(NZ - 1):
        mean = mean + z_recv[k]
    gathered[piece(z, x)] = mean * (1.0 / NDP)

    for k in NEAR_FIRST:
        remote(gathered.at[piece(z, x)], gathered.at[piece(z, x)], az_ssem, az_rsem.at[k], ((z + k) % NZ * NX + x, mp)).start()

    unit_own = z * BLOCK + REST + x
    remote(xb_recv, xb_recv, xb_ssem, xb_rsem, (dp, mp)).wait_recv()
    total = b_send[x] + xb_recv[0] + xb_recv[1] + xb_recv[2]
    gathered[unit_own] = total * (1.0 / NDP)
    for i in (2, 1, 3):
        to = (x + i) % NX
        remote(gathered.at[unit_own], gathered.at[unit_own], xg_ssem, xg_rsem, (z * NX + to, mp)).start()

    def on_to_x(t):
        for i in range(1, NX):
            remote(gathered.at[piece(t, x)], gathered.at[piece(t, x)], ax_ssem, ax_rsem.at[t], (z * NX + (x + i) % NX, mp)).start()

    on_to_x(z)
    remote(x_recv, x_recv, x_ssem, x_rsem.at[0], (dp, mp)).wait_send()
    remote(z_recv, z_recv, z_ssem, z_rsem, (dp, mp)).wait_send()
    remote(zb_recv, zb_recv, zb_ssem, zb_rsem, (dp, mp)).wait_send()
    remote(xb_recv, xb_recv, xb_ssem, xb_rsem, (dp, mp)).wait_send()
    for k in NEAR_FIRST:
        t = (z + NZ - k) % NZ
        remote(gathered.at[piece(t, x)], gathered.at[piece(t, x)], az_ssem, az_rsem.at[k], (dp, mp)).wait_recv()
        on_to_x(t)
        if k == 7:
            remote(xb_recv, xb_recv, xg_ssem, xg_rsem, (dp, mp)).wait_recv()
            for j in reversed(NEAR_FIRST):
                remote(gathered.at[rest(z)], gathered.at[rest(z)], bz_ssem, bz_rsem.at[j],
                       ((z + j) % NZ * NX + x, mp)).start()

    def accumulate(c):
        cols = pl.ds(pl.multiple_of(c * CHUNK, CHUNK), CHUNK)
        for j in range(CHUNK // 128):
            for group in range(RANK // 4):
                p_full[4 * group:4 * group + 4, 128 * j:128 * (j + 1)] = gathered[c * 32 + (j * 16 + group)]
        p_high, p_low = split(p_full[...])
        p_out[:RANK, cols] = p_high
        p_out[RANK:, cols] = p_low
        p_both = jnp.concatenate([p_high, p_low], axis=0)
        both = dot(p_both, mh[:, cols], ((1,), (1,)))
        t_full[...] += both[:RANK] + both[RANK:] + dot(p_high, ml[:, cols], ((1,), (1,)))
        both = dot(p_both, p_both, ((1,), (1,)))
        g_full[:, :RANK] += both[:RANK, :RANK] + both[:RANK, RANK:] + both[RANK:, :RANK]

    t_full[...] = jnp.zeros_like(t_full)
    g_full[...] = jnp.zeros_like(g_full)
    for k, chunks in ((0, ()), (1, (0,)), (7, (7,)), (2, (1,)), (6, (6,)), (3, (2,)), (5, (5,)), (4, (3, 4))):
        t = (z + k) % NZ
        remote(x_recv.at[t], x_recv.at[t], ax_ssem, ax_rsem.at[t], (dp, mp)).wait_recv()
        if k:
            remote(gathered.at[rest(t)], gathered.at[rest(t)], bz_ssem, bz_rsem.at[NZ - k], (dp, mp)).wait_recv()
        for o in chunks:
            c = (z + o) % NZ
            pl.when(c < NCHUNK)(functools.partial(accumulate, c))

    for j in range(NMP):
        t_send[j] = t_full[4 * j:4 * j + 4, :]
        g_send[j] = g_full[4 * j:4 * j + 4, :]

    for k in MP_FAR_FIRST:
        to = (mp + k) % NMP
        remote(t_send.at[to], t_recv.at[k - 1], ts_sem, tr_sem, (dp, to)).start()
    for k in MP_FAR_FIRST:
        to = (mp + k) % NMP
        remote(g_send.at[to], g_recv.at[k - 1], gs_sem, gr_sem, (dp, to)).start()
    remote(xb_recv, xb_recv, xg_ssem, xg_rsem, (dp, mp)).wait_send()
    remote(zb_recv, zb_recv, bz_ssem, bz_rsem.at[1], (dp, mp)).wait_send()
    remote(x_recv, x_recv, ax_ssem, ax_rsem.at[0], (dp, mp)).wait_send()
    remote(z_recv, z_recv, az_ssem, az_rsem.at[1], (dp, mp)).wait_send()
    remote(t_recv, t_recv, ts_sem, tr_sem, (dp, mp)).wait_recv()
    slice_sum = t_send[mp]
    for k in range(NMP - 1):
        slice_sum = slice_sum + t_recv[k]
    t_all[dp] = slice_sum
    t_part[...] = slice_sum

    for i, j in DP_FAR_FIRST:
        to = (z + i) % NZ * NX + (x + j) % NX
        remote(t_part, t_all.at[dp], ta_ssem, ta_rsem, (to, mp)).start()
    remote(g_recv, g_recv, gs_sem, gr_sem, (dp, mp)).wait_recv()
    slice_sum = g_send[mp]
    for k in range(NMP - 1):
        slice_sum = slice_sum + g_recv[k]
    g_gather[mp] = slice_sum
    for k in MP_FAR_FIRST:
        remote(g_gather.at[mp], g_gather.at[mp], gg_ssem, gg_rsem, (dp, (mp + k) % NMP)).start()
    rest_g = g_gather.at[pl.ds(0, NMP - 1)]
    remote(rest_g, rest_g, gg_ssem, gg_rsem, (dp, mp)).wait_recv()
    for j in range(NMP):
        g_full[4 * j:4 * j + 4, :] = g_gather[j]
    remote(t_recv, t_recv, ts_sem, tr_sem, (dp, mp)).wait_send()
    remote(g_recv, g_recv, gs_sem, gr_sem, (dp, mp)).wait_send()
    remote(rest_g, rest_g, gg_ssem, gg_rsem, (dp, mp)).wait_send()

    rest_t = t_all.at[pl.ds(0, NDP - 1)]
    remote(rest_t, rest_t, ta_ssem, ta_rsem, (dp, mp)).wait_recv()
    total = t_all[0]
    for k in range(1, NDP):
        total = total + t_all[k]
    t_gather[mp] = total

    for k in MP_FAR_FIRST:
        remote(t_gather.at[mp], t_gather.at[mp], tg_ssem, tg_rsem, (dp, (mp + k) % NMP)).start()
    remote(rest_t, rest_t, ta_ssem, ta_rsem, (dp, mp)).wait_send()
    inverse = inverse_factor(g_full[...])
    rest_s = t_gather.at[pl.ds(0, NMP - 1)]
    remote(rest_s, rest_s, tg_ssem, tg_rsem, (dp, mp)).wait_recv()
    for j in range(NMP):
        t_full[4 * j:4 * j + 4, :] = t_gather[j]
    exact = lax.Precision.HIGHEST
    q_rows = lax.dot_general(
        inverse, t_full[...] * (1.0 / NDP), (((1,), (0,)), ((), ())),
        precision=exact, preferred_element_type=F32,
    )[:, :COLS]
    q_out[0] = q_rows
    v_out[...] = lax.dot_general(
        q_rows, inverse, (((0,), (0,)), ((), ())), precision=exact, preferred_element_type=F32
    )
    remote(rest_s, rest_s, tg_ssem, tg_rsem, (dp, mp)).wait_send()


def output_kernel(m_ref, p_ref, v_ref, q_ref, u_hbm, e_hbm, q_out, u_buf, e_buf, store_sem):
    v_high, v_low = split(v_ref[...])
    left = jnp.concatenate([v_high, v_low, v_high], axis=1)

    def store(c):
        cols = pl.ds(c * CHUNK, CHUNK)
        return (
            pltpu.make_async_copy(u_buf.at[:, cols], u_hbm.at[:, cols], store_sem.at[c, 0]),
            pltpu.make_async_copy(e_buf.at[:, cols], e_hbm.at[0, :, cols], store_sem.at[c, 1]),
        )

    for c in range(NCHUNK):
        cols = slice(c * CHUNK, (c + 1) * CHUNK)
        p_high = p_ref[:RANK, cols]
        right = jnp.concatenate([p_high, p_high, p_ref[RANK:, cols]], axis=0)
        update = dot(left, right, ((1,), (0,)))
        u_buf[:, cols] = update.astype(BF16)
        e_buf[:, cols] = m_ref[:, cols] - update
        for copy in store(c):
            copy.start()
    q_out[...] = q_ref[...]
    for c in range(NCHUNK):
        for copy in store(c):
            copy.wait()


def on_device(gradients, errors, q_start):
    vmem = pl.BlockSpec(memory_space=pltpu.VMEM)
    hbm = pl.BlockSpec(memory_space=pl.ANY)
    dma, reg = pltpu.SemaphoreType.DMA, pltpu.SemaphoreType.REGULAR
    merged, p_both, v, q_rows = pl.pallas_call(
        round_kernel,
        name="power_round",
        out_shape=(
            jax.ShapeDtypeStruct((COLS, FL), F32),
            jax.ShapeDtypeStruct((2 * RANK, FL), BF16),
            jax.ShapeDtypeStruct((COLS, RANK), F32),
            jax.ShapeDtypeStruct((1, RANK, COLS), F32),
        ),
        in_specs=[hbm, hbm, hbm],
        out_specs=(vmem, vmem, vmem, vmem),
        scratch_shapes=[
            pltpu.VMEM((NCHUNK, COLS, CHUNK), BF16),
            pltpu.VMEM((NCHUNK, COLS, CHUNK), F32),
            pltpu.VMEM((1, RANK, COLS), F32),
            pltpu.VMEM((256, FL), BF16),
            pltpu.VMEM((256, FL), BF16),
            pltpu.VMEM((UNITS, 4, 128), F32),
            pltpu.VMEM((NZ, NX - 1, PIECE, 4, 128), F32),
            pltpu.VMEM((NZ, PIECE, 4, 128), F32),
            pltpu.VMEM((NZ - 1, PIECE, 4, 128), F32),
            pltpu.VMEM((NZ - 1, NX, 4, 128), F32),
            pltpu.VMEM((NX, 4, 128), F32),
            pltpu.VMEM((NX - 1, 4, 128), F32),
            pltpu.VMEM((UNITS, 4, 128), F32),
            pltpu.VMEM((RANK, CHUNK), F32),
            pltpu.VMEM((NMP, 4, 256), F32),
            pltpu.VMEM((NMP - 1, 4, 256), F32),
            pltpu.VMEM((NMP, 4, 128), F32),
            pltpu.VMEM((NMP - 1, 4, 128), F32),
            pltpu.VMEM((4, 256), F32),
            pltpu.VMEM((NDP, 4, 256), F32),
            pltpu.VMEM((NMP, 4, 256), F32),
            pltpu.VMEM((NMP, 4, 128), F32),
            pltpu.VMEM((RANK, 256), F32),
            pltpu.VMEM((RANK, 128), F32),
            dma((NCHUNK, 2)), dma,
            dma, dma((NZ,)), dma, dma, dma, dma((NZ,)), dma, dma((NZ,)),
            dma, dma, dma, dma, dma, dma, dma, dma((NZ,)), dma, dma,
            dma, dma, dma, dma, dma, dma, dma, dma,
        ],
        compiler_params=pltpu.CompilerParams(
            collective_id=0, has_side_effects=True, vmem_limit_bytes=LIMIT
        ),
    )(*(pltpu.with_memory_space_constraint(a, pltpu.HBM) for a in (gradients, errors, jnp.swapaxes(q_start, 1, 2))))

    update_grad, new_errors, q_rows = pl.pallas_call(
        output_kernel,
        name="outputs",
        out_shape=(
            jax.ShapeDtypeStruct((COLS, FL), BF16),
            jax.ShapeDtypeStruct((1, COLS, FL), F32),
            jax.ShapeDtypeStruct((1, RANK, COLS), F32),
        ),
        in_specs=[vmem, vmem, vmem, vmem],
        out_specs=(hbm, hbm, vmem),
        scratch_shapes=[
            pltpu.VMEM((COLS, FL), BF16),
            pltpu.VMEM((COLS, FL), F32),
            dma((NCHUNK, 2)),
        ],
        compiler_params=pltpu.CompilerParams(vmem_limit_bytes=LIMIT),
    )(merged, p_both, v, q_rows)
    return update_grad, new_errors, jnp.swapaxes(q_rows, 1, 2)


def solution(mesh):
    return jax.shard_map(
        on_device,
        mesh=mesh,
        in_specs=(P("dp", None, "mp"), P("dp", None, "mp"), P()),
        out_specs=(P(None, "mp"), P("dp", None, "mp"), P()),
        check_vma=False,
    )
```

```python
import functools

import jax
import jax.numpy as jnp
from jax import lax
from jax.experimental import pallas as pl
from jax.experimental.pallas import tpu as pltpu
from jax.sharding import PartitionSpec as P

MESH = pl.DeviceIdType.MESH
NX, NY, NZ, NMP = 4, 8, 8, 16
NDP = NX * NZ
COLS, RANK, FL = 240, 64, 1792
CHUNK = 256
NCHUNK = FL // CHUNK
LIMIT = 30 << 20
F32, BF16 = jnp.float32, jnp.bfloat16
UNITS = FL // 128 * 16
BLOCK = UNITS // NZ
PIECE = 6
REST = NX * PIECE
NEAR_FIRST = (1, 7, 2, 6, 3, 5, 4)
MP_FAR_FIRST = (9, 8, 7, 10, 11, 6, 5, 12, 13, 4, 3, 14, 15, 2, 1)


def ring(offset, size):
    return min(offset % size, -offset % size)


DP_FAR_FIRST = sorted(
    ((i, j) for i in range(NZ) for j in range(NX) if i or j),
    key=lambda o: (-ring(o[0], NZ) - ring(o[1], NX), -o[0], -o[1]),
)


def split(value):
    high = value.astype(BF16)
    return high, (value - high.astype(F32)).astype(BF16)


def dot(a, b, dims):
    return lax.dot_general(a, b, (dims, ((), ())), preferred_element_type=F32)


def remote(src, dst, send, recv, target):
    return pltpu.make_async_remote_copy(
        src_ref=src, dst_ref=dst, send_sem=send, recv_sem=recv,
        device_id=target, device_id_type=MESH,
    )


def inverse_factor(gram):
    row_at = lax.broadcasted_iota(jnp.int32, (RANK, 2 * RANK), 0)
    col_at = lax.broadcasted_iota(jnp.int32, (RANK, 2 * RANK), 1)
    work = jnp.where(col_at == row_at + RANK, 1.0, gram)
    done = []
    for j in range(RANK):
        base = 8 * (j // 8)
        local = j - base
        pivot = work[local:local + 1, j:j + 1]
        row = work[local:local + 1, :]
        below = lax.broadcasted_iota(jnp.int32, work.shape, 0) > local
        factor = work[:, j:j + 1] / pivot
        work = work - jnp.where(below, factor * row, 0.0)
        if local == 7:
            done.append(work[:8])
            work = work[8:]
    full = jnp.concatenate(done, axis=0)
    diagonal = jnp.sum(jnp.where(col_at == row_at, full, 0.0), axis=1, keepdims=True)
    return (full / jnp.sqrt(diagonal))[:, RANK:]


def round_kernel(g_hbm, e_hbm, q_hbm, m_out, p_out, v_out, q_out,
                 g_buf, e_buf, q_buf, mh, ml, local_p, x_recv, z_send, z_recv, zb_recv, b_send, xb_recv, gathered, p_full,
                 t_recv, g_recv, t_part, t_all, t_full, g_full, t_total, g_total,
                 load_sem, q_sem, x_ssem, x_rsem, z_ssem, z_rsem, az_ssem, az_rsem, ax_ssem, ax_rsem,
                 zb_ssem, zb_rsem, xb_ssem, xb_rsem, xg_ssem, xg_rsem, bz_ssem, bz_rsem,
                 ts_sem, tr_sem, gs_sem, gr_sem, ta_ssem, ta_rsem, tg_ssem, tg_rsem, gg_ssem, gg_rsem):
    dp = lax.axis_index("dp")
    mp = lax.axis_index("mp")
    z, x = dp // NX, dp % NX
    y, core = mp // 2, mp % 2

    barrier = pltpu.get_barrier_semaphore()

    def greet(target):
        pl.semaphore_signal(barrier, inc=1, device_id=target, device_id_type=MESH)

    for k in reversed(NEAR_FIRST):
        greet(((z + k) % NZ * NX + x, mp))
    for k in MP_FAR_FIRST:
        greet((dp, (mp + k) % NMP))
    for i in (2, 1, 3):
        greet((z * NX + (x + i) % NX, mp))

    def place(i):
        c = (z + i) % NCHUNK
        return c, pl.ds(pl.multiple_of(c * CHUNK, CHUNK), CHUNK)

    def load(i):
        cols = place(i)[1]
        return (
            pltpu.make_async_copy(g_hbm.at[0, :, cols], g_buf.at[i], load_sem.at[i, 0]),
            pltpu.make_async_copy(e_hbm.at[0, :, cols], e_buf.at[i], load_sem.at[i, 1]),
        )

    q_copy = pltpu.make_async_copy(q_hbm, q_buf, q_sem)
    q_copy.start()
    for i in range(NCHUNK):
        for copy in load(i):
            copy.start()

    mh[COLS:256, :] = jnp.zeros((256 - COLS, FL), BF16)
    ml[COLS:256, :] = jnp.zeros((256 - COLS, FL), BF16)
    q_copy.wait()
    q_high, q_low = split(q_buf[0])
    q_both = jnp.concatenate([q_high, q_low], axis=0)

    def piece(t, to):
        return pl.ds(t * BLOCK + to * PIECE, PIECE)

    def rest(t):
        return pl.ds(t * BLOCK + REST, NX)

    def send_x(k):
        t = (z + 1 + k) % NZ
        for i in (2, 1, 3):
            to = (x + i) % NX
            remote(local_p.at[piece(t, to)], x_recv.at[t, i - 1], x_ssem, x_rsem.at[t], (z * NX + to, mp)).start()
        if k < NZ - 1:
            remote(local_p.at[rest(t)], zb_recv.at[k], zb_ssem, zb_rsem, (t * NX + x, mp)).start()

    for i in range(NCHUNK):
        c, cols = place(i)
        for copy in load(i):
            copy.wait()
        merged = g_buf[i].astype(F32) + e_buf[i]
        m_out[:, cols] = merged
        high, low = split(merged)
        mh[:COLS, cols] = high
        ml[:COLS, cols] = low
        both = dot(q_both, high, ((1,), (0,)))
        part = both[:RANK] + both[RANK:] + dot(q_high, low, ((1,), (0,)))
        for j in range(CHUNK // 128):
            for group in range(RANK // 4):
                unit = part[4 * group:4 * group + 4, 128 * j:128 * (j + 1)]
                local_p[c * 32 + (j * 16 + group)] = unit
        if i == 1:
            pl.semaphore_wait(barrier, NX - 1 + NZ - 1 + NMP - 1)
        if i:
            send_x(i - 1)
    send_x(NCHUNK - 1)
    send_x(NCHUNK)

    for k in range(NZ):
        t = (z + 1 + k) % NZ
        remote(x_recv.at[t], x_recv.at[t], x_ssem, x_rsem.at[t], (dp, mp)).wait_recv()
        z_send[k] = local_p[piece(t, x)] + x_recv[t, 0] + x_recv[t, 1] + x_recv[t, 2]
        if k < NZ - 1:
            remote(z_send.at[k], z_recv.at[k], z_ssem, z_rsem, (t * NX + x, mp)).start()
        if k == 4:
            remote(zb_recv, zb_recv, zb_ssem, zb_rsem, (dp, mp)).wait_recv()
            total = local_p[rest(z)]
            for j in range(NZ - 1):
                total = total + zb_recv[j]
            b_send[...] = total
            for i in (2, 1, 3):
                to = (x + i) % NX
                remote(b_send.at[to], xb_recv.at[i - 1], xb_ssem, xb_rsem, (z * NX + to, mp)).start()
    remote(z_recv, z_recv, z_ssem, z_rsem, (dp, mp)).wait_recv()
    mean = z_send[NZ - 1]
    for k in range(NZ - 1):
        mean = mean + z_recv[k]
    gathered[piece(z, x)] = mean * (1.0 / NDP)

    for k in NEAR_FIRST:
        remote(gathered.at[piece(z, x)], gathered.at[piece(z, x)], az_ssem, az_rsem.at[k], ((z + k) % NZ * NX + x, mp)).start()

    unit_own = z * BLOCK + REST + x
    remote(xb_recv, xb_recv, xb_ssem, xb_rsem, (dp, mp)).wait_recv()
    total = b_send[x] + xb_recv[0] + xb_recv[1] + xb_recv[2]
    gathered[unit_own] = total * (1.0 / NDP)
    for i in (2, 1, 3):
        to = (x + i) % NX
        remote(gathered.at[unit_own], gathered.at[unit_own], xg_ssem, xg_rsem, (z * NX + to, mp)).start()

    def on_to_x(t):
        for i in range(1, NX):
            remote(gathered.at[piece(t, x)], gathered.at[piece(t, x)], ax_ssem, ax_rsem.at[t], (z * NX + (x + i) % NX, mp)).start()

    on_to_x(z)
    remote(x_recv, x_recv, x_ssem, x_rsem.at[0], (dp, mp)).wait_send()
    remote(z_recv, z_recv, z_ssem, z_rsem, (dp, mp)).wait_send()
    remote(zb_recv, zb_recv, zb_ssem, zb_rsem, (dp, mp)).wait_send()
    remote(xb_recv, xb_recv, xb_ssem, xb_rsem, (dp, mp)).wait_send()
    for k in NEAR_FIRST:
        t = (z + NZ - k) % NZ
        remote(gathered.at[piece(t, x)], gathered.at[piece(t, x)], az_ssem, az_rsem.at[k], (dp, mp)).wait_recv()
        on_to_x(t)
        if k == 7:
            remote(xb_recv, xb_recv, xg_ssem, xg_rsem, (dp, mp)).wait_recv()
            for j in reversed(NEAR_FIRST):
                remote(gathered.at[rest(z)], gathered.at[rest(z)], bz_ssem, bz_rsem.at[j],
                       ((z + j) % NZ * NX + x, mp)).start()

    def accumulate(c):
        cols = pl.ds(pl.multiple_of(c * CHUNK, CHUNK), CHUNK)
        for j in range(CHUNK // 128):
            for group in range(RANK // 4):
                p_full[4 * group:4 * group + 4, 128 * j:128 * (j + 1)] = gathered[c * 32 + (j * 16 + group)]
        p_high, p_low = split(p_full[...])
        p_out[:RANK, cols] = p_high
        p_out[RANK:, cols] = p_low
        p_both = jnp.concatenate([p_high, p_low], axis=0)
        both = dot(p_both, mh[:, cols], ((1,), (1,)))
        t_full[...] += both[:RANK] + both[RANK:] + dot(p_high, ml[:, cols], ((1,), (1,)))
        both = dot(p_both, p_both, ((1,), (1,)))
        g_full[:, :RANK] += both[:RANK, :RANK] + both[:RANK, RANK:] + both[RANK:, :RANK]

    t_full[...] = jnp.zeros_like(t_full)
    g_full[...] = jnp.zeros_like(g_full)
    for k, chunks in ((0, ()), (1, (0,)), (7, (7,)), (2, (1,)), (6, (6,)), (3, (2,)), (5, (5,)), (4, (3, 4))):
        t = (z + k) % NZ
        remote(x_recv.at[t], x_recv.at[t], ax_ssem, ax_rsem.at[t], (dp, mp)).wait_recv()
        if k:
            remote(gathered.at[rest(t)], gathered.at[rest(t)], bz_ssem, bz_rsem.at[NZ - k], (dp, mp)).wait_recv()
        for o in chunks:
            c = (z + o) % NZ
            pl.when(c < NCHUNK)(functools.partial(accumulate, c))

    def rows(at):
        return pl.ds(pl.multiple_of(at * 8, 8), 8)

    def to_owner(ref, recv, ssem, rsem, k):
        owner = (y + k) % NY
        remote(ref.at[rows(owner)], recv.at[2 * k + core], ssem, rsem, (dp, 2 * owner)).start()

    for ref, recv, ssem, rsem in ((t_full, t_recv, ts_sem, tr_sem), (g_full, g_recv, gs_sem, gr_sem)):
        for k in reversed(NEAR_FIRST):
            to_owner(ref, recv, ssem, rsem, k)
        pl.when(core == 1)(functools.partial(to_owner, ref, recv, ssem, rsem, 0))
    remote(xb_recv, xb_recv, xg_ssem, xg_rsem, (dp, mp)).wait_send()
    remote(zb_recv, zb_recv, bz_ssem, bz_rsem.at[1], (dp, mp)).wait_send()
    remote(x_recv, x_recv, ax_ssem, ax_rsem.at[0], (dp, mp)).wait_send()
    remote(z_recv, z_recv, az_ssem, az_rsem.at[1], (dp, mp)).wait_send()

    def own_sum(ref, recv, ssem, rsem):
        arrived = recv.at[pl.ds(1, NMP - 1)]
        remote(arrived, arrived, ssem, rsem, (dp, mp)).wait_recv()
        total = ref[rows(y), :]
        for k in range(1, NMP):
            total = total + recv[k]
        return total

    def to_all(ref, ssem, rsem):
        for k in MP_FAR_FIRST:
            remote(ref.at[rows(y)], ref.at[rows(y)], ssem, rsem, (dp, (mp + k) % NMP)).start()

    @pl.when(core == 0)
    def _():
        total = own_sum(t_full, t_recv, ts_sem, tr_sem)
        t_all[dp] = total
        t_part[...] = total
        for i, j in DP_FAR_FIRST:
            to = (z + i) % NZ * NX + (x + j) % NX
            remote(t_part, t_all.at[dp], ta_ssem, ta_rsem, (to, mp)).start()
        g_total[rows(y), :] = own_sum(g_full, g_recv, gs_sem, gr_sem)
        to_all(g_total, gg_ssem, gg_rsem)
        for sent, ssem, rsem in (
            (t_full.at[pl.ds(0, 8 * (NY - 1))], ts_sem, tr_sem),
            (g_full.at[pl.ds(0, 8 * (NY - 1))], gs_sem, gr_sem),
        ):
            remote(sent, sent, ssem, rsem, (dp, mp)).wait_send()
        arrived = t_all.at[pl.ds(0, NDP - 1)]
        remote(arrived, arrived, ta_ssem, ta_rsem, (dp, mp)).wait_recv()
        total = t_all[0]
        for k in range(1, NDP):
            total = total + t_all[k]
        t_total[rows(y), :] = total
        to_all(t_total, tg_ssem, tg_rsem)
        remote(arrived, arrived, ta_ssem, ta_rsem, (dp, mp)).wait_send()

    @pl.when(core == 1)
    def _():
        remote(t_full, t_full, ts_sem, tr_sem, (dp, mp)).wait_send()
        remote(g_full, g_full, gs_sem, gr_sem, (dp, mp)).wait_send()

    def wait_rows(ref, ssem, rsem):
        @pl.when(core == 0)
        def _():
            others = ref.at[pl.ds(0, 8 * (NY - 1))]
            remote(others, others, ssem, rsem, (dp, mp)).wait_recv()

        @pl.when(core == 1)
        def _():
            remote(ref, ref, ssem, rsem, (dp, mp)).wait_recv()

    wait_rows(g_total, gg_ssem, gg_rsem)
    inverse = inverse_factor(g_total[...])
    wait_rows(t_total, tg_ssem, tg_rsem)
    exact = lax.Precision.HIGHEST
    q_rows = lax.dot_general(
        inverse, t_total[...] * (1.0 / NDP), (((1,), (0,)), ((), ())),
        precision=exact, preferred_element_type=F32,
    )[:, :COLS]
    q_out[0] = q_rows
    v_out[...] = lax.dot_general(
        q_rows, inverse, (((0,), (0,)), ((), ())), precision=exact, preferred_element_type=F32
    )

    @pl.when(core == 0)
    def _():
        for recv, ssem, rsem in ((g_recv, gg_ssem, gg_rsem), (t_recv, tg_ssem, tg_rsem)):
            sent = recv.at[pl.ds(1, NMP - 1)]
            remote(sent, sent, ssem, rsem, (dp, mp)).wait_send()


def output_kernel(m_ref, p_ref, v_ref, q_ref, u_hbm, e_hbm, q_out, u_buf, e_buf, store_sem):
    v_high, v_low = split(v_ref[...])
    left = jnp.concatenate([v_high, v_low, v_high], axis=1)

    def store(c):
        cols = pl.ds(c * CHUNK, CHUNK)
        return (
            pltpu.make_async_copy(u_buf.at[:, cols], u_hbm.at[:, cols], store_sem.at[c, 0]),
            pltpu.make_async_copy(e_buf.at[:, cols], e_hbm.at[0, :, cols], store_sem.at[c, 1]),
        )

    for c in range(NCHUNK):
        cols = slice(c * CHUNK, (c + 1) * CHUNK)
        p_high = p_ref[:RANK, cols]
        right = jnp.concatenate([p_high, p_high, p_ref[RANK:, cols]], axis=0)
        update = dot(left, right, ((1,), (0,)))
        u_buf[:, cols] = update.astype(BF16)
        e_buf[:, cols] = m_ref[:, cols] - update
        for copy in store(c):
            copy.start()
    q_out[...] = q_ref[...]
    for c in range(NCHUNK):
        for copy in store(c):
            copy.wait()


def on_device(gradients, errors, q_start):
    vmem = pl.BlockSpec(memory_space=pltpu.VMEM)
    hbm = pl.BlockSpec(memory_space=pl.ANY)
    dma, reg = pltpu.SemaphoreType.DMA, pltpu.SemaphoreType.REGULAR
    merged, p_both, v, q_rows = pl.pallas_call(
        round_kernel,
        name="power_round",
        out_shape=(
            jax.ShapeDtypeStruct((COLS, FL), F32),
            jax.ShapeDtypeStruct((2 * RANK, FL), BF16),
            jax.ShapeDtypeStruct((COLS, RANK), F32),
            jax.ShapeDtypeStruct((1, RANK, COLS), F32),
        ),
        in_specs=[hbm, hbm, hbm],
        out_specs=(vmem, vmem, vmem, vmem),
        scratch_shapes=[
            pltpu.VMEM((NCHUNK, COLS, CHUNK), BF16),
            pltpu.VMEM((NCHUNK, COLS, CHUNK), F32),
            pltpu.VMEM((1, RANK, COLS), F32),
            pltpu.VMEM((256, FL), BF16),
            pltpu.VMEM((256, FL), BF16),
            pltpu.VMEM((UNITS, 4, 128), F32),
            pltpu.VMEM((NZ, NX - 1, PIECE, 4, 128), F32),
            pltpu.VMEM((NZ, PIECE, 4, 128), F32),
            pltpu.VMEM((NZ - 1, PIECE, 4, 128), F32),
            pltpu.VMEM((NZ - 1, NX, 4, 128), F32),
            pltpu.VMEM((NX, 4, 128), F32),
            pltpu.VMEM((NX - 1, 4, 128), F32),
            pltpu.VMEM((UNITS, 4, 128), F32),
            pltpu.VMEM((RANK, CHUNK), F32),
            pltpu.VMEM((NMP, 8, 256), F32),
            pltpu.VMEM((NMP, 8, 128), F32),
            pltpu.VMEM((8, 256), F32),
            pltpu.VMEM((NDP, 8, 256), F32),
            pltpu.VMEM((RANK, 256), F32),
            pltpu.VMEM((RANK, 128), F32),
            pltpu.VMEM((RANK, 256), F32),
            pltpu.VMEM((RANK, 128), F32),
            dma((NCHUNK, 2)), dma,
            dma, dma((NZ,)), dma, dma, dma, dma((NZ,)), dma, dma((NZ,)),
            dma, dma, dma, dma, dma, dma, dma, dma((NZ,)), dma, dma,
            dma, dma, dma, dma, dma, dma, dma, dma,
        ],
        compiler_params=pltpu.CompilerParams(
            collective_id=0, has_side_effects=True, vmem_limit_bytes=LIMIT
        ),
    )(*(pltpu.with_memory_space_constraint(a, pltpu.HBM) for a in (gradients, errors, jnp.swapaxes(q_start, 1, 2))))

    update_grad, new_errors, q_rows = pl.pallas_call(
        output_kernel,
        name="outputs",
        out_shape=(
            jax.ShapeDtypeStruct((COLS, FL), BF16),
            jax.ShapeDtypeStruct((1, COLS, FL), F32),
            jax.ShapeDtypeStruct((1, RANK, COLS), F32),
        ),
        in_specs=[vmem, vmem, vmem, vmem],
        out_specs=(hbm, hbm, vmem),
        scratch_shapes=[
            pltpu.VMEM((COLS, FL), BF16),
            pltpu.VMEM((COLS, FL), F32),
            dma((NCHUNK, 2)),
        ],
        compiler_params=pltpu.CompilerParams(vmem_limit_bytes=LIMIT),
    )(merged, p_both, v, q_rows)
    return update_grad, new_errors, jnp.swapaxes(q_rows, 1, 2)


def solution(mesh):
    return jax.shard_map(
        on_device,
        mesh=mesh,
        in_specs=(P("dp", None, "mp"), P("dp", None, "mp"), P()),
        out_specs=(P(None, "mp"), P("dp", None, "mp"), P()),
        check_vma=False,
    )
```

```python
import functools

import jax
import jax.numpy as jnp
from jax import lax
from jax.experimental import pallas as pl
from jax.experimental.pallas import tpu as pltpu
from jax.sharding import PartitionSpec as P

MESH = pl.DeviceIdType.MESH
NX, NY, NZ, NMP = 4, 8, 8, 16
NDP = NX * NZ
COLS, RANK, FL = 240, 64, 1792
CHUNK = 256
NCHUNK = FL // CHUNK
LIMIT = 30 << 20
F32, BF16 = jnp.float32, jnp.bfloat16
UNITS = FL // 128 * 16
BLOCK = UNITS // NZ
PIECE = 6
REST = NX * PIECE
NEAR_FIRST = (1, 7, 2, 6, 3, 5, 4)
MP_FAR_FIRST = (9, 8, 7, 10, 11, 6, 5, 12, 13, 4, 3, 14, 15, 2, 1)


def ring(offset, size):
    return min(offset % size, -offset % size)


DP_FAR_FIRST = sorted(
    ((i, j) for i in range(NZ) for j in range(NX) if i or j),
    key=lambda o: (-ring(o[0], NZ) - ring(o[1], NX), -o[0], -o[1]),
)


def split(value):
    high = value.astype(BF16)
    return high, (value - high.astype(F32)).astype(BF16)


def dot(a, b, dims):
    return lax.dot_general(a, b, (dims, ((), ())), preferred_element_type=F32)


def remote(src, dst, send, recv, target):
    return pltpu.make_async_remote_copy(
        src_ref=src, dst_ref=dst, send_sem=send, recv_sem=recv,
        device_id=target, device_id_type=MESH,
    )


def inverse_factor(gram):
    row_at = lax.broadcasted_iota(jnp.int32, (RANK, 2 * RANK), 0)
    col_at = lax.broadcasted_iota(jnp.int32, (RANK, 2 * RANK), 1)
    work = jnp.where(col_at == row_at + RANK, 1.0, gram)
    done = []
    for first in range(0, RANK, 8):
        at = lax.broadcasted_iota(jnp.int32, work.shape, 0)
        columns = [jnp.broadcast_to(work[:, first + k:first + k + 1], work.shape) for k in range(8)]
        for k in range(8):
            factor = jnp.where(at > k, columns[k] * (1.0 / columns[k][k:k + 1, :]), 0.0)
            for m in range(k + 1, 8):
                columns[m] = columns[m] - factor * columns[m][k:k + 1, :]
            work = work - factor * work[k:k + 1, :]
        done.append(work[:8])
        work = work[8:]
    full = jnp.concatenate(done, axis=0)
    diagonal = jnp.sum(jnp.where(col_at == row_at, full, 0.0), axis=1, keepdims=True)
    return (full / jnp.sqrt(diagonal))[:, RANK:]


def round_kernel(g_hbm, e_hbm, q_hbm, m_out, p_out, v_out, q_out,
                 g_buf, e_buf, q_buf, mh, ml, local_p, x_recv, z_send, z_recv, zb_recv, b_send, xb_recv, gathered, p_full,
                 t_recv, g_recv, t_part, t_all, t_full, g_full, t_total, g_total,
                 load_sem, q_sem, x_ssem, x_rsem, z_ssem, z_rsem, az_ssem, az_rsem, ax_ssem, ax_rsem,
                 zb_ssem, zb_rsem, xb_ssem, xb_rsem, xg_ssem, xg_rsem, bz_ssem, bz_rsem,
                 ts_sem, tr_sem, gs_sem, gr_sem, ta_ssem, ta_rsem, tg_ssem, tg_rsem, gg_ssem, gg_rsem):
    dp = lax.axis_index("dp")
    mp = lax.axis_index("mp")
    z, x = dp // NX, dp % NX
    y, core = mp // 2, mp % 2

    barrier = pltpu.get_barrier_semaphore()

    def greet(target):
        pl.semaphore_signal(barrier, inc=1, device_id=target, device_id_type=MESH)

    for k in reversed(NEAR_FIRST):
        greet(((z + k) % NZ * NX + x, mp))
    for k in MP_FAR_FIRST:
        greet((dp, (mp + k) % NMP))
    for i in (2, 1, 3):
        greet((z * NX + (x + i) % NX, mp))

    def place(i):
        c = (z + i) % NCHUNK
        return c, pl.ds(pl.multiple_of(c * CHUNK, CHUNK), CHUNK)

    def load(i):
        cols = place(i)[1]
        return (
            pltpu.make_async_copy(g_hbm.at[0, :, cols], g_buf.at[i], load_sem.at[i, 0]),
            pltpu.make_async_copy(e_hbm.at[0, :, cols], e_buf.at[i], load_sem.at[i, 1]),
        )

    q_copy = pltpu.make_async_copy(q_hbm, q_buf, q_sem)
    q_copy.start()
    for i in range(NCHUNK):
        for copy in load(i):
            copy.start()

    mh[COLS:256, :] = jnp.zeros((256 - COLS, FL), BF16)
    ml[COLS:256, :] = jnp.zeros((256 - COLS, FL), BF16)
    q_copy.wait()
    q_high, q_low = split(q_buf[0])
    q_both = jnp.concatenate([q_high, q_low], axis=0)

    def piece(t, to):
        return pl.ds(t * BLOCK + to * PIECE, PIECE)

    def rest(t):
        return pl.ds(t * BLOCK + REST, NX)

    def send_x(k):
        t = (z + 1 + k) % NZ
        for i in (2, 1, 3):
            to = (x + i) % NX
            remote(local_p.at[piece(t, to)], x_recv.at[t, i - 1], x_ssem, x_rsem.at[t], (z * NX + to, mp)).start()
        if k < NZ - 1:
            remote(local_p.at[rest(t)], zb_recv.at[k], zb_ssem, zb_rsem, (t * NX + x, mp)).start()

    for i in range(NCHUNK):
        c, cols = place(i)
        for copy in load(i):
            copy.wait()
        merged = g_buf[i].astype(F32) + e_buf[i]
        m_out[:, cols] = merged
        high, low = split(merged)
        mh[:COLS, cols] = high
        ml[:COLS, cols] = low
        both = dot(q_both, high, ((1,), (0,)))
        part = both[:RANK] + both[RANK:] + dot(q_high, low, ((1,), (0,)))
        for j in range(CHUNK // 128):
            for group in range(RANK // 4):
                unit = part[4 * group:4 * group + 4, 128 * j:128 * (j + 1)]
                local_p[c * 32 + (j * 16 + group)] = unit
        if i == 1:
            pl.semaphore_wait(barrier, NX - 1 + NZ - 1 + NMP - 1)
        if i:
            send_x(i - 1)
    send_x(NCHUNK - 1)
    send_x(NCHUNK)

    for k in range(NZ):
        t = (z + 1 + k) % NZ
        remote(x_recv.at[t], x_recv.at[t], x_ssem, x_rsem.at[t], (dp, mp)).wait_recv()
        z_send[k] = local_p[piece(t, x)] + x_recv[t, 0] + x_recv[t, 1] + x_recv[t, 2]
        if k < NZ - 1:
            remote(z_send.at[k], z_recv.at[k], z_ssem, z_rsem, (t * NX + x, mp)).start()
        if k == 4:
            remote(zb_recv, zb_recv, zb_ssem, zb_rsem, (dp, mp)).wait_recv()
            total = local_p[rest(z)]
            for j in range(NZ - 1):
                total = total + zb_recv[j]
            b_send[...] = total
            for i in (2, 1, 3):
                to = (x + i) % NX
                remote(b_send.at[to], xb_recv.at[i - 1], xb_ssem, xb_rsem, (z * NX + to, mp)).start()
    remote(z_recv, z_recv, z_ssem, z_rsem, (dp, mp)).wait_recv()
    mean = z_send[NZ - 1]
    for k in range(NZ - 1):
        mean = mean + z_recv[k]
    gathered[piece(z, x)] = mean * (1.0 / NDP)

    for k in NEAR_FIRST:
        remote(gathered.at[piece(z, x)], gathered.at[piece(z, x)], az_ssem, az_rsem.at[k], ((z + k) % NZ * NX + x, mp)).start()

    unit_own = z * BLOCK + REST + x
    remote(xb_recv, xb_recv, xb_ssem, xb_rsem, (dp, mp)).wait_recv()
    total = b_send[x] + xb_recv[0] + xb_recv[1] + xb_recv[2]
    gathered[unit_own] = total * (1.0 / NDP)
    for i in (2, 1, 3):
        to = (x + i) % NX
        remote(gathered.at[unit_own], gathered.at[unit_own], xg_ssem, xg_rsem, (z * NX + to, mp)).start()

    def on_to_x(t):
        for i in range(1, NX):
            remote(gathered.at[piece(t, x)], gathered.at[piece(t, x)], ax_ssem, ax_rsem.at[t], (z * NX + (x + i) % NX, mp)).start()

    on_to_x(z)
    remote(x_recv, x_recv, x_ssem, x_rsem.at[0], (dp, mp)).wait_send()
    remote(z_recv, z_recv, z_ssem, z_rsem, (dp, mp)).wait_send()
    remote(zb_recv, zb_recv, zb_ssem, zb_rsem, (dp, mp)).wait_send()
    remote(xb_recv, xb_recv, xb_ssem, xb_rsem, (dp, mp)).wait_send()
    for k in NEAR_FIRST:
        t = (z + NZ - k) % NZ
        remote(gathered.at[piece(t, x)], gathered.at[piece(t, x)], az_ssem, az_rsem.at[k], (dp, mp)).wait_recv()
        on_to_x(t)
        if k == 7:
            remote(xb_recv, xb_recv, xg_ssem, xg_rsem, (dp, mp)).wait_recv()
            for j in reversed(NEAR_FIRST):
                remote(gathered.at[rest(z)], gathered.at[rest(z)], bz_ssem, bz_rsem.at[j],
                       ((z + j) % NZ * NX + x, mp)).start()

    def accumulate(c):
        cols = pl.ds(pl.multiple_of(c * CHUNK, CHUNK), CHUNK)
        for j in range(CHUNK // 128):
            for group in range(RANK // 4):
                p_full[4 * group:4 * group + 4, 128 * j:128 * (j + 1)] = gathered[c * 32 + (j * 16 + group)]
        p_high, p_low = split(p_full[...])
        p_out[:RANK, cols] = p_high
        p_out[RANK:, cols] = p_low
        p_both = jnp.concatenate([p_high, p_low], axis=0)
        both = dot(p_both, mh[:, cols], ((1,), (1,)))
        t_full[...] += both[:RANK] + both[RANK:] + dot(p_high, ml[:, cols], ((1,), (1,)))
        both = dot(p_both, p_both, ((1,), (1,)))
        g_full[:, :RANK] += both[:RANK, :RANK] + both[:RANK, RANK:] + both[RANK:, :RANK]

    t_full[...] = jnp.zeros_like(t_full)
    g_full[...] = jnp.zeros_like(g_full)
    for k, chunks in ((0, ()), (1, (0,)), (7, (7,)), (2, (1,)), (6, (6,)), (3, (2,)), (5, (5,)), (4, (3, 4))):
        t = (z + k) % NZ
        remote(x_recv.at[t], x_recv.at[t], ax_ssem, ax_rsem.at[t], (dp, mp)).wait_recv()
        if k:
            remote(gathered.at[rest(t)], gathered.at[rest(t)], bz_ssem, bz_rsem.at[NZ - k], (dp, mp)).wait_recv()
        for o in chunks:
            c = (z + o) % NZ
            pl.when(c < NCHUNK)(functools.partial(accumulate, c))

    def rows(at):
        return pl.ds(pl.multiple_of(at * 8, 8), 8)

    def to_owner(ref, recv, ssem, rsem, k):
        owner = (y + k) % NY
        remote(ref.at[rows(owner)], recv.at[2 * k + core], ssem, rsem, (dp, 2 * owner)).start()

    for ref, recv, ssem, rsem in ((t_full, t_recv, ts_sem, tr_sem), (g_full, g_recv, gs_sem, gr_sem)):
        for k in reversed(NEAR_FIRST):
            to_owner(ref, recv, ssem, rsem, k)
        pl.when(core == 1)(functools.partial(to_owner, ref, recv, ssem, rsem, 0))
    remote(xb_recv, xb_recv, xg_ssem, xg_rsem, (dp, mp)).wait_send()
    remote(zb_recv, zb_recv, bz_ssem, bz_rsem.at[1], (dp, mp)).wait_send()
    remote(x_recv, x_recv, ax_ssem, ax_rsem.at[0], (dp, mp)).wait_send()
    remote(z_recv, z_recv, az_ssem, az_rsem.at[1], (dp, mp)).wait_send()

    def own_sum(ref, recv, ssem, rsem):
        arrived = recv.at[pl.ds(1, NMP - 1)]
        remote(arrived, arrived, ssem, rsem, (dp, mp)).wait_recv()
        total = ref[rows(y), :]
        for k in range(1, NMP):
            total = total + recv[k]
        return total

    def to_all(ref, ssem, rsem):
        for k in MP_FAR_FIRST:
            remote(ref.at[rows(y)], ref.at[rows(y)], ssem, rsem, (dp, (mp + k) % NMP)).start()

    @pl.when(core == 0)
    def _():
        total = own_sum(t_full, t_recv, ts_sem, tr_sem)
        t_all[dp] = total
        t_part[...] = total
        for i, j in DP_FAR_FIRST:
            to = (z + i) % NZ * NX + (x + j) % NX
            remote(t_part, t_all.at[dp], ta_ssem, ta_rsem, (to, mp)).start()
        g_total[rows(y), :] = own_sum(g_full, g_recv, gs_sem, gr_sem)
        to_all(g_total, gg_ssem, gg_rsem)
        for sent, ssem, rsem in (
            (t_full.at[pl.ds(0, 8 * (NY - 1))], ts_sem, tr_sem),
            (g_full.at[pl.ds(0, 8 * (NY - 1))], gs_sem, gr_sem),
        ):
            remote(sent, sent, ssem, rsem, (dp, mp)).wait_send()
        arrived = t_all.at[pl.ds(0, NDP - 1)]
        remote(arrived, arrived, ta_ssem, ta_rsem, (dp, mp)).wait_recv()
        total = t_all[0]
        for k in range(1, NDP):
            total = total + t_all[k]
        t_total[rows(y), :] = total
        to_all(t_total, tg_ssem, tg_rsem)
        remote(arrived, arrived, ta_ssem, ta_rsem, (dp, mp)).wait_send()

    @pl.when(core == 1)
    def _():
        remote(t_full, t_full, ts_sem, tr_sem, (dp, mp)).wait_send()
        remote(g_full, g_full, gs_sem, gr_sem, (dp, mp)).wait_send()

    def wait_rows(ref, ssem, rsem):
        @pl.when(core == 0)
        def _():
            others = ref.at[pl.ds(0, 8 * (NY - 1))]
            remote(others, others, ssem, rsem, (dp, mp)).wait_recv()

        @pl.when(core == 1)
        def _():
            remote(ref, ref, ssem, rsem, (dp, mp)).wait_recv()

    wait_rows(g_total, gg_ssem, gg_rsem)
    inverse = inverse_factor(g_total[...])
    wait_rows(t_total, tg_ssem, tg_rsem)
    exact = lax.Precision.HIGHEST
    q_rows = lax.dot_general(
        inverse, t_total[...] * (1.0 / NDP), (((1,), (0,)), ((), ())),
        precision=exact, preferred_element_type=F32,
    )[:, :COLS]
    q_out[0] = q_rows
    v_out[...] = lax.dot_general(
        q_rows, inverse, (((0,), (0,)), ((), ())), precision=exact, preferred_element_type=F32
    )

    @pl.when(core == 0)
    def _():
        for recv, ssem, rsem in ((g_recv, gg_ssem, gg_rsem), (t_recv, tg_ssem, tg_rsem)):
            sent = recv.at[pl.ds(1, NMP - 1)]
            remote(sent, sent, ssem, rsem, (dp, mp)).wait_send()


def output_kernel(m_ref, p_ref, v_ref, q_ref, u_hbm, e_hbm, q_out, u_buf, e_buf, store_sem):
    v_high, v_low = split(v_ref[...])
    left = jnp.concatenate([v_high, v_low, v_high], axis=1)

    def store(c):
        cols = pl.ds(c * CHUNK, CHUNK)
        return (
            pltpu.make_async_copy(u_buf.at[:, cols], u_hbm.at[:, cols], store_sem.at[c, 0]),
            pltpu.make_async_copy(e_buf.at[:, cols], e_hbm.at[0, :, cols], store_sem.at[c, 1]),
        )

    for c in range(NCHUNK):
        cols = slice(c * CHUNK, (c + 1) * CHUNK)
        p_high = p_ref[:RANK, cols]
        right = jnp.concatenate([p_high, p_high, p_ref[RANK:, cols]], axis=0)
        update = dot(left, right, ((1,), (0,)))
        u_buf[:, cols] = update.astype(BF16)
        e_buf[:, cols] = m_ref[:, cols] - update
        for copy in store(c):
            copy.start()
    q_out[...] = q_ref[...]
    for c in range(NCHUNK):
        for copy in store(c):
            copy.wait()


def on_device(gradients, errors, q_start):
    vmem = pl.BlockSpec(memory_space=pltpu.VMEM)
    hbm = pl.BlockSpec(memory_space=pl.ANY)
    dma, reg = pltpu.SemaphoreType.DMA, pltpu.SemaphoreType.REGULAR
    merged, p_both, v, q_rows = pl.pallas_call(
        round_kernel,
        name="power_round",
        out_shape=(
            jax.ShapeDtypeStruct((COLS, FL), F32),
            jax.ShapeDtypeStruct((2 * RANK, FL), BF16),
            jax.ShapeDtypeStruct((COLS, RANK), F32),
            jax.ShapeDtypeStruct((1, RANK, COLS), F32),
        ),
        in_specs=[hbm, hbm, hbm],
        out_specs=(vmem, vmem, vmem, vmem),
        scratch_shapes=[
            pltpu.VMEM((NCHUNK, COLS, CHUNK), BF16),
            pltpu.VMEM((NCHUNK, COLS, CHUNK), F32),
            pltpu.VMEM((1, RANK, COLS), F32),
            pltpu.VMEM((256, FL), BF16),
            pltpu.VMEM((256, FL), BF16),
            pltpu.VMEM((UNITS, 4, 128), F32),
            pltpu.VMEM((NZ, NX - 1, PIECE, 4, 128), F32),
            pltpu.VMEM((NZ, PIECE, 4, 128), F32),
            pltpu.VMEM((NZ - 1, PIECE, 4, 128), F32),
            pltpu.VMEM((NZ - 1, NX, 4, 128), F32),
            pltpu.VMEM((NX, 4, 128), F32),
            pltpu.VMEM((NX - 1, 4, 128), F32),
            pltpu.VMEM((UNITS, 4, 128), F32),
            pltpu.VMEM((RANK, CHUNK), F32),
            pltpu.VMEM((NMP, 8, 256), F32),
            pltpu.VMEM((NMP, 8, 128), F32),
            pltpu.VMEM((8, 256), F32),
            pltpu.VMEM((NDP, 8, 256), F32),
            pltpu.VMEM((RANK, 256), F32),
            pltpu.VMEM((RANK, 128), F32),
            pltpu.VMEM((RANK, 256), F32),
            pltpu.VMEM((RANK, 128), F32),
            dma((NCHUNK, 2)), dma,
            dma, dma((NZ,)), dma, dma, dma, dma((NZ,)), dma, dma((NZ,)),
            dma, dma, dma, dma, dma, dma, dma, dma((NZ,)), dma, dma,
            dma, dma, dma, dma, dma, dma, dma, dma,
        ],
        compiler_params=pltpu.CompilerParams(
            collective_id=0, has_side_effects=True, vmem_limit_bytes=LIMIT
        ),
    )(*(pltpu.with_memory_space_constraint(a, pltpu.HBM) for a in (gradients, errors, jnp.swapaxes(q_start, 1, 2))))

    update_grad, new_errors, q_rows = pl.pallas_call(
        output_kernel,
        name="outputs",
        out_shape=(
            jax.ShapeDtypeStruct((COLS, FL), BF16),
            jax.ShapeDtypeStruct((1, COLS, FL), F32),
            jax.ShapeDtypeStruct((1, RANK, COLS), F32),
        ),
        in_specs=[vmem, vmem, vmem, vmem],
        out_specs=(hbm, hbm, vmem),
        scratch_shapes=[
            pltpu.VMEM((COLS, FL), BF16),
            pltpu.VMEM((COLS, FL), F32),
            dma((NCHUNK, 2)),
        ],
        compiler_params=pltpu.CompilerParams(vmem_limit_bytes=LIMIT),
    )(merged, p_both, v, q_rows)
    return update_grad, new_errors, jnp.swapaxes(q_rows, 1, 2)


def solution(mesh):
    return jax.shard_map(
        on_device,
        mesh=mesh,
        in_specs=(P("dp", None, "mp"), P("dp", None, "mp"), P()),
        out_specs=(P(None, "mp"), P("dp", None, "mp"), P()),
        check_vma=False,
    )
```

```python
import functools

import jax
import jax.numpy as jnp
from jax import lax
from jax.experimental import pallas as pl
from jax.experimental.pallas import tpu as pltpu
from jax.sharding import PartitionSpec as P

MESH = pl.DeviceIdType.MESH
NX, NY, NZ, NMP = 4, 8, 8, 16
NDP = NX * NZ
COLS, RANK, FL = 240, 64, 1792
CHUNK = 256
NCHUNK = FL // CHUNK
LIMIT = 30 << 20
F32, BF16 = jnp.float32, jnp.bfloat16
UNITS = FL // 128 * 16
BLOCK = UNITS // NZ
PIECE = 6
REST = NX * PIECE
NEAR_FIRST = (1, 7, 2, 6, 3, 5, 4)
MP_FAR_FIRST = (9, 8, 7, 10, 11, 6, 5, 12, 13, 4, 3, 14, 15, 2, 1)


def ring(offset, size):
    return min(offset % size, -offset % size)


DP_FAR_FIRST = sorted(
    ((i, j) for i in range(NZ) for j in range(NX) if i or j),
    key=lambda o: (-ring(o[0], NZ) - ring(o[1], NX), -o[0], -o[1]),
)


def split(value):
    high = value.astype(BF16)
    return high, (value - high.astype(F32)).astype(BF16)


def dot(a, b, dims):
    return lax.dot_general(a, b, (dims, ((), ())), preferred_element_type=F32)


def remote(src, dst, send, recv, target):
    return pltpu.make_async_remote_copy(
        src_ref=src, dst_ref=dst, send_sem=send, recv_sem=recv,
        device_id=target, device_id_type=MESH,
    )


def inverse_factor(gram):
    row_at = lax.broadcasted_iota(jnp.int32, (RANK, 2 * RANK), 0)
    col_at = lax.broadcasted_iota(jnp.int32, (RANK, 2 * RANK), 1)
    work = jnp.where(col_at == row_at + RANK, 1.0, gram)
    done = []
    for first in range(0, RANK, 8):
        at = lax.broadcasted_iota(jnp.int32, work.shape, 0)
        columns = [jnp.broadcast_to(work[:, first + k:first + k + 1], work.shape) for k in range(8)]
        for k in range(8):
            factor = jnp.where(at > k, columns[k] * (1.0 / columns[k][k:k + 1, :]), 0.0)
            for m in range(k + 1, 8):
                columns[m] = columns[m] - factor * columns[m][k:k + 1, :]
            work = work - factor * work[k:k + 1, :]
        done.append(work[:8])
        work = work[8:]
    full = jnp.concatenate(done, axis=0)
    diagonal = jnp.sum(jnp.where(col_at == row_at, full, 0.0), axis=1, keepdims=True)
    return (full / jnp.sqrt(diagonal))[:, RANK:]


def round_kernel(g_hbm, e_hbm, q_hbm, m_out, p_out, v_out, q_out,
                 g_buf, e_buf, q_buf, mh, ml, local_p, x_recv, z_send, z_recv, zb_recv, b_send, xb_recv, gathered, p_full,
                 t_recv, t_part, t_all, t_full, t_total, g_total,
                 load_sem, q_sem, x_ssem, x_rsem, z_ssem, z_rsem, az_ssem, az_rsem, ax_ssem, ax_rsem,
                 zb_ssem, zb_rsem, xb_ssem, xb_rsem, xg_ssem, xg_rsem, bz_ssem, bz_rsem,
                 ts_sem, tr_sem, gh_ssem, gh_rsem, ta_ssem, ta_rsem, tg_ssem, tg_rsem, gg_ssem, gg_rsem):
    dp = lax.axis_index("dp")
    mp = lax.axis_index("mp")
    z, x = dp // NX, dp % NX
    y, core = mp // 2, mp % 2

    barrier = pltpu.get_barrier_semaphore()

    def greet(target):
        pl.semaphore_signal(barrier, inc=1, device_id=target, device_id_type=MESH)

    for k in reversed(NEAR_FIRST):
        greet(((z + k) % NZ * NX + x, mp))
    for k in MP_FAR_FIRST:
        greet((dp, (mp + k) % NMP))
    for i in (2, 1, 3):
        greet((z * NX + (x + i) % NX, mp))

    def place(i):
        c = (z + i) % NCHUNK
        return c, pl.ds(pl.multiple_of(c * CHUNK, CHUNK), CHUNK)

    def load(i):
        cols = place(i)[1]
        return (
            pltpu.make_async_copy(g_hbm.at[0, :, cols], g_buf.at[i], load_sem.at[i, 0]),
            pltpu.make_async_copy(e_hbm.at[0, :, cols], e_buf.at[i], load_sem.at[i, 1]),
        )

    q_copy = pltpu.make_async_copy(q_hbm, q_buf, q_sem)
    q_copy.start()
    for i in range(NCHUNK):
        for copy in load(i):
            copy.start()

    mh[COLS:256, :] = jnp.zeros((256 - COLS, FL), BF16)
    ml[COLS:256, :] = jnp.zeros((256 - COLS, FL), BF16)
    q_copy.wait()
    q_high, q_low = split(q_buf[0])
    q_both = jnp.concatenate([q_high, q_low], axis=0)

    def piece(t, to):
        return pl.ds(t * BLOCK + to * PIECE, PIECE)

    def rest(t):
        return pl.ds(t * BLOCK + REST, NX)

    def send_x(k):
        t = (z + 1 + k) % NZ
        for i in (2, 1, 3):
            to = (x + i) % NX
            remote(local_p.at[piece(t, to)], x_recv.at[t, i - 1], x_ssem, x_rsem.at[t], (z * NX + to, mp)).start()
        if k < NZ - 1:
            remote(local_p.at[rest(t)], zb_recv.at[k], zb_ssem, zb_rsem, (t * NX + x, mp)).start()

    for i in range(NCHUNK):
        c, cols = place(i)
        for copy in load(i):
            copy.wait()
        merged = g_buf[i].astype(F32) + e_buf[i]
        m_out[:, cols] = merged
        high, low = split(merged)
        mh[:COLS, cols] = high
        ml[:COLS, cols] = low
        both = dot(q_both, high, ((1,), (0,)))
        part = both[:RANK] + both[RANK:] + dot(q_high, low, ((1,), (0,)))
        for j in range(CHUNK // 128):
            for group in range(RANK // 4):
                unit = part[4 * group:4 * group + 4, 128 * j:128 * (j + 1)]
                local_p[c * 32 + (j * 16 + group)] = unit
        if i == 1:
            pl.semaphore_wait(barrier, NX - 1 + NZ - 1 + NMP - 1)
        if i:
            send_x(i - 1)
    send_x(NCHUNK - 1)
    send_x(NCHUNK)

    for k in range(NZ):
        t = (z + 1 + k) % NZ
        remote(x_recv.at[t], x_recv.at[t], x_ssem, x_rsem.at[t], (dp, mp)).wait_recv()
        z_send[k] = local_p[piece(t, x)] + x_recv[t, 0] + x_recv[t, 1] + x_recv[t, 2]
        if k < NZ - 1:
            remote(z_send.at[k], z_recv.at[k], z_ssem, z_rsem, (t * NX + x, mp)).start()
        if k == 4:
            remote(zb_recv, zb_recv, zb_ssem, zb_rsem, (dp, mp)).wait_recv()
            total = local_p[rest(z)]
            for j in range(NZ - 1):
                total = total + zb_recv[j]
            b_send[...] = total
            for i in (2, 1, 3):
                to = (x + i) % NX
                remote(b_send.at[to], xb_recv.at[i - 1], xb_ssem, xb_rsem, (z * NX + to, mp)).start()
    remote(z_recv, z_recv, z_ssem, z_rsem, (dp, mp)).wait_recv()
    mean = z_send[NZ - 1]
    for k in range(NZ - 1):
        mean = mean + z_recv[k]
    gathered[piece(z, x)] = mean * (1.0 / NDP)

    for k in NEAR_FIRST:
        remote(gathered.at[piece(z, x)], gathered.at[piece(z, x)], az_ssem, az_rsem.at[k], ((z + k) % NZ * NX + x, mp)).start()

    unit_own = z * BLOCK + REST + x
    remote(xb_recv, xb_recv, xb_ssem, xb_rsem, (dp, mp)).wait_recv()
    total = b_send[x] + xb_recv[0] + xb_recv[1] + xb_recv[2]
    gathered[unit_own] = total * (1.0 / NDP)
    for i in (2, 1, 3):
        to = (x + i) % NX
        remote(gathered.at[unit_own], gathered.at[unit_own], xg_ssem, xg_rsem, (z * NX + to, mp)).start()

    def on_to_x(t):
        for i in range(1, NX):
            remote(gathered.at[piece(t, x)], gathered.at[piece(t, x)], ax_ssem, ax_rsem.at[t], (z * NX + (x + i) % NX, mp)).start()

    on_to_x(z)
    remote(x_recv, x_recv, x_ssem, x_rsem.at[0], (dp, mp)).wait_send()
    remote(z_recv, z_recv, z_ssem, z_rsem, (dp, mp)).wait_send()
    remote(zb_recv, zb_recv, zb_ssem, zb_rsem, (dp, mp)).wait_send()
    remote(xb_recv, xb_recv, xb_ssem, xb_rsem, (dp, mp)).wait_send()
    for k in NEAR_FIRST:
        t = (z + NZ - k) % NZ
        remote(gathered.at[piece(t, x)], gathered.at[piece(t, x)], az_ssem, az_rsem.at[k], (dp, mp)).wait_recv()
        on_to_x(t)
        if k == 7:
            remote(xb_recv, xb_recv, xg_ssem, xg_rsem, (dp, mp)).wait_recv()
            for j in reversed(NEAR_FIRST):
                remote(gathered.at[rest(z)], gathered.at[rest(z)], bz_ssem, bz_rsem.at[j],
                       ((z + j) % NZ * NX + x, mp)).start()

    def accumulate(c):
        cols = pl.ds(pl.multiple_of(c * CHUNK, CHUNK), CHUNK)
        for j in range(CHUNK // 128):
            for group in range(RANK // 4):
                p_full[4 * group:4 * group + 4, 128 * j:128 * (j + 1)] = gathered[c * 32 + (j * 16 + group)]
        p_high, p_low = split(p_full[...])
        p_out[:RANK, cols] = p_high
        p_out[RANK:, cols] = p_low
        p_both = jnp.concatenate([p_high, p_low], axis=0)
        both = dot(p_both, mh[:, cols], ((1,), (1,)))
        t_full[:, :256] += both[:RANK] + both[RANK:] + dot(p_high, ml[:, cols], ((1,), (1,)))
        both = dot(p_both, p_both, ((1,), (1,)))
        t_full[:, 256:256 + RANK] += both[:RANK, :RANK] + both[:RANK, RANK:] + both[RANK:, :RANK]

    t_full[...] = jnp.zeros_like(t_full)
    for k, chunks in ((0, ()), (1, (0,)), (7, (7,)), (2, (1,)), (6, (6,)), (3, (2,)), (5, (5,)), (4, (3, 4))):
        t = (z + k) % NZ
        remote(x_recv.at[t], x_recv.at[t], ax_ssem, ax_rsem.at[t], (dp, mp)).wait_recv()
        if k:
            remote(gathered.at[rest(t)], gathered.at[rest(t)], bz_ssem, bz_rsem.at[NZ - k], (dp, mp)).wait_recv()
        for o in chunks:
            c = (z + o) % NZ
            pl.when(c < NCHUNK)(functools.partial(accumulate, c))

    def rows(at):
        return pl.ds(pl.multiple_of(at * 8, 8), 8)

    def to_owner(k):
        owner = (y + k) % NY
        remote(t_full.at[rows(owner)], t_recv.at[2 * k + core], ts_sem, tr_sem, (dp, 2 * owner)).start()

    for k in reversed(NEAR_FIRST):
        to_owner(k)
    pl.when(core == 1)(functools.partial(to_owner, 0))
    remote(xb_recv, xb_recv, xg_ssem, xg_rsem, (dp, mp)).wait_send()
    remote(zb_recv, zb_recv, bz_ssem, bz_rsem.at[1], (dp, mp)).wait_send()
    remote(x_recv, x_recv, ax_ssem, ax_rsem.at[0], (dp, mp)).wait_send()
    remote(z_recv, z_recv, az_ssem, az_rsem.at[1], (dp, mp)).wait_send()

    def handed(core_1):
        return remote(g_total, g_total, gh_ssem, gh_rsem, (dp, core_1))

    @pl.when(core == 0)
    def _():
        arrived = t_recv.at[pl.ds(1, NMP - 1)]
        remote(arrived, arrived, ts_sem, tr_sem, (dp, mp)).wait_recv()
        total = t_full[rows(y), :]
        for k in range(1, NMP):
            total = total + t_recv[k]
        t_all[dp] = total[:, :256]
        t_part[...] = total[:, :256]
        g_total[rows(y), :] = total[:, 256:]
        for i, j in DP_FAR_FIRST:
            to = (z + i) % NZ * NX + (x + j) % NX
            remote(t_part, t_all.at[dp], ta_ssem, ta_rsem, (to, mp)).start()
        for k in reversed(NEAR_FIRST):
            mine = g_total.at[rows(y)]
            remote(mine, mine, gg_ssem, gg_rsem, (dp, 2 * ((y + k) % NY))).start()
        sent = t_full.at[pl.ds(0, 8 * (NY - 1))]
        remote(sent, sent, ts_sem, tr_sem, (dp, mp)).wait_send()
        others = g_total.at[pl.ds(0, 8 * (NY - 1))]
        remote(others, others, gg_ssem, gg_rsem, (dp, mp)).wait_recv()
        handed(mp + 1).start()
        arrived = t_all.at[pl.ds(0, NDP - 1)]
        remote(arrived, arrived, ta_ssem, ta_rsem, (dp, mp)).wait_recv()
        total = t_all[0]
        for k in range(1, NDP):
            total = total + t_all[k]
        t_total[rows(y), :] = total
        for k in MP_FAR_FIRST:
            mine = t_total.at[rows(y)]
            remote(mine, mine, tg_ssem, tg_rsem, (dp, (mp + k) % NMP)).start()
        remote(arrived, arrived, ta_ssem, ta_rsem, (dp, mp)).wait_send()
        remote(others, others, gg_ssem, gg_rsem, (dp, mp)).wait_send()

    @pl.when(core == 1)
    def _():
        remote(t_full, t_full, ts_sem, tr_sem, (dp, mp)).wait_send()
        handed(mp).wait_recv()

    inverse = inverse_factor(g_total[...])

    @pl.when(core == 0)
    def _():
        others = t_total.at[pl.ds(0, 8 * (NY - 1))]
        remote(others, others, tg_ssem, tg_rsem, (dp, mp)).wait_recv()

    @pl.when(core == 1)
    def _():
        remote(t_total, t_total, tg_ssem, tg_rsem, (dp, mp)).wait_recv()

    exact = lax.Precision.HIGHEST
    q_rows = lax.dot_general(
        inverse, t_total[...] * (1.0 / NDP), (((1,), (0,)), ((), ())),
        precision=exact, preferred_element_type=F32,
    )[:, :COLS]
    q_out[0] = q_rows
    v_out[...] = lax.dot_general(
        q_rows, inverse, (((0,), (0,)), ((), ())), precision=exact, preferred_element_type=F32
    )

    @pl.when(core == 0)
    def _():
        sent = t_all.at[pl.ds(0, NMP - 1)]
        remote(sent, sent, tg_ssem, tg_rsem, (dp, mp)).wait_send()
        handed(mp).wait_send()


def output_kernel(m_ref, p_ref, v_ref, q_ref, u_hbm, e_hbm, q_out, u_buf, e_buf, store_sem):
    v_high, v_low = split(v_ref[...])
    left = jnp.concatenate([v_high, v_low, v_high], axis=1)

    def store(c):
        cols = pl.ds(c * CHUNK, CHUNK)
        return (
            pltpu.make_async_copy(u_buf.at[:, cols], u_hbm.at[:, cols], store_sem.at[c, 0]),
            pltpu.make_async_copy(e_buf.at[:, cols], e_hbm.at[0, :, cols], store_sem.at[c, 1]),
        )

    for c in range(NCHUNK):
        cols = slice(c * CHUNK, (c + 1) * CHUNK)
        p_high = p_ref[:RANK, cols]
        right = jnp.concatenate([p_high, p_high, p_ref[RANK:, cols]], axis=0)
        update = dot(left, right, ((1,), (0,)))
        u_buf[:, cols] = update.astype(BF16)
        e_buf[:, cols] = m_ref[:, cols] - update
        for copy in store(c):
            copy.start()
    q_out[...] = q_ref[...]
    for c in range(NCHUNK):
        for copy in store(c):
            copy.wait()


def on_device(gradients, errors, q_start):
    vmem = pl.BlockSpec(memory_space=pltpu.VMEM)
    hbm = pl.BlockSpec(memory_space=pl.ANY)
    dma, reg = pltpu.SemaphoreType.DMA, pltpu.SemaphoreType.REGULAR
    merged, p_both, v, q_rows = pl.pallas_call(
        round_kernel,
        name="power_round",
        out_shape=(
            jax.ShapeDtypeStruct((COLS, FL), F32),
            jax.ShapeDtypeStruct((2 * RANK, FL), BF16),
            jax.ShapeDtypeStruct((COLS, RANK), F32),
            jax.ShapeDtypeStruct((1, RANK, COLS), F32),
        ),
        in_specs=[hbm, hbm, hbm],
        out_specs=(vmem, vmem, vmem, vmem),
        scratch_shapes=[
            pltpu.VMEM((NCHUNK, COLS, CHUNK), BF16),
            pltpu.VMEM((NCHUNK, COLS, CHUNK), F32),
            pltpu.VMEM((1, RANK, COLS), F32),
            pltpu.VMEM((256, FL), BF16),
            pltpu.VMEM((256, FL), BF16),
            pltpu.VMEM((UNITS, 4, 128), F32),
            pltpu.VMEM((NZ, NX - 1, PIECE, 4, 128), F32),
            pltpu.VMEM((NZ, PIECE, 4, 128), F32),
            pltpu.VMEM((NZ - 1, PIECE, 4, 128), F32),
            pltpu.VMEM((NZ - 1, NX, 4, 128), F32),
            pltpu.VMEM((NX, 4, 128), F32),
            pltpu.VMEM((NX - 1, 4, 128), F32),
            pltpu.VMEM((UNITS, 4, 128), F32),
            pltpu.VMEM((RANK, CHUNK), F32),
            pltpu.VMEM((NMP, 8, 384), F32),
            pltpu.VMEM((8, 256), F32),
            pltpu.VMEM((NDP, 8, 256), F32),
            pltpu.VMEM((RANK, 384), F32),
            pltpu.VMEM((RANK, 256), F32),
            pltpu.VMEM((RANK, 128), F32),
            dma((NCHUNK, 2)), dma,
            dma, dma((NZ,)), dma, dma, dma, dma((NZ,)), dma, dma((NZ,)),
            dma, dma, dma, dma, dma, dma, dma, dma((NZ,)), dma, dma,
            dma, dma, dma, dma, dma, dma, dma, dma,
        ],
        compiler_params=pltpu.CompilerParams(
            collective_id=0, has_side_effects=True, vmem_limit_bytes=LIMIT
        ),
    )(*(pltpu.with_memory_space_constraint(a, pltpu.HBM) for a in (gradients, errors, jnp.swapaxes(q_start, 1, 2))))

    update_grad, new_errors, q_rows = pl.pallas_call(
        output_kernel,
        name="outputs",
        out_shape=(
            jax.ShapeDtypeStruct((COLS, FL), BF16),
            jax.ShapeDtypeStruct((1, COLS, FL), F32),
            jax.ShapeDtypeStruct((1, RANK, COLS), F32),
        ),
        in_specs=[vmem, vmem, vmem, vmem],
        out_specs=(hbm, hbm, vmem),
        scratch_shapes=[
            pltpu.VMEM((COLS, FL), BF16),
            pltpu.VMEM((COLS, FL), F32),
            dma((NCHUNK, 2)),
        ],
        compiler_params=pltpu.CompilerParams(vmem_limit_bytes=LIMIT),
    )(merged, p_both, v, q_rows)
    return update_grad, new_errors, jnp.swapaxes(q_rows, 1, 2)


def solution(mesh):
    return jax.shard_map(
        on_device,
        mesh=mesh,
        in_specs=(P("dp", None, "mp"), P("dp", None, "mp"), P()),
        out_specs=(P(None, "mp"), P("dp", None, "mp"), P()),
        check_vma=False,
    )
```

```python
import functools

import jax
import jax.numpy as jnp
from jax import lax
from jax.experimental import pallas as pl
from jax.experimental.pallas import tpu as pltpu
from jax.sharding import PartitionSpec as P

MESH = pl.DeviceIdType.MESH
NX, NY, NZ, NMP = 4, 8, 8, 16
NDP = NX * NZ
COLS, RANK, FL = 240, 64, 1792
CHUNK = 256
NCHUNK = FL // CHUNK
LIMIT = 30 << 20
F32, BF16 = jnp.float32, jnp.bfloat16
UNITS = FL // 128 * 16
BLOCK = UNITS // NZ
PIECE = 6
REST = NX * PIECE
NEAR_FIRST = (1, 7, 2, 6, 3, 5, 4)
MP_FAR_FIRST = (9, 8, 7, 10, 11, 6, 5, 12, 13, 4, 3, 14, 15, 2, 1)


def ring(offset, size):
    return min(offset % size, -offset % size)


DP_FAR_FIRST = sorted(
    ((i, j) for i in range(NZ) for j in range(NX) if i or j),
    key=lambda o: (-ring(o[0], NZ) - ring(o[1], NX), -o[0], -o[1]),
)


def split(value):
    high = value.astype(BF16)
    return high, (value - high.astype(F32)).astype(BF16)


def dot(a, b, dims):
    return lax.dot_general(a, b, (dims, ((), ())), preferred_element_type=F32)


def remote(src, dst, send, recv, target):
    return pltpu.make_async_remote_copy(
        src_ref=src, dst_ref=dst, send_sem=send, recv_sem=recv,
        device_id=target, device_id_type=MESH,
    )


def inverse_factor(gram):
    row_at = lax.broadcasted_iota(jnp.int32, (RANK, 2 * RANK), 0)
    col_at = lax.broadcasted_iota(jnp.int32, (RANK, 2 * RANK), 1)
    work = jnp.where(col_at == row_at + RANK, 1.0, gram)
    done = []
    for first in range(0, RANK, 8):
        at = lax.broadcasted_iota(jnp.int32, work.shape, 0)
        columns = [jnp.broadcast_to(work[:, first + k:first + k + 1], work.shape) for k in range(8)]
        for k in range(8):
            factor = jnp.where(at > k, columns[k] * (1.0 / columns[k][k:k + 1, :]), 0.0)
            for m in range(k + 1, 8):
                columns[m] = columns[m] - factor * columns[m][k:k + 1, :]
            work = work - factor * work[k:k + 1, :]
        done.append(work[:8])
        work = work[8:]
    full = jnp.concatenate(done, axis=0)
    diagonal = jnp.sum(jnp.where(col_at == row_at, full, 0.0), axis=1, keepdims=True)
    return (full / jnp.sqrt(diagonal))[:, RANK:]


def round_kernel(g_hbm, e_hbm, q_hbm, m_out, p_out, v_out, q_out,
                 g_buf, e_buf, q_buf, mh, ml, local_p, x_recv, z_send, z_recv, zb_recv, b_send, xb_recv, gathered, p_full,
                 t_recv, t_part, t_all, t_full, t_total, g_full, g_peer, g_recv, g_total,
                 load_sem, q_sem, x_ssem, x_rsem, z_ssem, z_rsem, az_ssem, az_rsem, ax_ssem, ax_rsem,
                 zb_ssem, zb_rsem, xb_ssem, xb_rsem, xg_ssem, xg_rsem, bz_ssem, bz_rsem,
                 ts_sem, tr_sem, gh_ssem, gh_rsem, ta_ssem, ta_rsem, tg_ssem, tg_rsem, gg_ssem, gg_rsem, gp_ssem, gp_rsem, gs_ssem, gs_rsem):
    dp = lax.axis_index("dp")
    mp = lax.axis_index("mp")
    z, x = dp // NX, dp % NX
    y, core = mp // 2, mp % 2

    barrier = pltpu.get_barrier_semaphore()

    def greet(target):
        pl.semaphore_signal(barrier, inc=1, device_id=target, device_id_type=MESH)

    for k in reversed(NEAR_FIRST):
        greet(((z + k) % NZ * NX + x, mp))
    for k in MP_FAR_FIRST:
        greet((dp, (mp + k) % NMP))
    for i in (2, 1, 3):
        greet((z * NX + (x + i) % NX, mp))

    def place(i):
        c = (z + i) % NCHUNK
        return c, pl.ds(pl.multiple_of(c * CHUNK, CHUNK), CHUNK)

    def load(i):
        cols = place(i)[1]
        return (
            pltpu.make_async_copy(g_hbm.at[0, :, cols], g_buf.at[i], load_sem.at[i, 0]),
            pltpu.make_async_copy(e_hbm.at[0, :, cols], e_buf.at[i], load_sem.at[i, 1]),
        )

    q_copy = pltpu.make_async_copy(q_hbm, q_buf, q_sem)
    q_copy.start()
    for i in range(NCHUNK):
        for copy in load(i):
            copy.start()

    mh[COLS:256, :] = jnp.zeros((256 - COLS, FL), BF16)
    ml[COLS:256, :] = jnp.zeros((256 - COLS, FL), BF16)
    q_copy.wait()
    q_high, q_low = split(q_buf[0])
    q_both = jnp.concatenate([q_high, q_low], axis=0)

    def piece(t, to):
        return pl.ds(t * BLOCK + to * PIECE, PIECE)

    def rest(t):
        return pl.ds(t * BLOCK + REST, NX)

    def send_x(k):
        t = (z + 1 + k) % NZ
        for i in (2, 1, 3):
            to = (x + i) % NX
            remote(local_p.at[piece(t, to)], x_recv.at[t, i - 1], x_ssem, x_rsem.at[t], (z * NX + to, mp)).start()
        if k < NZ - 1:
            remote(local_p.at[rest(t)], zb_recv.at[k], zb_ssem, zb_rsem, (t * NX + x, mp)).start()

    for i in range(NCHUNK):
        c, cols = place(i)
        for copy in load(i):
            copy.wait()
        merged = g_buf[i].astype(F32) + e_buf[i]
        m_out[:, cols] = merged
        high, low = split(merged)
        mh[:COLS, cols] = high
        ml[:COLS, cols] = low
        both = dot(q_both, high, ((1,), (0,)))
        part = both[:RANK] + both[RANK:] + dot(q_high, low, ((1,), (0,)))
        for j in range(CHUNK // 128):
            for group in range(RANK // 4):
                unit = part[4 * group:4 * group + 4, 128 * j:128 * (j + 1)]
                local_p[c * 32 + (j * 16 + group)] = unit
        if i == 1:
            pl.semaphore_wait(barrier, NX - 1 + NZ - 1 + NMP - 1)
        if i:
            send_x(i - 1)
    send_x(NCHUNK - 1)
    send_x(NCHUNK)

    for k in range(NZ):
        t = (z + 1 + k) % NZ
        remote(x_recv.at[t], x_recv.at[t], x_ssem, x_rsem.at[t], (dp, mp)).wait_recv()
        z_send[k] = local_p[piece(t, x)] + x_recv[t, 0] + x_recv[t, 1] + x_recv[t, 2]
        if k < NZ - 1:
            remote(z_send.at[k], z_recv.at[k], z_ssem, z_rsem, (t * NX + x, mp)).start()
        if k == 4:
            remote(zb_recv, zb_recv, zb_ssem, zb_rsem, (dp, mp)).wait_recv()
            total = local_p[rest(z)]
            for j in range(NZ - 1):
                total = total + zb_recv[j]
            b_send[...] = total
            for i in (2, 1, 3):
                to = (x + i) % NX
                remote(b_send.at[to], xb_recv.at[i - 1], xb_ssem, xb_rsem, (z * NX + to, mp)).start()
    remote(z_recv, z_recv, z_ssem, z_rsem, (dp, mp)).wait_recv()
    mean = z_send[NZ - 1]
    for k in range(NZ - 1):
        mean = mean + z_recv[k]
    gathered[piece(z, x)] = mean * (1.0 / NDP)

    for k in (1, 7, 4, 2, 6, 3, 5):
        remote(gathered.at[piece(z, x)], gathered.at[piece(z, x)], az_ssem, az_rsem.at[k], ((z + k) % NZ * NX + x, mp)).start()

    unit_own = z * BLOCK + REST + x
    remote(xb_recv, xb_recv, xb_ssem, xb_rsem, (dp, mp)).wait_recv()
    total = b_send[x] + xb_recv[0] + xb_recv[1] + xb_recv[2]
    gathered[unit_own] = total * (1.0 / NDP)
    for i in (2, 1, 3):
        to = (x + i) % NX
        remote(gathered.at[unit_own], gathered.at[unit_own], xg_ssem, xg_rsem, (z * NX + to, mp)).start()

    def on_to_x(t):
        for i in (2, 1, 3):
            remote(gathered.at[piece(t, x)], gathered.at[piece(t, x)], ax_ssem, ax_rsem.at[t], (z * NX + (x + i) % NX, mp)).start()

    on_to_x(z)
    remote(x_recv, x_recv, x_ssem, x_rsem.at[0], (dp, mp)).wait_send()
    remote(z_recv, z_recv, z_ssem, z_rsem, (dp, mp)).wait_send()
    remote(zb_recv, zb_recv, zb_ssem, zb_rsem, (dp, mp)).wait_send()
    remote(xb_recv, xb_recv, xb_ssem, xb_rsem, (dp, mp)).wait_send()
    for k in NEAR_FIRST:
        t = (z + NZ - k) % NZ
        remote(gathered.at[piece(t, x)], gathered.at[piece(t, x)], az_ssem, az_rsem.at[k], (dp, mp)).wait_recv()
        on_to_x(t)
        if k == 7:
            remote(xb_recv, xb_recv, xg_ssem, xg_rsem, (dp, mp)).wait_recv()
            for j in reversed(NEAR_FIRST):
                remote(gathered.at[rest(z)], gathered.at[rest(z)], bz_ssem, bz_rsem.at[j],
                       ((z + j) % NZ * NX + x, mp)).start()

    def accumulate(c):
        cols = pl.ds(pl.multiple_of(c * CHUNK, CHUNK), CHUNK)
        for j in range(CHUNK // 128):
            for group in range(RANK // 4):
                p_full[4 * group:4 * group + 4, 128 * j:128 * (j + 1)] = gathered[c * 32 + (j * 16 + group)]
        p_high, p_low = split(p_full[...])
        p_out[:RANK, cols] = p_high
        p_out[RANK:, cols] = p_low
        p_both = jnp.concatenate([p_high, p_low], axis=0)
        both = dot(p_both, mh[:, cols], ((1,), (1,)))
        t_full[...] += both[:RANK] + both[RANK:] + dot(p_high, ml[:, cols], ((1,), (1,)))
        both = dot(p_both, p_both, ((1,), (1,)))
        g_full[:, :RANK] += both[:RANK, :RANK] + both[:RANK, RANK:] + both[RANK:, :RANK]

    t_full[...] = jnp.zeros_like(t_full)
    g_full[...] = jnp.zeros_like(g_full)
    for k, chunks in ((0, ()), (1, (0,)), (7, (7,)), (2, (1,)), (6, (6,)), (3, (2,)), (5, (5,)), (4, (3, 4))):
        t = (z + k) % NZ
        remote(x_recv.at[t], x_recv.at[t], ax_ssem, ax_rsem.at[t], (dp, mp)).wait_recv()
        if k:
            remote(gathered.at[rest(t)], gathered.at[rest(t)], bz_ssem, bz_rsem.at[NZ - k], (dp, mp)).wait_recv()
        for o in chunks:
            c = (z + o) % NZ
            pl.when(c < NCHUNK)(functools.partial(accumulate, c))

    def rows(at):
        return pl.ds(pl.multiple_of(at * 8, 8), 8)

    def to_owner(k):
        owner = (y + k) % NY
        remote(t_full.at[rows(owner)], t_recv.at[2 * k + core], ts_sem, tr_sem, (dp, 2 * owner)).start()

    def own_gram(core_0):
        return remote(g_full, g_peer, gp_ssem, gp_rsem, (dp, core_0))

    @pl.when(core == 1)
    def _():
        own_gram(mp - 1).start()

    for k in reversed(NEAR_FIRST):
        to_owner(k)
    pl.when(core == 1)(functools.partial(to_owner, 0))
    remote(xb_recv, xb_recv, xg_ssem, xg_rsem, (dp, mp)).wait_send()
    remote(zb_recv, zb_recv, bz_ssem, bz_rsem.at[1], (dp, mp)).wait_send()
    remote(x_recv, x_recv, ax_ssem, ax_rsem.at[0], (dp, mp)).wait_send()
    remote(z_recv, z_recv, az_ssem, az_rsem.at[1], (dp, mp)).wait_send()

    def handed(core_1):
        return remote(g_total, g_total, gh_ssem, gh_rsem, (dp, core_1))

    @pl.when(core == 0)
    def _():
        own_gram(mp).wait_recv()
        g_full[...] += g_peer[...]
        for k in reversed(NEAR_FIRST):
            owner = (y + k) % NY
            remote(g_full.at[rows(owner)], g_recv.at[k - 1], gs_ssem, gs_rsem, (dp, 2 * owner)).start()
        arrived = t_recv.at[pl.ds(1, NMP - 1)]
        remote(arrived, arrived, ts_sem, tr_sem, (dp, mp)).wait_recv()
        total = t_full[rows(y), :]
        for k in range(1, NMP):
            total = total + t_recv[k]
        t_all[dp] = total
        t_part[...] = total
        for i, j in DP_FAR_FIRST:
            to = (z + i) % NZ * NX + (x + j) % NX
            remote(t_part, t_all.at[dp], ta_ssem, ta_rsem, (to, mp)).start()
        remote(g_recv, g_recv, gs_ssem, gs_rsem, (dp, mp)).wait_recv()
        total = g_full[rows(y), :]
        for k in range(NY - 1):
            total = total + g_recv[k]
        g_total[rows(y), :] = total
        for k in reversed(NEAR_FIRST):
            mine = g_total.at[rows(y)]
            remote(mine, mine, gg_ssem, gg_rsem, (dp, 2 * ((y + k) % NY))).start()
        sent = t_full.at[pl.ds(0, 8 * (NY - 1))]
        remote(sent, sent, ts_sem, tr_sem, (dp, mp)).wait_send()
        remote(g_recv, g_recv, gs_ssem, gs_rsem, (dp, mp)).wait_send()
        others = g_total.at[pl.ds(0, 8 * (NY - 1))]
        remote(others, others, gg_ssem, gg_rsem, (dp, mp)).wait_recv()
        handed(mp + 1).start()
        arrived = t_all.at[pl.ds(0, NDP - 1)]
        remote(arrived, arrived, ta_ssem, ta_rsem, (dp, mp)).wait_recv()
        total = t_all[0]
        for k in range(1, NDP):
            total = total + t_all[k]
        t_total[rows(y), :] = total
        for k in MP_FAR_FIRST:
            mine = t_total.at[rows(y)]
            remote(mine, mine, tg_ssem, tg_rsem, (dp, (mp + k) % NMP)).start()
        remote(arrived, arrived, ta_ssem, ta_rsem, (dp, mp)).wait_send()
        remote(others, others, gg_ssem, gg_rsem, (dp, mp)).wait_send()

    @pl.when(core == 1)
    def _():
        remote(t_full, t_full, ts_sem, tr_sem, (dp, mp)).wait_send()
        own_gram(mp).wait_send()
        handed(mp).wait_recv()

    inverse = inverse_factor(g_total[...])

    @pl.when(core == 0)
    def _():
        others = t_total.at[pl.ds(0, 8 * (NY - 1))]
        remote(others, others, tg_ssem, tg_rsem, (dp, mp)).wait_recv()

    @pl.when(core == 1)
    def _():
        remote(t_total, t_total, tg_ssem, tg_rsem, (dp, mp)).wait_recv()

    exact = lax.Precision.HIGHEST
    q_rows = lax.dot_general(
        inverse, t_total[...] * (1.0 / NDP), (((1,), (0,)), ((), ())),
        precision=exact, preferred_element_type=F32,
    )[:, :COLS]
    q_out[0] = q_rows
    v_out[...] = lax.dot_general(
        q_rows, inverse, (((0,), (0,)), ((), ())), precision=exact, preferred_element_type=F32
    )

    @pl.when(core == 0)
    def _():
        sent = t_all.at[pl.ds(0, NMP - 1)]
        remote(sent, sent, tg_ssem, tg_rsem, (dp, mp)).wait_send()
        handed(mp).wait_send()


def output_kernel(m_ref, p_ref, v_ref, q_ref, u_hbm, e_hbm, q_out, u_buf, e_buf, store_sem):
    v_high, v_low = split(v_ref[...])
    left = jnp.concatenate([v_high, v_low, v_high], axis=1)

    def store(c):
        cols = pl.ds(c * CHUNK, CHUNK)
        return (
            pltpu.make_async_copy(u_buf.at[:, cols], u_hbm.at[:, cols], store_sem.at[c, 0]),
            pltpu.make_async_copy(e_buf.at[:, cols], e_hbm.at[0, :, cols], store_sem.at[c, 1]),
        )

    for c in range(NCHUNK):
        cols = slice(c * CHUNK, (c + 1) * CHUNK)
        p_high = p_ref[:RANK, cols]
        right = jnp.concatenate([p_high, p_high, p_ref[RANK:, cols]], axis=0)
        update = dot(left, right, ((1,), (0,)))
        u_buf[:, cols] = update.astype(BF16)
        e_buf[:, cols] = m_ref[:, cols] - update
        for copy in store(c):
            copy.start()
    q_out[...] = q_ref[...]
    for c in range(NCHUNK):
        for copy in store(c):
            copy.wait()


def on_device(gradients, errors, q_start):
    vmem = pl.BlockSpec(memory_space=pltpu.VMEM)
    hbm = pl.BlockSpec(memory_space=pl.ANY)
    dma, reg = pltpu.SemaphoreType.DMA, pltpu.SemaphoreType.REGULAR
    merged, p_both, v, q_rows = pl.pallas_call(
        round_kernel,
        name="power_round",
        out_shape=(
            jax.ShapeDtypeStruct((COLS, FL), F32),
            jax.ShapeDtypeStruct((2 * RANK, FL), BF16),
            jax.ShapeDtypeStruct((COLS, RANK), F32),
            jax.ShapeDtypeStruct((1, RANK, COLS), F32),
        ),
        in_specs=[hbm, hbm, hbm],
        out_specs=(vmem, vmem, vmem, vmem),
        scratch_shapes=[
            pltpu.VMEM((NCHUNK, COLS, CHUNK), BF16),
            pltpu.VMEM((NCHUNK, COLS, CHUNK), F32),
            pltpu.VMEM((1, RANK, COLS), F32),
            pltpu.VMEM((256, FL), BF16),
            pltpu.VMEM((256, FL), BF16),
            pltpu.VMEM((UNITS, 4, 128), F32),
            pltpu.VMEM((NZ, NX - 1, PIECE, 4, 128), F32),
            pltpu.VMEM((NZ, PIECE, 4, 128), F32),
            pltpu.VMEM((NZ - 1, PIECE, 4, 128), F32),
            pltpu.VMEM((NZ - 1, NX, 4, 128), F32),
            pltpu.VMEM((NX, 4, 128), F32),
            pltpu.VMEM((NX - 1, 4, 128), F32),
            pltpu.VMEM((UNITS, 4, 128), F32),
            pltpu.VMEM((RANK, CHUNK), F32),
            pltpu.VMEM((NMP, 8, 256), F32),
            pltpu.VMEM((8, 256), F32),
            pltpu.VMEM((NDP, 8, 256), F32),
            pltpu.VMEM((RANK, 256), F32),
            pltpu.VMEM((RANK, 256), F32),
            pltpu.VMEM((RANK, 128), F32),
            pltpu.VMEM((RANK, 128), F32),
            pltpu.VMEM((NY - 1, 8, 128), F32),
            pltpu.VMEM((RANK, 128), F32),
            dma((NCHUNK, 2)), dma,
            dma, dma((NZ,)), dma, dma, dma, dma((NZ,)), dma, dma((NZ,)),
            dma, dma, dma, dma, dma, dma, dma, dma((NZ,)), dma, dma,
            dma, dma, dma, dma, dma, dma, dma, dma,
            dma, dma, dma, dma,
        ],
        compiler_params=pltpu.CompilerParams(
            collective_id=0, has_side_effects=True, vmem_limit_bytes=LIMIT
        ),
    )(*(pltpu.with_memory_space_constraint(a, pltpu.HBM) for a in (gradients, errors, jnp.swapaxes(q_start, 1, 2))))

    update_grad, new_errors, q_rows = pl.pallas_call(
        output_kernel,
        name="outputs",
        out_shape=(
            jax.ShapeDtypeStruct((COLS, FL), BF16),
            jax.ShapeDtypeStruct((1, COLS, FL), F32),
            jax.ShapeDtypeStruct((1, RANK, COLS), F32),
        ),
        in_specs=[vmem, vmem, vmem, vmem],
        out_specs=(hbm, hbm, vmem),
        scratch_shapes=[
            pltpu.VMEM((COLS, FL), BF16),
            pltpu.VMEM((COLS, FL), F32),
            dma((NCHUNK, 2)),
        ],
        compiler_params=pltpu.CompilerParams(vmem_limit_bytes=LIMIT),
    )(merged, p_both, v, q_rows)
    return update_grad, new_errors, jnp.swapaxes(q_rows, 1, 2)


def solution(mesh):
    return jax.shard_map(
        on_device,
        mesh=mesh,
        in_specs=(P("dp", None, "mp"), P("dp", None, "mp"), P()),
        out_specs=(P(None, "mp"), P("dp", None, "mp"), P()),
        check_vma=False,
    )
```

```python
import functools

import jax
import jax.numpy as jnp
from jax import lax
from jax.experimental import pallas as pl
from jax.experimental.pallas import tpu as pltpu
from jax.sharding import PartitionSpec as P

MESH = pl.DeviceIdType.MESH
NX, NZ, NMP = 4, 8, 16
NDP = NX * NZ
COLS, RANK, FL = 240, 64, 1792
CHUNK = 256
NCHUNK = FL // CHUNK
LIMIT = 30 << 20
F32, BF16 = jnp.float32, jnp.bfloat16
UNITS = FL // 128 * 16
BLOCK = UNITS // NZ
PIECE = 6
REST = NX * PIECE
NEAR_FIRST = (1, 7, 2, 6, 3, 5, 4)
MP_FAR_FIRST = (9, 8, 7, 10, 11, 6, 5, 12, 13, 4, 3, 14, 15, 2, 1)


def ring(offset, size):
    return min(offset % size, -offset % size)


DP_FAR_FIRST = sorted(
    ((i, j) for i in range(NZ) for j in range(NX) if i or j),
    key=lambda o: (-ring(o[0], NZ) - ring(o[1], NX), -o[0], -o[1]),
)


def split(value):
    high = value.astype(BF16)
    return high, (value - high.astype(F32)).astype(BF16)


def dot(a, b, dims):
    return lax.dot_general(a, b, (dims, ((), ())), preferred_element_type=F32)


def remote(src, dst, send, recv, target):
    return pltpu.make_async_remote_copy(
        src_ref=src, dst_ref=dst, send_sem=send, recv_sem=recv,
        device_id=target, device_id_type=MESH,
    )


def inverse_factor(gram):
    row_at = lax.broadcasted_iota(jnp.int32, (RANK, 2 * RANK), 0)
    col_at = lax.broadcasted_iota(jnp.int32, (RANK, 2 * RANK), 1)
    work = jnp.where(col_at == row_at + RANK, 1.0, gram)
    done = []
    for first in range(0, RANK, 8):
        at = lax.broadcasted_iota(jnp.int32, work.shape, 0)
        columns = [jnp.broadcast_to(work[:, first + k:first + k + 1], work.shape) for k in range(8)]
        for k in range(8):
            factor = jnp.where(at > k, columns[k] * (1.0 / columns[k][k:k + 1, :]), 0.0)
            for m in range(k + 1, 8):
                columns[m] = columns[m] - factor * columns[m][k:k + 1, :]
            work = work - factor * work[k:k + 1, :]
        done.append(work[:8])
        work = work[8:]
    full = jnp.concatenate(done, axis=0)
    diagonal = jnp.sum(jnp.where(col_at == row_at, full, 0.0), axis=1, keepdims=True)
    return (full / jnp.sqrt(diagonal))[:, RANK:]


def round_kernel(g_hbm, e_hbm, q_hbm, m_out, p_out, v_out, q_out,
                 g_buf, e_buf, q_buf, mh, ml, local_p, x_recv, z_send, z_recv, zb_recv, b_send, xb_recv, gathered, p_full,
                 t_send, t_recv, g_send, g_recv, t_part, t_all, t_gather, g_gather, t_full, g_full,
                 load_sem, q_sem, x_ssem, x_rsem, z_ssem, z_rsem, az_ssem, az_rsem, ax_ssem, ax_rsem,
                 zb_ssem, zb_rsem, xb_ssem, xb_rsem, xg_ssem, xg_rsem, bz_ssem, bz_rsem,
                 ts_sem, tr_sem, gs_sem, gr_sem, ta_ssem, ta_rsem, tg_ssem, tg_rsem, gg_ssem, gg_rsem):
    dp = lax.axis_index("dp")
    mp = lax.axis_index("mp")
    z, x = dp // NX, dp % NX

    barrier = pltpu.get_barrier_semaphore()

    def greet(target):
        pl.semaphore_signal(barrier, inc=1, device_id=target, device_id_type=MESH)

    for k in reversed(NEAR_FIRST):
        greet(((z + k) % NZ * NX + x, mp))
    for k in MP_FAR_FIRST:
        greet((dp, (mp + k) % NMP))
    for i in (2, 1, 3):
        greet((z * NX + (x + i) % NX, mp))

    def place(i):
        c = (z + i) % NCHUNK
        return c, pl.ds(pl.multiple_of(c * CHUNK, CHUNK), CHUNK)

    def load(i):
        cols = place(i)[1]
        return (
            pltpu.make_async_copy(g_hbm.at[0, :, cols], g_buf.at[i], load_sem.at[i, 0]),
            pltpu.make_async_copy(e_hbm.at[0, :, cols], e_buf.at[i], load_sem.at[i, 1]),
        )

    q_copy = pltpu.make_async_copy(q_hbm, q_buf, q_sem)
    q_copy.start()
    for i in range(NCHUNK):
        for copy in load(i):
            copy.start()

    mh[COLS:256, :] = jnp.zeros((256 - COLS, FL), BF16)
    ml[COLS:256, :] = jnp.zeros((256 - COLS, FL), BF16)
    q_copy.wait()
    q_high, q_low = split(q_buf[0])
    q_both = jnp.concatenate([q_high, q_low], axis=0)

    def piece(t, to):
        return pl.ds(t * BLOCK + to * PIECE, PIECE)

    def rest(t):
        return pl.ds(t * BLOCK + REST, NX)

    def send_x(k):
        t = (z + 1 + k) % NZ
        for i in (2, 1, 3):
            to = (x + i) % NX
            remote(local_p.at[piece(t, to)], x_recv.at[t, i - 1], x_ssem, x_rsem.at[t], (z * NX + to, mp)).start()
        if k < NZ - 1:
            remote(local_p.at[rest(t)], zb_recv.at[k], zb_ssem, zb_rsem, (t * NX + x, mp)).start()

    for i in range(NCHUNK):
        c, cols = place(i)
        for copy in load(i):
            copy.wait()
        merged = g_buf[i].astype(F32) + e_buf[i]
        m_out[:, cols] = merged
        high, low = split(merged)
        mh[:COLS, cols] = high
        ml[:COLS, cols] = low
        both = dot(q_both, high, ((1,), (0,)))
        part = both[:RANK] + both[RANK:] + dot(q_high, low, ((1,), (0,)))
        for j in range(CHUNK // 128):
            for group in range(RANK // 4):
                unit = part[4 * group:4 * group + 4, 128 * j:128 * (j + 1)]
                local_p[c * 32 + (j * 16 + group)] = unit
        if i == 1:
            pl.semaphore_wait(barrier, NX - 1 + NZ - 1 + NMP - 1)
        if i:
            send_x(i - 1)
    send_x(NCHUNK - 1)
    send_x(NCHUNK)

    for k in range(NZ):
        t = (z + 1 + k) % NZ
        remote(x_recv.at[t], x_recv.at[t], x_ssem, x_rsem.at[t], (dp, mp)).wait_recv()
        z_send[k] = local_p[piece(t, x)] + x_recv[t, 0] + x_recv[t, 1] + x_recv[t, 2]
        if k < NZ - 1:
            remote(z_send.at[k], z_recv.at[k], z_ssem, z_rsem, (t * NX + x, mp)).start()
        if k == 4:
            remote(zb_recv, zb_recv, zb_ssem, zb_rsem, (dp, mp)).wait_recv()
            total = local_p[rest(z)]
            for j in range(NZ - 1):
                total = total + zb_recv[j]
            b_send[...] = total
            for i in (2, 1, 3):
                to = (x + i) % NX
                remote(b_send.at[to], xb_recv.at[i - 1], xb_ssem, xb_rsem, (z * NX + to, mp)).start()
    remote(z_recv, z_recv, z_ssem, z_rsem, (dp, mp)).wait_recv()
    mean = z_send[NZ - 1]
    for k in range(NZ - 1):
        mean = mean + z_recv[k]
    gathered[piece(z, x)] = mean * (1.0 / NDP)

    for k in NEAR_FIRST:
        remote(gathered.at[piece(z, x)], gathered.at[piece(z, x)], az_ssem, az_rsem.at[k], ((z + k) % NZ * NX + x, mp)).start()

    unit_own = z * BLOCK + REST + x
    remote(xb_recv, xb_recv, xb_ssem, xb_rsem, (dp, mp)).wait_recv()
    total = b_send[x] + xb_recv[0] + xb_recv[1] + xb_recv[2]
    gathered[unit_own] = total * (1.0 / NDP)
    for i in (2, 1, 3):
        to = (x + i) % NX
        remote(gathered.at[unit_own], gathered.at[unit_own], xg_ssem, xg_rsem, (z * NX + to, mp)).start()

    def on_to_x(t):
        for i in range(1, NX):
            remote(gathered.at[piece(t, x)], gathered.at[piece(t, x)], ax_ssem, ax_rsem.at[t], (z * NX + (x + i) % NX, mp)).start()

    on_to_x(z)
    remote(x_recv, x_recv, x_ssem, x_rsem.at[0], (dp, mp)).wait_send()
    remote(z_recv, z_recv, z_ssem, z_rsem, (dp, mp)).wait_send()
    remote(zb_recv, zb_recv, zb_ssem, zb_rsem, (dp, mp)).wait_send()
    remote(xb_recv, xb_recv, xb_ssem, xb_rsem, (dp, mp)).wait_send()
    for k in NEAR_FIRST:
        t = (z + NZ - k) % NZ
        remote(gathered.at[piece(t, x)], gathered.at[piece(t, x)], az_ssem, az_rsem.at[k], (dp, mp)).wait_recv()
        on_to_x(t)
        if k == 7:
            remote(xb_recv, xb_recv, xg_ssem, xg_rsem, (dp, mp)).wait_recv()
            for j in reversed(NEAR_FIRST):
                remote(gathered.at[rest(z)], gathered.at[rest(z)], bz_ssem, bz_rsem.at[j],
                       ((z + j) % NZ * NX + x, mp)).start()

    def accumulate(c):
        cols = pl.ds(pl.multiple_of(c * CHUNK, CHUNK), CHUNK)
        for j in range(CHUNK // 128):
            for group in range(RANK // 4):
                p_full[4 * group:4 * group + 4, 128 * j:128 * (j + 1)] = gathered[c * 32 + (j * 16 + group)]
        p_high, p_low = split(p_full[...])
        p_out[:RANK, cols] = p_high
        p_out[RANK:, cols] = p_low
        p_both = jnp.concatenate([p_high, p_low], axis=0)
        both = dot(p_both, mh[:, cols], ((1,), (1,)))
        t_full[...] += both[:RANK] + both[RANK:] + dot(p_high, ml[:, cols], ((1,), (1,)))
        both = dot(p_both, p_both, ((1,), (1,)))
        g_full[:, :RANK] += both[:RANK, :RANK] + both[:RANK, RANK:] + both[RANK:, :RANK]

    t_full[...] = jnp.zeros_like(t_full)
    g_full[...] = jnp.zeros_like(g_full)
    for k, chunks in ((0, ()), (1, (0,)), (7, (7,)), (2, (1,)), (6, (6,)), (3, (2,)), (5, (5,)), (4, (3, 4))):
        t = (z + k) % NZ
        remote(x_recv.at[t], x_recv.at[t], ax_ssem, ax_rsem.at[t], (dp, mp)).wait_recv()
        if k:
            remote(gathered.at[rest(t)], gathered.at[rest(t)], bz_ssem, bz_rsem.at[NZ - k], (dp, mp)).wait_recv()
        for o in chunks:
            c = (z + o) % NZ
            pl.when(c < NCHUNK)(functools.partial(accumulate, c))

    for j in range(NMP):
        t_send[j] = t_full[4 * j:4 * j + 4, :]
        g_send[j] = g_full[4 * j:4 * j + 4, :]

    for k in MP_FAR_FIRST:
        to = (mp + k) % NMP
        remote(t_send.at[to], t_recv.at[k - 1], ts_sem, tr_sem, (dp, to)).start()
    for k in MP_FAR_FIRST:
        to = (mp + k) % NMP
        remote(g_send.at[to], g_recv.at[k - 1], gs_sem, gr_sem, (dp, to)).start()
    remote(xb_recv, xb_recv, xg_ssem, xg_rsem, (dp, mp)).wait_send()
    remote(zb_recv, zb_recv, bz_ssem, bz_rsem.at[1], (dp, mp)).wait_send()
    remote(x_recv, x_recv, ax_ssem, ax_rsem.at[0], (dp, mp)).wait_send()
    remote(z_recv, z_recv, az_ssem, az_rsem.at[1], (dp, mp)).wait_send()
    remote(t_recv, t_recv, ts_sem, tr_sem, (dp, mp)).wait_recv()
    slice_sum = t_send[mp]
    for k in range(NMP - 1):
        slice_sum = slice_sum + t_recv[k]
    t_all[dp] = slice_sum
    t_part[...] = slice_sum

    for i, j in DP_FAR_FIRST:
        to = (z + i) % NZ * NX + (x + j) % NX
        remote(t_part, t_all.at[dp], ta_ssem, ta_rsem, (to, mp)).start()
    remote(g_recv, g_recv, gs_sem, gr_sem, (dp, mp)).wait_recv()
    slice_sum = g_send[mp]
    for k in range(NMP - 1):
        slice_sum = slice_sum + g_recv[k]
    g_gather[mp] = slice_sum
    for k in MP_FAR_FIRST:
        remote(g_gather.at[mp], g_gather.at[mp], gg_ssem, gg_rsem, (dp, (mp + k) % NMP)).start()
    rest_g = g_gather.at[pl.ds(0, NMP - 1)]
    remote(rest_g, rest_g, gg_ssem, gg_rsem, (dp, mp)).wait_recv()
    for j in range(NMP):
        g_full[4 * j:4 * j + 4, :] = g_gather[j]
    remote(t_recv, t_recv, ts_sem, tr_sem, (dp, mp)).wait_send()
    remote(g_recv, g_recv, gs_sem, gr_sem, (dp, mp)).wait_send()
    remote(rest_g, rest_g, gg_ssem, gg_rsem, (dp, mp)).wait_send()

    rest_t = t_all.at[pl.ds(0, NDP - 1)]
    remote(rest_t, rest_t, ta_ssem, ta_rsem, (dp, mp)).wait_recv()
    total = t_all[0]
    for k in range(1, NDP):
        total = total + t_all[k]
    t_gather[mp] = total

    for k in MP_FAR_FIRST:
        remote(t_gather.at[mp], t_gather.at[mp], tg_ssem, tg_rsem, (dp, (mp + k) % NMP)).start()
    remote(rest_t, rest_t, ta_ssem, ta_rsem, (dp, mp)).wait_send()
    inverse = inverse_factor(g_full[...])
    rest_s = t_gather.at[pl.ds(0, NMP - 1)]
    remote(rest_s, rest_s, tg_ssem, tg_rsem, (dp, mp)).wait_recv()
    for j in range(NMP):
        t_full[4 * j:4 * j + 4, :] = t_gather[j]
    exact = lax.Precision.HIGHEST
    q_rows = lax.dot_general(
        inverse, t_full[...] * (1.0 / NDP), (((1,), (0,)), ((), ())),
        precision=exact, preferred_element_type=F32,
    )[:, :COLS]
    q_out[0] = q_rows
    v_out[...] = lax.dot_general(
        q_rows, inverse, (((0,), (0,)), ((), ())), precision=exact, preferred_element_type=F32
    )
    remote(rest_s, rest_s, tg_ssem, tg_rsem, (dp, mp)).wait_send()


def output_kernel(m_ref, p_ref, v_ref, q_ref, u_hbm, e_hbm, q_out, u_buf, e_buf, store_sem):
    v_high, v_low = split(v_ref[...])
    left = jnp.concatenate([v_high, v_low, v_high], axis=1)

    def store(c):
        cols = pl.ds(c * CHUNK, CHUNK)
        return (
            pltpu.make_async_copy(u_buf.at[:, cols], u_hbm.at[:, cols], store_sem.at[c, 0]),
            pltpu.make_async_copy(e_buf.at[:, cols], e_hbm.at[0, :, cols], store_sem.at[c, 1]),
        )

    for c in range(NCHUNK):
        cols = slice(c * CHUNK, (c + 1) * CHUNK)
        p_high = p_ref[:RANK, cols]
        right = jnp.concatenate([p_high, p_high, p_ref[RANK:, cols]], axis=0)
        update = dot(left, right, ((1,), (0,)))
        u_buf[:, cols] = update.astype(BF16)
        e_buf[:, cols] = m_ref[:, cols] - update
        for copy in store(c):
            copy.start()
    q_out[...] = q_ref[...]
    for c in range(NCHUNK):
        for copy in store(c):
            copy.wait()


def on_device(gradients, errors, q_start):
    vmem = pl.BlockSpec(memory_space=pltpu.VMEM)
    hbm = pl.BlockSpec(memory_space=pl.ANY)
    dma, reg = pltpu.SemaphoreType.DMA, pltpu.SemaphoreType.REGULAR
    merged, p_both, v, q_rows = pl.pallas_call(
        round_kernel,
        name="power_round",
        out_shape=(
            jax.ShapeDtypeStruct((COLS, FL), F32),
            jax.ShapeDtypeStruct((2 * RANK, FL), BF16),
            jax.ShapeDtypeStruct((COLS, RANK), F32),
            jax.ShapeDtypeStruct((1, RANK, COLS), F32),
        ),
        in_specs=[hbm, hbm, hbm],
        out_specs=(vmem, vmem, vmem, vmem),
        scratch_shapes=[
            pltpu.VMEM((NCHUNK, COLS, CHUNK), BF16),
            pltpu.VMEM((NCHUNK, COLS, CHUNK), F32),
            pltpu.VMEM((1, RANK, COLS), F32),
            pltpu.VMEM((256, FL), BF16),
            pltpu.VMEM((256, FL), BF16),
            pltpu.VMEM((UNITS, 4, 128), F32),
            pltpu.VMEM((NZ, NX - 1, PIECE, 4, 128), F32),
            pltpu.VMEM((NZ, PIECE, 4, 128), F32),
            pltpu.VMEM((NZ - 1, PIECE, 4, 128), F32),
            pltpu.VMEM((NZ - 1, NX, 4, 128), F32),
            pltpu.VMEM((NX, 4, 128), F32),
            pltpu.VMEM((NX - 1, 4, 128), F32),
            pltpu.VMEM((UNITS, 4, 128), F32),
            pltpu.VMEM((RANK, CHUNK), F32),
            pltpu.VMEM((NMP, 4, 256), F32),
            pltpu.VMEM((NMP - 1, 4, 256), F32),
            pltpu.VMEM((NMP, 4, 128), F32),
            pltpu.VMEM((NMP - 1, 4, 128), F32),
            pltpu.VMEM((4, 256), F32),
            pltpu.VMEM((NDP, 4, 256), F32),
            pltpu.VMEM((NMP, 4, 256), F32),
            pltpu.VMEM((NMP, 4, 128), F32),
            pltpu.VMEM((RANK, 256), F32),
            pltpu.VMEM((RANK, 128), F32),
            dma((NCHUNK, 2)), dma,
            dma, dma((NZ,)), dma, dma, dma, dma((NZ,)), dma, dma((NZ,)),
            dma, dma, dma, dma, dma, dma, dma, dma((NZ,)), dma, dma,
            dma, dma, dma, dma, dma, dma, dma, dma,
        ],
        compiler_params=pltpu.CompilerParams(
            collective_id=0, has_side_effects=True, vmem_limit_bytes=LIMIT
        ),
    )(*(pltpu.with_memory_space_constraint(a, pltpu.HBM) for a in (gradients, errors, jnp.swapaxes(q_start, 1, 2))))

    update_grad, new_errors, q_rows = pl.pallas_call(
        output_kernel,
        name="outputs",
        out_shape=(
            jax.ShapeDtypeStruct((COLS, FL), BF16),
            jax.ShapeDtypeStruct((1, COLS, FL), F32),
            jax.ShapeDtypeStruct((1, RANK, COLS), F32),
        ),
        in_specs=[vmem, vmem, vmem, vmem],
        out_specs=(hbm, hbm, vmem),
        scratch_shapes=[
            pltpu.VMEM((COLS, FL), BF16),
            pltpu.VMEM((COLS, FL), F32),
            dma((NCHUNK, 2)),
        ],
        compiler_params=pltpu.CompilerParams(vmem_limit_bytes=LIMIT),
    )(merged, p_both, v, q_rows)
    return update_grad, new_errors, jnp.swapaxes(q_rows, 1, 2)


def solution(mesh):
    return jax.shard_map(
        on_device,
        mesh=mesh,
        in_specs=(P("dp", None, "mp"), P("dp", None, "mp"), P()),
        out_specs=(P(None, "mp"), P("dp", None, "mp"), P()),
        check_vma=False,
    )
```

```python
import functools

import jax
import jax.numpy as jnp
from jax import lax
from jax.experimental import pallas as pl
from jax.experimental.pallas import tpu as pltpu
from jax.sharding import PartitionSpec as P

MESH = pl.DeviceIdType.MESH
NX, NZ, NMP = 4, 8, 16
NDP = NX * NZ
COLS, RANK, FL = 240, 64, 1792
CHUNK = 256
NCHUNK = FL // CHUNK
LIMIT = 30 << 20
F32, BF16 = jnp.float32, jnp.bfloat16
UNITS = FL // 128 * 16
BLOCK = UNITS // NZ
PIECE = 6
REST = NX * PIECE
NEAR_FIRST = (1, 7, 2, 6, 3, 5, 4)
MP_FAR_FIRST = (9, 8, 7, 10, 11, 6, 5, 12, 13, 4, 3, 14, 15, 2, 1)


def ring(offset, size):
    return min(offset % size, -offset % size)


DP_FAR_FIRST = sorted(
    ((i, j) for i in range(NZ) for j in range(NX) if i or j),
    key=lambda o: (-ring(o[0], NZ) - ring(o[1], NX), -o[0], -o[1]),
)


def split(value):
    high = value.astype(BF16)
    return high, (value - high.astype(F32)).astype(BF16)


def dot(a, b, dims):
    return lax.dot_general(a, b, (dims, ((), ())), preferred_element_type=F32)


def remote(src, dst, send, recv, target):
    return pltpu.make_async_remote_copy(
        src_ref=src, dst_ref=dst, send_sem=send, recv_sem=recv,
        device_id=target, device_id_type=MESH,
    )


def inverse_factor(gram):
    row_at = lax.broadcasted_iota(jnp.int32, (RANK, 2 * RANK), 0)
    col_at = lax.broadcasted_iota(jnp.int32, (RANK, 2 * RANK), 1)
    work = jnp.where(col_at == row_at + RANK, 1.0, gram)
    done = []
    for first in range(0, RANK, 8):
        at = lax.broadcasted_iota(jnp.int32, work.shape, 0)
        columns = [jnp.broadcast_to(work[:, first + k:first + k + 1], work.shape) for k in range(8)]
        for k in range(8):
            factor = jnp.where(at > k, columns[k] * (1.0 / columns[k][k:k + 1, :]), 0.0)
            for m in range(k + 1, 8):
                columns[m] = columns[m] - factor * columns[m][k:k + 1, :]
            work = work - factor * work[k:k + 1, :]
        done.append(work[:8])
        work = work[8:]
    full = jnp.concatenate(done, axis=0)
    diagonal = jnp.sum(jnp.where(col_at == row_at, full, 0.0), axis=1, keepdims=True)
    return (full / jnp.sqrt(diagonal))[:, RANK:]


def round_kernel(g_hbm, e_hbm, q_hbm, m_out, p_out, v_out, q_out,
                 g_buf, e_buf, q_buf, mh, ml, local_p, x_recv, z_send, z_recv, zb_recv, b_send, xb_recv, gathered, p_full,
                 t_send, t_recv, t_part, t_all, t_gather, g_gather, t_full, g_full,
                 load_sem, q_sem, x_ssem, x_rsem, z_ssem, z_rsem, az_ssem, az_rsem, ax_ssem, ax_rsem,
                 zb_ssem, zb_rsem, xb_ssem, xb_rsem, xg_ssem, xg_rsem, bz_ssem, bz_rsem,
                 ts_sem, tr_sem, ta_ssem, ta_rsem, tg_ssem, tg_rsem, gg_ssem, gg_rsem):
    dp = lax.axis_index("dp")
    mp = lax.axis_index("mp")
    z, x = dp // NX, dp % NX

    barrier = pltpu.get_barrier_semaphore()

    def greet(target):
        pl.semaphore_signal(barrier, inc=1, device_id=target, device_id_type=MESH)

    for k in reversed(NEAR_FIRST):
        greet(((z + k) % NZ * NX + x, mp))
    for k in MP_FAR_FIRST:
        greet((dp, (mp + k) % NMP))
    for i in (2, 1, 3):
        greet((z * NX + (x + i) % NX, mp))

    def place(i):
        c = (z + i) % NCHUNK
        return c, pl.ds(pl.multiple_of(c * CHUNK, CHUNK), CHUNK)

    def load(i):
        cols = place(i)[1]
        return (
            pltpu.make_async_copy(g_hbm.at[0, :, cols], g_buf.at[i], load_sem.at[i, 0]),
            pltpu.make_async_copy(e_hbm.at[0, :, cols], e_buf.at[i], load_sem.at[i, 1]),
        )

    q_copy = pltpu.make_async_copy(q_hbm, q_buf, q_sem)
    q_copy.start()
    for i in range(NCHUNK):
        for copy in load(i):
            copy.start()

    mh[COLS:256, :] = jnp.zeros((256 - COLS, FL), BF16)
    ml[COLS:256, :] = jnp.zeros((256 - COLS, FL), BF16)
    q_copy.wait()
    q_high, q_low = split(q_buf[0])
    q_both = jnp.concatenate([q_high, q_low], axis=0)

    def piece(t, to):
        return pl.ds(t * BLOCK + to * PIECE, PIECE)

    def rest(t):
        return pl.ds(t * BLOCK + REST, NX)

    def send_x(k):
        t = (z + 1 + k) % NZ
        for i in (2, 1, 3):
            to = (x + i) % NX
            remote(local_p.at[piece(t, to)], x_recv.at[t, i - 1], x_ssem, x_rsem.at[t], (z * NX + to, mp)).start()
        if k < NZ - 1:
            remote(local_p.at[rest(t)], zb_recv.at[k], zb_ssem, zb_rsem, (t * NX + x, mp)).start()

    for i in range(NCHUNK):
        c, cols = place(i)
        for copy in load(i):
            copy.wait()
        merged = g_buf[i].astype(F32) + e_buf[i]
        m_out[:, cols] = merged
        high, low = split(merged)
        mh[:COLS, cols] = high
        ml[:COLS, cols] = low
        both = dot(q_both, high, ((1,), (0,)))
        part = both[:RANK] + both[RANK:] + dot(q_high, low, ((1,), (0,)))
        for j in range(CHUNK // 128):
            for group in range(RANK // 4):
                unit = part[4 * group:4 * group + 4, 128 * j:128 * (j + 1)]
                local_p[c * 32 + (j * 16 + group)] = unit
        if i == 1:
            pl.semaphore_wait(barrier, NX - 1 + NZ - 1 + NMP - 1)
        if i:
            send_x(i - 1)
    send_x(NCHUNK - 1)
    send_x(NCHUNK)

    for k in range(NZ):
        t = (z + 1 + k) % NZ
        remote(x_recv.at[t], x_recv.at[t], x_ssem, x_rsem.at[t], (dp, mp)).wait_recv()
        z_send[k] = local_p[piece(t, x)] + x_recv[t, 0] + x_recv[t, 1] + x_recv[t, 2]
        if k < NZ - 1:
            remote(z_send.at[k], z_recv.at[k], z_ssem, z_rsem, (t * NX + x, mp)).start()
        if k == 4:
            remote(zb_recv, zb_recv, zb_ssem, zb_rsem, (dp, mp)).wait_recv()
            total = local_p[rest(z)]
            for j in range(NZ - 1):
                total = total + zb_recv[j]
            b_send[...] = total
            for i in (2, 1, 3):
                to = (x + i) % NX
                remote(b_send.at[to], xb_recv.at[i - 1], xb_ssem, xb_rsem, (z * NX + to, mp)).start()
    remote(z_recv, z_recv, z_ssem, z_rsem, (dp, mp)).wait_recv()
    mean = z_send[NZ - 1]
    for k in range(NZ - 1):
        mean = mean + z_recv[k]
    gathered[piece(z, x)] = mean * (1.0 / NDP)

    for k in NEAR_FIRST:
        remote(gathered.at[piece(z, x)], gathered.at[piece(z, x)], az_ssem, az_rsem.at[k], ((z + k) % NZ * NX + x, mp)).start()

    unit_own = z * BLOCK + REST + x
    remote(xb_recv, xb_recv, xb_ssem, xb_rsem, (dp, mp)).wait_recv()
    total = b_send[x] + xb_recv[0] + xb_recv[1] + xb_recv[2]
    gathered[unit_own] = total * (1.0 / NDP)
    for i in (2, 1, 3):
        to = (x + i) % NX
        remote(gathered.at[unit_own], gathered.at[unit_own], xg_ssem, xg_rsem, (z * NX + to, mp)).start()

    def on_to_x(t):
        for i in range(1, NX):
            remote(gathered.at[piece(t, x)], gathered.at[piece(t, x)], ax_ssem, ax_rsem.at[t], (z * NX + (x + i) % NX, mp)).start()

    on_to_x(z)
    remote(x_recv, x_recv, x_ssem, x_rsem.at[0], (dp, mp)).wait_send()
    remote(z_recv, z_recv, z_ssem, z_rsem, (dp, mp)).wait_send()
    remote(zb_recv, zb_recv, zb_ssem, zb_rsem, (dp, mp)).wait_send()
    remote(xb_recv, xb_recv, xb_ssem, xb_rsem, (dp, mp)).wait_send()
    for k in NEAR_FIRST:
        t = (z + NZ - k) % NZ
        remote(gathered.at[piece(t, x)], gathered.at[piece(t, x)], az_ssem, az_rsem.at[k], (dp, mp)).wait_recv()
        on_to_x(t)
        if k == 7:
            remote(xb_recv, xb_recv, xg_ssem, xg_rsem, (dp, mp)).wait_recv()
            for j in reversed(NEAR_FIRST):
                remote(gathered.at[rest(z)], gathered.at[rest(z)], bz_ssem, bz_rsem.at[j],
                       ((z + j) % NZ * NX + x, mp)).start()

    def accumulate(c):
        cols = pl.ds(pl.multiple_of(c * CHUNK, CHUNK), CHUNK)
        for j in range(CHUNK // 128):
            for group in range(RANK // 4):
                p_full[4 * group:4 * group + 4, 128 * j:128 * (j + 1)] = gathered[c * 32 + (j * 16 + group)]
        p_high, p_low = split(p_full[...])
        p_out[:RANK, cols] = p_high
        p_out[RANK:, cols] = p_low
        p_both = jnp.concatenate([p_high, p_low], axis=0)
        both = dot(p_both, mh[:, cols], ((1,), (1,)))
        t_full[...] += both[:RANK] + both[RANK:] + dot(p_high, ml[:, cols], ((1,), (1,)))
        both = dot(p_both, p_both, ((1,), (1,)))
        g_full[:, :RANK] += both[:RANK, :RANK] + both[:RANK, RANK:] + both[RANK:, :RANK]

    t_full[...] = jnp.zeros_like(t_full)
    g_full[...] = jnp.zeros_like(g_full)
    for k, chunks in ((0, ()), (1, (0,)), (7, (7,)), (2, (1,)), (6, (6,)), (3, (2,)), (5, (5,)), (4, (3, 4))):
        t = (z + k) % NZ
        remote(x_recv.at[t], x_recv.at[t], ax_ssem, ax_rsem.at[t], (dp, mp)).wait_recv()
        if k:
            remote(gathered.at[rest(t)], gathered.at[rest(t)], bz_ssem, bz_rsem.at[NZ - k], (dp, mp)).wait_recv()
        for o in chunks:
            c = (z + o) % NZ
            pl.when(c < NCHUNK)(functools.partial(accumulate, c))

    for j in range(NMP):
        t_send[j, :, :256] = t_full[4 * j:4 * j + 4, :]
        t_send[j, :, 256:] = g_full[4 * j:4 * j + 4, :]

    for k in MP_FAR_FIRST:
        to = (mp + k) % NMP
        remote(t_send.at[to], t_recv.at[k - 1], ts_sem, tr_sem, (dp, to)).start()
    remote(xb_recv, xb_recv, xg_ssem, xg_rsem, (dp, mp)).wait_send()
    remote(zb_recv, zb_recv, bz_ssem, bz_rsem.at[1], (dp, mp)).wait_send()
    remote(x_recv, x_recv, ax_ssem, ax_rsem.at[0], (dp, mp)).wait_send()
    remote(z_recv, z_recv, az_ssem, az_rsem.at[1], (dp, mp)).wait_send()
    remote(t_recv, t_recv, ts_sem, tr_sem, (dp, mp)).wait_recv()
    slice_sum = t_send[mp]
    for k in range(NMP - 1):
        slice_sum = slice_sum + t_recv[k]
    t_all[dp] = slice_sum[:, :256]
    t_part[...] = slice_sum[:, :256]
    g_gather[mp] = slice_sum[:, 256:]

    for i, j in DP_FAR_FIRST:
        to = (z + i) % NZ * NX + (x + j) % NX
        remote(t_part, t_all.at[dp], ta_ssem, ta_rsem, (to, mp)).start()
    for k in MP_FAR_FIRST:
        remote(g_gather.at[mp], g_gather.at[mp], gg_ssem, gg_rsem, (dp, (mp + k) % NMP)).start()
    remote(t_recv, t_recv, ts_sem, tr_sem, (dp, mp)).wait_send()

    rest_t = t_all.at[pl.ds(0, NDP - 1)]
    remote(rest_t, rest_t, ta_ssem, ta_rsem, (dp, mp)).wait_recv()
    total = t_all[0]
    for k in range(1, NDP):
        total = total + t_all[k]
    t_gather[mp] = total

    for k in MP_FAR_FIRST:
        remote(t_gather.at[mp], t_gather.at[mp], tg_ssem, tg_rsem, (dp, (mp + k) % NMP)).start()
    remote(rest_t, rest_t, ta_ssem, ta_rsem, (dp, mp)).wait_send()
    rest_g = g_gather.at[pl.ds(0, NMP - 1)]
    remote(rest_g, rest_g, gg_ssem, gg_rsem, (dp, mp)).wait_recv()
    for j in range(NMP):
        g_full[4 * j:4 * j + 4, :] = g_gather[j]
    remote(rest_g, rest_g, gg_ssem, gg_rsem, (dp, mp)).wait_send()
    inverse = inverse_factor(g_full[...])
    rest_s = t_gather.at[pl.ds(0, NMP - 1)]
    remote(rest_s, rest_s, tg_ssem, tg_rsem, (dp, mp)).wait_recv()
    for j in range(NMP):
        t_full[4 * j:4 * j + 4, :] = t_gather[j]
    exact = lax.Precision.HIGHEST
    q_rows = lax.dot_general(
        inverse, t_full[...] * (1.0 / NDP), (((1,), (0,)), ((), ())),
        precision=exact, preferred_element_type=F32,
    )[:, :COLS]
    q_out[0] = q_rows
    v_out[...] = lax.dot_general(
        q_rows, inverse, (((0,), (0,)), ((), ())), precision=exact, preferred_element_type=F32
    )
    remote(rest_s, rest_s, tg_ssem, tg_rsem, (dp, mp)).wait_send()


def output_kernel(m_ref, p_ref, v_ref, q_ref, u_hbm, e_hbm, q_out, u_buf, e_buf, store_sem):
    v_high, v_low = split(v_ref[...])
    left = jnp.concatenate([v_high, v_low, v_high], axis=1)

    def store(c):
        cols = pl.ds(c * CHUNK, CHUNK)
        return (
            pltpu.make_async_copy(u_buf.at[:, cols], u_hbm.at[:, cols], store_sem.at[c, 0]),
            pltpu.make_async_copy(e_buf.at[:, cols], e_hbm.at[0, :, cols], store_sem.at[c, 1]),
        )

    for c in range(NCHUNK):
        cols = slice(c * CHUNK, (c + 1) * CHUNK)
        p_high = p_ref[:RANK, cols]
        right = jnp.concatenate([p_high, p_high, p_ref[RANK:, cols]], axis=0)
        update = dot(left, right, ((1,), (0,)))
        u_buf[:, cols] = update.astype(BF16)
        e_buf[:, cols] = m_ref[:, cols] - update
        for copy in store(c):
            copy.start()
    q_out[...] = q_ref[...]
    for c in range(NCHUNK):
        for copy in store(c):
            copy.wait()


def on_device(gradients, errors, q_start):
    vmem = pl.BlockSpec(memory_space=pltpu.VMEM)
    hbm = pl.BlockSpec(memory_space=pl.ANY)
    dma, reg = pltpu.SemaphoreType.DMA, pltpu.SemaphoreType.REGULAR
    merged, p_both, v, q_rows = pl.pallas_call(
        round_kernel,
        name="power_round",
        out_shape=(
            jax.ShapeDtypeStruct((COLS, FL), F32),
            jax.ShapeDtypeStruct((2 * RANK, FL), BF16),
            jax.ShapeDtypeStruct((COLS, RANK), F32),
            jax.ShapeDtypeStruct((1, RANK, COLS), F32),
        ),
        in_specs=[hbm, hbm, hbm],
        out_specs=(vmem, vmem, vmem, vmem),
        scratch_shapes=[
            pltpu.VMEM((NCHUNK, COLS, CHUNK), BF16),
            pltpu.VMEM((NCHUNK, COLS, CHUNK), F32),
            pltpu.VMEM((1, RANK, COLS), F32),
            pltpu.VMEM((256, FL), BF16),
            pltpu.VMEM((256, FL), BF16),
            pltpu.VMEM((UNITS, 4, 128), F32),
            pltpu.VMEM((NZ, NX - 1, PIECE, 4, 128), F32),
            pltpu.VMEM((NZ, PIECE, 4, 128), F32),
            pltpu.VMEM((NZ - 1, PIECE, 4, 128), F32),
            pltpu.VMEM((NZ - 1, NX, 4, 128), F32),
            pltpu.VMEM((NX, 4, 128), F32),
            pltpu.VMEM((NX - 1, 4, 128), F32),
            pltpu.VMEM((UNITS, 4, 128), F32),
            pltpu.VMEM((RANK, CHUNK), F32),
            pltpu.VMEM((NMP, 4, 384), F32),
            pltpu.VMEM((NMP - 1, 4, 384), F32),
            pltpu.VMEM((4, 256), F32),
            pltpu.VMEM((NDP, 4, 256), F32),
            pltpu.VMEM((NMP, 4, 256), F32),
            pltpu.VMEM((NMP, 4, 128), F32),
            pltpu.VMEM((RANK, 256), F32),
            pltpu.VMEM((RANK, 128), F32),
            dma((NCHUNK, 2)), dma,
            dma, dma((NZ,)), dma, dma, dma, dma((NZ,)), dma, dma((NZ,)),
            dma, dma, dma, dma, dma, dma, dma, dma((NZ,)),
            dma, dma, dma, dma, dma, dma, dma, dma,
        ],
        compiler_params=pltpu.CompilerParams(
            collective_id=0, has_side_effects=True, vmem_limit_bytes=LIMIT
        ),
    )(*(pltpu.with_memory_space_constraint(a, pltpu.HBM) for a in (gradients, errors, jnp.swapaxes(q_start, 1, 2))))

    update_grad, new_errors, q_rows = pl.pallas_call(
        output_kernel,
        name="outputs",
        out_shape=(
            jax.ShapeDtypeStruct((COLS, FL), BF16),
            jax.ShapeDtypeStruct((1, COLS, FL), F32),
            jax.ShapeDtypeStruct((1, RANK, COLS), F32),
        ),
        in_specs=[vmem, vmem, vmem, vmem],
        out_specs=(hbm, hbm, vmem),
        scratch_shapes=[
            pltpu.VMEM((COLS, FL), BF16),
            pltpu.VMEM((COLS, FL), F32),
            dma((NCHUNK, 2)),
        ],
        compiler_params=pltpu.CompilerParams(vmem_limit_bytes=LIMIT),
    )(merged, p_both, v, q_rows)
    return update_grad, new_errors, jnp.swapaxes(q_rows, 1, 2)


def solution(mesh):
    return jax.shard_map(
        on_device,
        mesh=mesh,
        in_specs=(P("dp", None, "mp"), P("dp", None, "mp"), P()),
        out_specs=(P(None, "mp"), P("dp", None, "mp"), P()),
        check_vma=False,
    )
```
